32 devices in a mesh: seq: 16 (over z, y, x), blk: 2 (over core).
Axes of the slice: x: 2, y: 2, z: 4, core: 2. Of those that a mesh axis runs over, the one named last changes fastest.
Arguments:
- incoming_vectors: bfloat16 [16, 832, 768], P('seq', 'blk'), may hold values from -6 to 6
- caption_labels: int32 [16, 832], P('seq'), may hold values from 0 to 8, as said below
- loss_sensitivity: bfloat16 [16, 832, 768], P('seq', 'blk'), may hold values from -6 to 6
- asking_projection: bfloat16 [768, 768], replicated, may hold values from -0.21875 to 0.21875
- lookup_projection: bfloat16 [768, 768], replicated, may hold values from -0.21875 to 0.21875
- content_projection: bfloat16 [768, 768], replicated, may hold values from -0.21875 to 0.21875
- attention_result_projection: bfloat16 [768, 768], replicated, may hold values from -0.875 to 0.875
- expansion_projection: bfloat16 [768, 3072], replicated, may hold values from -0.21875 to 0.21875
- contraction_projection: bfloat16 [3072, 768], replicated, may hold values from -0.109375 to 0.109375
- attention_norm_scale: float32 [768], replicated, may hold values from 0.1 to 1.9
- attention_norm_offset: float32 [768], replicated, may hold values from -3 to 3
- asking_offset: float32 [768], replicated, may hold values from -3 to 3
- content_offset: float32 [768], replicated, may hold values from -3 to 3
- attention_result_offset: float32 [768], replicated, may hold values from -3 to 3
- feedforward_norm_scale: float32 [768], replicated, may hold values from 0.1 to 1.9
- feedforward_norm_offset: float32 [768], replicated, may hold values from -3 to 3
- expansion_offset: float32 [3072], replicated, may hold values from -3 to 3
- contraction_offset: float32 [768], replicated, may hold values from -3 to 3
Outputs:
- outputs: bfloat16 [16, 832, 768], P('seq', 'blk')
- input_grad: float32 [16, 832, 768], P('seq', 'blk')
- query_grad: float32 [589824], P(('seq', 'blk'))
- key_grad: float32 [589824], P(('seq', 'blk'))
- value_grad: float32 [589824], P(('seq', 'blk'))
- out_grad: float32 [589824], P(('seq', 'blk'))
- up_grad: float32 [2359296], P(('seq', 'blk'))
- down_grad: float32 [2359296], P(('seq', 'blk'))
- prenorm_gain_gradient: float32 [768], replicated
- prenorm_shift_gradient: float32 [768], replicated
- querybias_grad: float32 [768], replicated
- valuebias_grad: float32 [768], replicated
- outbias_grad: float32 [768], replicated
- midgain_grad: float32 [768], replicated
- midshift_grad: float32 [768], replicated
- upbias_grad: float32 [3072], replicated
- downbias_grad: float32 [768], replicated
The draws below stay inside these ranges and needn't reach their ends.
Inputs may be any that keep to these rules, and one draw needn't show every extreme that they name: `caption_labels`: in every sequence rows 0 to 198 - 1 (CLS and image) have segment 0; the text rows from 198 on carry caption numbers 1 to 8 that never fall, exactly 8 captions a sequence, and one caption covers rows 415 and 416.
All inputs are finite; a program needn't handle non-finite values.
Results may differ from the reference program's by a relative error of at most 0.012.
Values may be sent and summed in bfloat16 or wider, within the bound.
A program may use at most 192 MiB of HBM per device.

```python
import jax
import jax.numpy as jnp
from jax import lax

EMBED_DIMENSION = 768
H = 12
HD = 64
FF = 3072
IMG = 198
CAPS = 8
ROWS_DEV = 416
SEQ_LEN = 832
SEQS = 16


def draw_caption_labels(key, part):
    key = jax.random.fold_in(key, 7)
    positions = jnp.arange(SEQ_LEN, dtype=jnp.int32)
    margin = ROWS_DEV // 8
    nearby = (positions >= ROWS_DEV - margin) & (positions < ROWS_DEV + margin)
    eligible = (positions > IMG) & ~nearby
    noise = jax.random.randint(key, (SEQS, SEQ_LEN), 0, 1048576, dtype=jnp.int32)
    scores = jnp.where(eligible[None, :], noise * SEQ_LEN + positions[None, :], -1 - positions[None, :])
    discarded_result, chosen = lax.top_k(scores, CAPS - 1)
    picked = jnp.any(positions[None, None, :] == chosen[:, :, None].astype(jnp.int32), axis=1)
    starts = picked | (positions == IMG)[None, :]
    return jnp.cumsum(starts.astype(jnp.int32), axis=1).astype(jnp.int32)


def strengthened(values, key, source, target, shards_of, factor):
    owner, partner = [(jnp.arange(values.shape[axis_at]) // (values.shape[axis_at] // shards_of)).reshape([-1 if axis == axis_at else 1 for axis in range(values.ndim)]) for axis_at in (source, target)]
    chosen = jax.random.permutation(key, shards_of)[partner]
    strong = (owner == chosen) | (owner == (partner + shards_of // 2) % shards_of)
    return jnp.where(strong, factor * values, values)


def level_of(own_key, extent, cuts, least, largest):
    factor_of = 1.0
    for position, shards_of in cuts:
        draws = jax.random.uniform(jax.random.fold_in(jax.random.fold_in(own_key, 6), position), (shards_of,), jnp.float32, least / len(cuts), largest / len(cuts))
        factor_of = factor_of * jnp.repeat(jnp.exp(draws), extent[position] // shards_of).reshape((-1,) + (1,) * (len(extent) - 1 - position))
    return factor_of


def bell_draw(rng, dims, scale, most, split=(), kind=jnp.bfloat16):
    array = scale * jax.random.normal(rng, dims, jnp.float32)
    if split:
        array = array * level_of(rng, dims, split, -0.22, 0.18)
    return jnp.clip(array, -most, most).astype(kind)


def gaussian_with(stream_key, extent, scale, most, cuts, heavy, kind=jnp.bfloat16):
    drawn = scale * jax.random.normal(stream_key, extent, jnp.float32)
    if cuts:
        drawn = drawn * level_of(stream_key, extent, cuts, -0.22, 0.18)
    return jnp.clip(strengthened(drawn, jax.random.fold_in(stream_key, 3), *heavy), -most, most).astype(kind)


def setup_inputs(seed: int = 0) -> dict:
    streams_of = jax.random.split(jax.random.key(seed), 19)
    return {
        "incoming_vectors": bell_draw(streams_of[0], (SEQS, SEQ_LEN, EMBED_DIMENSION), 1.0, 6.0, ((0, 16), (1, 2))),
        "caption_labels": draw_caption_labels(jax.random.fold_in(streams_of[18], 71), 0),
        "loss_sensitivity": gaussian_with(streams_of[2], (SEQS, SEQ_LEN, EMBED_DIMENSION), 1.0, 6.0, ((0, 16), (1, 2)), (0, 2, 16, 2.0)),
        "asking_projection": bell_draw(streams_of[3], (EMBED_DIMENSION, EMBED_DIMENSION), EMBED_DIMENSION ** -0.5, 0.21875),
        "lookup_projection": bell_draw(streams_of[4], (EMBED_DIMENSION, EMBED_DIMENSION), EMBED_DIMENSION ** -0.5, 0.21875),
        "content_projection": bell_draw(streams_of[5], (EMBED_DIMENSION, EMBED_DIMENSION), EMBED_DIMENSION ** -0.5, 0.21875),
        "attention_result_projection": bell_draw(streams_of[6], (EMBED_DIMENSION, EMBED_DIMENSION), (EMBED_DIMENSION // 16) ** -0.5, 0.875),
        "expansion_projection": bell_draw(streams_of[7], (EMBED_DIMENSION, FF), EMBED_DIMENSION ** -0.5, 0.21875),
        "contraction_projection": bell_draw(streams_of[8], (FF, EMBED_DIMENSION), FF ** -0.5, 0.109375),
        "attention_norm_scale": jnp.clip(1.0 + 0.18 * jax.random.normal(streams_of[9], (EMBED_DIMENSION,), jnp.float32), 0.1, 1.9),
        "attention_norm_offset": bell_draw(streams_of[10], (EMBED_DIMENSION,), 0.5, 3.0, (), jnp.float32),
        "asking_offset": bell_draw(streams_of[11], (EMBED_DIMENSION,), 0.5, 3.0, (), jnp.float32),
        "content_offset": bell_draw(streams_of[12], (EMBED_DIMENSION,), 0.5, 3.0, (), jnp.float32),
        "attention_result_offset": bell_draw(streams_of[13], (EMBED_DIMENSION,), 0.5, 3.0, (), jnp.float32),
        "feedforward_norm_scale": jnp.clip(1.0 + 0.18 * jax.random.normal(streams_of[14], (EMBED_DIMENSION,), jnp.float32), 0.1, 1.9),
        "feedforward_norm_offset": bell_draw(streams_of[15], (EMBED_DIMENSION,), 0.5, 3.0, (), jnp.float32),
        "expansion_offset": bell_draw(streams_of[16], (FF,), 0.5, 3.0, (), jnp.float32),
        "contraction_offset": bell_draw(streams_of[17], (EMBED_DIMENSION,), 0.5, 3.0, (), jnp.float32),
    }


@jax.custom_vjp
def coarse_numeric_format(v):
    return lax.optimization_barrier(v.astype(jnp.bfloat16)).astype(jnp.float32)

@jax.custom_vjp
def low_back(v):
    return v

def low_keep(v):
    return (coarse_numeric_format(v), None)

def low_pass(kept, grad):
    return (grad,)

def back_keep(v):
    return (v, None)

def back_low(kept, grad):
    return (coarse_numeric_format(grad),)
coarse_numeric_format.defvjp(low_keep, low_pass)
low_back.defvjp(back_keep, back_low)
epsilon = 1e-05
masked_value = -1e+30

def standardize_features(values, gain, shift):
    center = values - lax.optimization_barrier(jnp.mean(values, axis=-1, keepdims=True))
    spread = lax.optimization_barrier(jnp.mean(center * center, axis=-1, keepdims=True))
    return center * lax.rsqrt(spread + epsilon) * gain + shift

def matmul(left, right):
    return jnp.dot(left, right, precision=lax.Precision.HIGHEST)

def sequence_layer(learnable_bundle, incoming_entry_batch, ids):
    asking_projection, lookup_projection, content_projection, attention_result_projection, expansion_projection, contraction_projection, attention_norm_scale, attention_norm_offset, asking_offset, content_offset, attention_result_offset, feedforward_norm_scale, feedforward_norm_offset, expansion_offset, contraction_offset = learnable_bundle
    length = incoming_entry_batch.shape[0]
    standardized_entries = coarse_numeric_format(standardize_features(incoming_entry_batch, attention_norm_scale, attention_norm_offset))
    queries = coarse_numeric_format(low_back(matmul(standardized_entries, asking_projection) + asking_offset)).reshape(length, H, HD)
    keys = coarse_numeric_format(low_back(matmul(standardized_entries, lookup_projection))).reshape(length, H, HD)
    vals = coarse_numeric_format(low_back(matmul(standardized_entries, content_projection) + content_offset)).reshape(length, H, HD)
    raw = jnp.einsum('qhd,khd->hqk', queries, keys, precision=lax.Precision.HIGHEST) * HD ** (-0.5)
    scores = low_back(raw)
    allowed = (ids[:, None] == ids[None, :]) | (ids[None, :] == 0)
    probs = jax.nn.softmax(jnp.where(allowed[None], scores, masked_value), axis=-1)
    attended = jnp.einsum('hqk,khd->qhd', coarse_numeric_format(probs), vals, precision=lax.Precision.HIGHEST)
    attended = coarse_numeric_format(low_back(attended.reshape(length, H * HD)))
    mixed = incoming_entry_batch + low_back(matmul(attended, attention_result_projection) + attention_result_offset)
    midnormed = coarse_numeric_format(standardize_features(mixed, feedforward_norm_scale, feedforward_norm_offset))
    hidden = low_back(matmul(midnormed, expansion_projection) + expansion_offset)
    activated = coarse_numeric_format(jax.nn.gelu(hidden, approximate=False))
    return mixed + matmul(activated, contraction_projection) + contraction_offset

def reference(incoming_vectors, caption_labels, loss_sensitivity, asking_projection, lookup_projection, content_projection, attention_result_projection, expansion_projection, contraction_projection, attention_norm_scale, attention_norm_offset, asking_offset, content_offset, attention_result_offset, feedforward_norm_scale, feedforward_norm_offset, expansion_offset, contraction_offset):
    learnable_bundle = tuple((coefficient_array.astype(jnp.float32) for coefficient_array in (asking_projection, lookup_projection, content_projection, attention_result_projection, expansion_projection, contraction_projection, attention_norm_scale, attention_norm_offset, asking_offset, content_offset, attention_result_offset, feedforward_norm_scale, feedforward_norm_offset, expansion_offset, contraction_offset)))
    start = incoming_vectors.astype(jnp.float32)

    def forward(values, weights):

        def single(items):
            return sequence_layer(weights, items[0], items[1])
        return lax.map(jax.checkpoint(single), (values, caption_labels))
    result, backward = jax.vjp(forward, start, learnable_bundle)
    input_grad, grads = backward(loss_sensitivity.astype(jnp.float32))
    return (result.astype(jnp.bfloat16), input_grad, grads[0].reshape(-1), grads[1].reshape(-1), grads[2].reshape(-1), grads[3].reshape(-1), grads[4].reshape(-1), grads[5].reshape(-1), grads[6], grads[7], grads[8], grads[9], grads[10], grads[11], grads[12], grads[13], grads[14])
```

```python
import math
from functools import partial

import jax
import jax.numpy as jnp
from jax import lax
from jax.experimental import pallas as pl
from jax.experimental.pallas import tpu as pltpu
from jax.sharding import PartitionSpec as P

HD = 64
MESH = pl.DeviceIdType.MESH


epsilon = 1e-05
masked_value = -1e30

HALF = 64
PAIR = 2 * HALF


def lane_mask(rows, head):
    lanes = lax.broadcasted_iota(jnp.int32, (rows, PAIR), 1)
    return (lanes < HALF) if head == 0 else (lanes >= HALF)


def only_head(values, head):
    return jnp.where(lane_mask(values.shape[0], head), values, jnp.zeros_like(values))


def as_row(ref):
    return ref[...].reshape(1, ref.shape[0])


def dot(left, right):
    return jnp.dot(left, right, preferred_element_type=jnp.float32)


def dot_bt(left, right):
    return lax.dot_general(left, right, (((1,), (1,)), ((), ())), preferred_element_type=jnp.float32)


def attention_kernel(
    rows,
    pairs,
    x_ref,
    all_ids_ref,
    gain_ref,
    shift_ref,
    query_bias_ref,
    value_bias_ref,
    wq_hbm,
    wk_hbm,
    wv_hbm,
    normed_t_ref,
    query_ref,
    key_ref,
    value_ref,
    attended_ref,
    probs_ref,
    wq,
    wk,
    wv,
    normed,
    queries,
    keys,
    values,
    attended,
    probs,
    bias,
    row_ids,
    load_sems,
    send_sems,
    recv_sems,
    out_sems,
):
    chip, core = lax.axis_index("seq"), lax.axis_index("blk")
    loads = [
        pltpu.make_async_copy(src, dst, load_sems.at[i])
        for i, (src, dst) in enumerate(((wk_hbm, wk), (wv_hbm, wv), (wq_hbm, wq)))
    ]
    for load in loads:
        load.start()
    barrier = pltpu.get_barrier_semaphore()
    pl.semaphore_signal(barrier, inc=1, device_id=(chip, 1 - core), device_id_type=MESH)

    query_bias, value_bias = as_row(query_bias_ref), as_row(value_bias_ref)
    x = x_ref[...].astype(jnp.float32)
    low = standardize(x, as_row(gain_ref), as_row(shift_ref)).astype(jnp.bfloat16)
    normed[...] = low
    own = pl.ds(pl.multiple_of(core * rows, rows), rows)

    loads[0].wait()
    for p in range(pairs):
        keys[p, own, :] = dot(low, wk[:, p * PAIR : (p + 1) * PAIR]).astype(jnp.bfloat16)
    pl.semaphore_wait(barrier, 1)
    sends = [
        pltpu.make_async_remote_copy(
            src_ref=buf.at[:, own],
            dst_ref=buf.at[:, own],
            send_sem=send_sems.at[i],
            recv_sem=recv_sems.at[i],
            device_id=(chip, 1 - core),
            device_id_type=MESH,
        )
        for i, buf in enumerate((keys, values))
    ]
    sends[0].start()
    loads[1].wait()
    for p in range(pairs):
        lanes = slice(p * PAIR, (p + 1) * PAIR)
        values[p, own, :] = (dot(low, wv[:, lanes]) + value_bias[:, lanes]).astype(jnp.bfloat16)
    sends[1].start()
    loads[2].wait()
    for p in range(pairs):
        lanes = slice(p * PAIR, (p + 1) * PAIR)
        asked = (dot(low, wq[:, lanes]) + query_bias[:, lanes]).astype(jnp.bfloat16)
        queries[p] = asked * jnp.bfloat16(HD ** (-0.5))
    col_ids = all_ids_ref[...]
    row_ids[...] = jnp.broadcast_to(col_ids.astype(jnp.float32), (8, col_ids.shape[1])).T
    own_ids = row_ids[own, 0:1].astype(jnp.int32)
    bias[...] = jnp.where((own_ids == col_ids) | (col_ids == 0), 0.0, masked_value)
    normed_t_ref[...] = low.T
    sends[0].wait()
    sends[1].wait()
    early = [
        pltpu.make_async_copy(src, dst, out_sems.at[i])
        for i, (src, dst) in enumerate(
            ((queries, query_ref), (keys, key_ref), (values, value_ref))
        )
    ]
    for copy in early:
        copy.start()

    def pair_step(p, carry):
        q, k, v = queries[p], keys[p], values[p]
        total = jnp.zeros((rows, PAIR), jnp.float32)
        for head in range(2):
            scores = dot_bt(only_head(q, head), k) + bias[...]
            expo = jnp.exp(scores - jnp.max(scores, axis=1, keepdims=True))
            share = (expo * (1.0 / jnp.sum(expo, axis=1, keepdims=True))).astype(jnp.bfloat16)
            probs[p, head] = share
            total = total + dot(share, only_head(v, head))
        attended[p] = total.astype(jnp.bfloat16)
        pltpu.make_async_copy(probs.at[p], probs_ref.at[p], out_sems.at[4 + p]).start()
        return carry

    lax.fori_loop(0, pairs, pair_step, 0)
    for p in range(pairs):
        attended_ref[:, p * PAIR : (p + 1) * PAIR] = attended[p]
    for copy in early:
        copy.wait()
    for p in range(pairs):
        pltpu.make_async_copy(probs.at[p], probs_ref.at[p], out_sems.at[4 + p]).wait()


def standardize(values, gain, shift):
    center = values - jnp.mean(values, axis=-1, keepdims=True)
    spread = jnp.mean(center * center, axis=-1, keepdims=True)
    return center * lax.rsqrt(spread + epsilon) * gain + shift


def run_attention(x, all_ids, gain, shift, query_bias, value_bias, wq, wk, wv):
    rows, width = x.shape
    cols = all_ids.shape[1]
    pairs = width // PAIR
    vmem, hbm = pl.BlockSpec(memory_space=pltpu.VMEM), pl.BlockSpec(memory_space=pl.ANY)
    low = jnp.bfloat16
    return pl.pallas_call(
        partial(attention_kernel, rows, pairs),
        out_shape=(
            jax.ShapeDtypeStruct((width, rows), low),
            jax.ShapeDtypeStruct((pairs, rows, PAIR), low),
            jax.ShapeDtypeStruct((pairs, cols, PAIR), low),
            jax.ShapeDtypeStruct((pairs, cols, PAIR), low),
            jax.ShapeDtypeStruct((rows, width), low),
            jax.ShapeDtypeStruct((pairs, 2, rows, cols), low),
        ),
        in_specs=[vmem] * 6 + [hbm] * 3,
        out_specs=(vmem, hbm, hbm, hbm, vmem, hbm),
        scratch_shapes=[
            pltpu.VMEM((width, width), low),
            pltpu.VMEM((width, width), low),
            pltpu.VMEM((width, width), low),
            pltpu.VMEM((rows, width), low),
            pltpu.VMEM((pairs, rows, PAIR), low),
            pltpu.VMEM((pairs, cols, PAIR), low),
            pltpu.VMEM((pairs, cols, PAIR), low),
            pltpu.VMEM((pairs, rows, PAIR), low),
            pltpu.VMEM((pairs, 2, rows, cols), low),
            pltpu.VMEM((rows, cols), jnp.float32),
            pltpu.VMEM((cols, 8), jnp.float32),
            pltpu.SemaphoreType.DMA((3,)),
            pltpu.SemaphoreType.DMA((2,)),
            pltpu.SemaphoreType.DMA((2,)),
            pltpu.SemaphoreType.DMA((4 + pairs,)),
        ],
        compiler_params=pltpu.CompilerParams(
            collective_id=1, has_side_effects=True, vmem_limit_bytes=56 << 20
        ),
    )(x, all_ids, gain, shift, query_bias, value_bias, wq, wk, wv)


X_BIT, Y_BIT, Z_BIT, ZZ_BIT = 1, 2, 4, 8
GROUPS = 16
CORE_ORDER = (X_BIT, Y_BIT, Z_BIT, ZZ_BIT)
FIRST_X = (X_BIT, Z_BIT, ZZ_BIT, Y_BIT)
FIRST_Y = (Y_BIT, Z_BIT, ZZ_BIT, X_BIT)
N_DOWN, N_UP = 4, 4
U_OUT = N_DOWN + N_UP
U_QKV = U_OUT + 1
UNITS = U_QKV + 3
LANDING = (0, 1, 2, 3, 4, 5, 6, 7, 0, 1, 2, 4)


def place_of(group, order):
    place = 0
    for bit in order:
        place = 2 * place + (1 if group & bit else 0)
    return place


def normal_parts(values):
    center = values - jnp.mean(values, axis=-1, keepdims=True)
    spread = jnp.mean(center * center, axis=-1, keepdims=True)
    inverse = lax.rsqrt(spread + epsilon)
    return center * inverse, inverse


def normal_back(hat, inverse, gain, grad):
    scaled = grad * gain
    first = jnp.mean(scaled, axis=-1, keepdims=True)
    second = jnp.mean(scaled * hat, axis=-1, keepdims=True)
    return inverse * (scaled - first - hat * second)


def column_sum(values):
    return jnp.sum(values, axis=0, keepdims=True)


def backward_kernel(
    rows,
    width,
    pairs,
    minor,
    x_ref,
    dy_ref,
    attended_ref,
    gain_ref,
    mid_gain_ref,
    mid_shift_ref,
    out_bias_ref,
    up_bias_ref,
    down_bias_ref,
    normed_t_hbm,
    query_hbm,
    key_hbm,
    value_hbm,
    probs_hbm,
    wo_hbm,
    wu_hbm,
    wd_hbm,
    wq_hbm,
    wk_hbm,
    wv_hbm,
    outputs_ref,
    input_grad_ref,
    qkv_out_ref,
    out_out_ref,
    up_out_ref,
    down_out_ref,
    vec_a_ref,
    vec_b_ref,
    wo,
    wu,
    wd,
    normed_t,
    queries,
    keys,
    values,
    probs,
    mixed,
    mid,
    mid_t,
    act,
    total,
    act_t,
    hid_grad,
    att_grad,
    qkv_grad,
    kv_part,
    kv_recv,
    own,
    stage,
    recv0,
    recv1,
    recv2,
    recv3,
    recv4,
    down3,
    down4,
    last,
    last_recv,
    down_last,
    down_last_recv,
    vec_recv,
    load_sems,
    probs_sems,
    unit_send,
    unit_recv,
    kv_send,
    kv_recv_sem,
    vec_send,
    vec_recv_sem,
):
    low = jnp.bfloat16
    f32 = jnp.float32
    half = width // 2
    chip, core = lax.axis_index("seq"), lax.axis_index("blk")
    group = lax.div(chip, minor)

    def my_bit(bit):
        return lax.rem(lax.div(group, bit), 2)

    def partner(bit):
        return (chip + (1 - 2 * my_bit(bit)) * (bit * minor), core)

    sibling = (chip, 1 - core)
    mine = pl.multiple_of(core * half, half)
    theirs = pl.multiple_of((1 - core) * half, half)

    def load(src, dst, i):
        copy = pltpu.make_async_copy(src, dst, load_sems.at[i])
        copy.start()
        return copy

    load_wo = load(wo_hbm, wo, 0)
    load_wu = load(wu_hbm, wu, 1)
    load_wd = load(wd_hbm, wd, 2)
    load_nt = load(normed_t_hbm, normed_t, 3)
    load_q = load(query_hbm, queries, 4)
    load_k = load(key_hbm, keys, 5)
    load_v = load(value_hbm, values, 6)

    def probs_copy(p, slot):
        return pltpu.make_async_copy(probs_hbm.at[p], probs.at[slot], probs_sems.at[slot])

    probs_copy(0, 0).start()
    probs_copy(1, 1).start()

    barrier = pltpu.get_barrier_semaphore()
    others = [sibling] + [partner(bit) for bit in CORE_ORDER]
    for device in others:
        pl.semaphore_signal(barrier, inc=1, device_id=device, device_id_type=MESH)

    def send(src, dst, sems_at, device, start=True):
        copy = pltpu.make_async_remote_copy(
            src_ref=src,
            dst_ref=dst,
            send_sem=unit_send.at[sems_at],
            recv_sem=unit_recv.at[sems_at],
            device_id=device,
            device_id_type=MESH,
        )
        if start:
            copy.start()
        return copy

    given = []
    flying = {}
    base = {}
    recvs = (recv0, recv1, recv2, recv3, recv4)

    def landing(unit, k):
        if k == 0:
            return recv0.at[LANDING[unit]]
        return recvs[k].at[unit if k < 3 else unit - N_DOWN]

    def order_of(unit):
        if unit < N_DOWN:
            return (X_BIT, Y_BIT) if unit % 2 == 0 else (Y_BIT, X_BIT)
        return FIRST_Y if unit % 2 == 0 else FIRST_X

    def put(unit, target, value):
        order = order_of(unit)
        if unit < N_DOWN:
            step = width // 4
            for yx in range(4):
                at = place_of(yx, order) * step
                target[at : at + step, :] = value[yx * step : (yx + 1) * step, :]
        else:
            step = width // GROUPS
            for g in range(GROUPS):
                at = place_of(g, order) * step
                target[at : at + step, :] = value[g * step : (g + 1) * step, :]

    def give(unit, value):
        slot = len(given) % stage.shape[0]
        if len(given) >= stage.shape[0]:
            flying[(given[-stage.shape[0]], 0)].wait_send()
        given.append(unit)
        put(unit, stage.at[slot], value)
        flying[(unit, 0)] = send(stage.at[slot], recv0.at[LANDING[unit]], (unit, 0), sibling)

    def keep(unit, value):
        put(unit, own.at[unit], value)
        base[unit] = 0

    def step(unit, k):
        size = width >> (k - 1)
        part = size // 2
        bit = order_of(unit)[k - 1]
        side = my_bit(bit)
        at = base[unit]
        flying[(unit, k - 1)].wait_recv()
        got = landing(unit, k - 1)
        away = pl.ds(pl.multiple_of((1 - side) * part, part), part)
        away_own = pl.ds(pl.multiple_of(at + (1 - side) * part, part), part)
        stay = pl.ds(pl.multiple_of(side * part, part), part)
        stay_own = pl.ds(pl.multiple_of(at + side * part, part), part)
        own[unit, away_own, :] += got[away, :]
        flying[(unit, k)] = send(
            own.at[unit, away_own], landing(unit, k), (unit, k), partner(bit)
        )
        own[unit, stay_own, :] += got[stay, :]
        base[unit] = at + side * part

    def finish(unit):
        size = width >> 4
        flying[(unit, 4)].wait_recv()
        at = pl.ds(pl.multiple_of(base[unit], size), size)
        spot = unit - N_DOWN
        last[spot] = own[unit, at, :].astype(f32) + recv4[spot].astype(f32)
        if minor == 1:
            flying[(unit, 5)] = send(
                last.at[spot, pl.ds(pl.multiple_of((1 - core) * (size // 2), size // 2), size // 2)],
                last_recv.at[spot],
                (unit, 5),
                sibling,
            )

    def down_pair(pair):
        size = width // 4
        side = my_bit(Z_BIT)
        for c in (0, 1):
            unit = 2 * pair + c
            flying[(unit, 2)].wait_recv()
            at = pl.ds(pl.multiple_of(base[unit], size), size)
            own[unit, at, :] += recv2[unit]
        away = 2 * pair + 1 - side
        at0, at1 = base[2 * pair], base[2 * pair + 1]
        at = jnp.where(side == 1, at0, at1)
        flying[(2 * pair, 3)] = send(
            own.at[away, pl.ds(pl.multiple_of(at, size), size)],
            down3.at[pair],
            (2 * pair, 3),
            partner(Z_BIT),
        )

    def down_cross():
        size = width // 4
        side, high = my_bit(Z_BIT), my_bit(ZZ_BIT)
        at = pl.ds(pl.multiple_of(jnp.where(side == 0, base[0], base[1]), size), size)
        for pair in (0, 1):
            flying[(2 * pair, 3)].wait_recv()
            own[2 * pair + side, at, :] += down3[pair]
        flying[(0, 4)] = send(
            own.at[2 * (1 - high) + side, at], down4, (0, 4), partner(ZZ_BIT)
        )

    def down_finish():
        size = width // 4
        side, high = my_bit(Z_BIT), my_bit(ZZ_BIT)
        at = pl.ds(pl.multiple_of(jnp.where(side == 0, base[0], base[1]), size), size)
        flying[(0, 4)].wait_recv()
        down_last[...] = own[2 * high + side, at, :].astype(f32) + down4[...].astype(f32)
        if minor == 1:
            flying[(0, 5)] = send(
                down_last.at[pl.ds(pl.multiple_of((1 - core) * (size // 2), size // 2), size // 2)],
                down_last_recv,
                (0, 5),
                sibling,
            )

    def vec_step(buf, which, k):
        if k > 0:
            flying[("v", which, k - 1)].wait()
            buf[...] += vec_recv[which, k - 1]
        if k < 5:
            device = sibling if k == 0 else partner(CORE_ORDER[k - 1])
            copy = pltpu.make_async_remote_copy(
                src_ref=buf,
                dst_ref=vec_recv.at[which, k],
                send_sem=vec_send.at[which, k],
                recv_sem=vec_recv_sem.at[which, k],
                device_id=device,
                device_id_type=MESH,
            )
            copy.start()
            flying[("v", which, k)] = copy

    load_wo.wait()
    mixed[...] = (
        x_ref[...].astype(f32) + dot(attended_ref[...], wo[...]) + as_row(out_bias_ref)
    )
    hat, _ = normal_parts(mixed[...])
    mid_low = (hat * as_row(mid_gain_ref) + as_row(mid_shift_ref)).astype(low)
    mid[...] = mid_low
    mid_t[...] = mid_low.T
    pl.semaphore_wait(barrier, len(others))

    load_wu.wait()
    load_wd.wait()
    vec_a_ref[0:1, :] = column_sum(dy_ref[...].astype(f32))
    for c in range(4):
        lanes = slice(c * width, (c + 1) * width)
        hidden = dot(mid[...], wu[:, lanes]) + as_row(up_bias_ref)[:, lanes]
        cdf = 0.5 * (1.0 + lax.erf(hidden * (0.5**0.5)))
        active = (hidden * cdf).astype(low)
        slope = cdf + hidden * (jnp.exp(-0.5 * hidden * hidden) * ((2.0 * math.pi) ** -0.5))
        act[...] = active
        act_t[...] = active.T
        back = (dot_bt(dy_ref[...], wd[lanes, :]) * slope).astype(low)
        hid_grad[...] = back
        deeper = dot_bt(back, wu[:, lanes])
        if c == 0:
            input_grad_ref[...] = deeper
        else:
            input_grad_ref[...] += deeper
        vec_a_ref[4 + c : 5 + c, :] = column_sum(back.astype(f32))
        give(c, dot(act_t[...], dy_ref[:, pl.ds(theirs, half)]).astype(low))
        keep(c, dot(act_t[...], dy_ref[:, pl.ds(mine, half)]).astype(low))
        give(N_DOWN + c, dot(mid_t[...], hid_grad[:, pl.ds(theirs, half)]).astype(low))
        step(c, 1)
        keep(N_DOWN + c, dot(mid_t[...], hid_grad[:, pl.ds(mine, half)]).astype(low))
        step(N_DOWN + c, 1)
        further = dot(act[...], wd[lanes, :])
        if c == 0:
            total[...] = mixed[...] + as_row(down_bias_ref) + further
        else:
            total[...] += further
        if c == 2:
            step(0, 2)
            step(4, 2)
        if c == 3:
            step(1, 2)
            step(5, 2)
    hat, inverse = normal_parts(mixed[...])
    grad = input_grad_ref[...]
    vec_a_ref[2:3, :] = column_sum(grad * hat)
    vec_a_ref[3:4, :] = column_sum(grad)
    whole = dy_ref[...].astype(f32) + normal_back(hat, inverse, as_row(mid_gain_ref), grad)
    input_grad_ref[...] = whole
    branch_low = whole.astype(low)
    hid_grad[...] = branch_low
    vec_a_ref[1:2, :] = column_sum(branch_low.astype(f32))
    vec_step(vec_a_ref, 0, 0)
    act_t[...] = attended_ref[...].T
    give(U_OUT, dot(act_t[...], hid_grad[:, pl.ds(theirs, half)]).astype(low))
    keep(U_OUT, dot(act_t[...], hid_grad[:, pl.ds(mine, half)]).astype(low))
    for p in range(pairs):
        att_grad[p] = dot_bt(hid_grad[...], wo[p * PAIR : (p + 1) * PAIR, :]).astype(low)
    step(U_OUT, 1)
    step(4, 3)

    outputs_ref[...] = total[...].astype(low)
    load_qkv = []
    for p in range(pairs):
        for i, src in enumerate((wq_hbm, wk_hbm, wv_hbm)):
            at = (3 * p + i) * PAIR
            load_qkv.append(
                load(
                    src.at[:, p * PAIR : (p + 1) * PAIR],
                    wu.at[:, at : at + PAIR],
                    7 + 3 * p + i,
                )
            )
    for copy in (load_nt, load_q, load_k, load_v):
        copy.wait()

    def pair_back(p, slot):
        q, k, v, grad = queries[p], keys[p], values[p], att_grad[p]
        probs_copy(p, slot).wait()
        out = attended_ref[:, pl.ds(pl.multiple_of(p * PAIR, PAIR), PAIR)]
        product = grad.astype(f32) * out.astype(f32)
        q_t, grad_t = q.T, grad.T
        query_total = jnp.zeros((rows, PAIR), f32)
        key_parts, value_parts = [], []
        for head in range(2):
            share = probs[slot, head]
            delta = jnp.sum(only_head(product, head), axis=1, keepdims=True)
            score = dot_bt(only_head(grad, head), v)
            score = (share.astype(f32) * (score - delta)).astype(low)
            query_total = query_total + dot(score, only_head(k, head))
            at = slice(head * HALF, (head + 1) * HALF)
            key_parts.append(dot(q_t[at, :], score).astype(low))
            value_parts.append(dot(grad_t[at, :], share).astype(low))
        kv_part[p, 0] = jnp.concatenate(key_parts, axis=0).T
        kv_part[p, 1] = jnp.concatenate(value_parts, axis=0).T
        at = pl.multiple_of(3 * p * PAIR, PAIR)
        qkv_grad[:, pl.ds(at, PAIR)] = (query_total * HD ** (-0.5)).astype(low)

    own_rows = pl.ds(pl.multiple_of(core * rows, rows), rows)
    their_rows = pl.ds(pl.multiple_of((1 - core) * rows, rows), rows)

    def attention_round(r):
        for i in range(2):
            p = 2 * r + i
            pair_back(p, i)
            if p + 2 < pairs:
                probs_copy(p + 2, i).start()
            copy = pltpu.make_async_remote_copy(
                src_ref=kv_part.at[p, :, their_rows],
                dst_ref=kv_recv.at[p],
                send_sem=kv_send.at[p],
                recv_sem=kv_recv_sem.at[p],
                device_id=sibling,
                device_id_type=MESH,
            )
            copy.start()
            flying[("kv", p)] = copy

    def weight_round(r):
        for i in range(2):
            p = 2 * r + i
            flying[("kv", p)].wait_recv()
            for j in range(2):
                qkv_grad[:, (3 * p + 1 + j) * PAIR : (3 * p + 2 + j) * PAIR] = (
                    kv_part[p, j, own_rows, :] + kv_recv[p, j]
                )
        for which, action in ((1 - core, give), (core, keep)):
            at = pl.multiple_of((2 * r + which) * 3 * PAIR, PAIR)
            action(U_QKV + r, dot(normed_t[...], qkv_grad[:, pl.ds(at, 3 * PAIR)]).astype(low))

    attention_round(0)
    step(6, 2)
    step(2, 2)
    step(5, 3)
    weight_round(0)
    attention_round(1)
    step(U_QKV, 1)
    step(3, 2)
    step(7, 2)
    step(4, 4)
    down_pair(0)
    for k in range(1, 3):
        vec_step(vec_a_ref, 0, k)
    weight_round(1)
    attention_round(2)
    step(U_QKV + 1, 1)
    step(U_OUT, 2)
    step(6, 3)
    step(5, 4)
    down_pair(1)
    weight_round(2)
    step(U_QKV, 2)
    step(7, 3)
    step(6, 4)
    finish(4)
    down_cross()
    step(U_QKV + 2, 1)

    step(U_OUT, 3)
    step(U_QKV + 1, 2)
    finish(5)

    for copy in load_qkv:
        copy.wait()
    size = 3 * pairs * PAIR
    grad = dot_bt(qkv_grad[...], wu[:, :size])
    hat, inverse = normal_parts(x_ref[...].astype(f32))
    input_grad_ref[...] += normal_back(hat, inverse, as_row(gain_ref), grad)
    vec_b_ref[...] = jnp.zeros_like(vec_b_ref)
    vec_b_ref[0:1, :] = column_sum(grad * hat)
    vec_b_ref[1:2, :] = column_sum(grad)
    for p in range(pairs):
        lanes = slice(p * PAIR, (p + 1) * PAIR)
        for row, j in ((2, 0), (3, 2)):
            part = qkv_grad[:, (3 * p + j) * PAIR : (3 * p + j + 1) * PAIR]
            vec_b_ref[row : row + 1, lanes] = column_sum(part.astype(f32))
    vec_step(vec_b_ref, 1, 0)
    vec_step(vec_a_ref, 0, 3)
    step(7, 4)
    step(U_QKV, 3)
    vec_step(vec_b_ref, 1, 1)
    step(U_QKV + 2, 2)
    step(U_OUT, 4)
    vec_step(vec_a_ref, 0, 4)
    step(U_QKV + 1, 3)
    vec_step(vec_b_ref, 1, 2)
    step(U_QKV, 4)
    finish(6)
    down_finish()
    step(U_QKV + 2, 3)
    vec_step(vec_b_ref, 1, 3)
    step(U_QKV + 1, 4)
    finish(7)
    finish(U_OUT)
    vec_step(vec_a_ref, 0, 5)
    step(U_QKV + 2, 4)
    vec_step(vec_b_ref, 1, 4)
    finish(U_QKV)
    finish(U_QKV + 1)
    finish(U_QKV + 2)
    vec_step(vec_b_ref, 1, 5)

    size = width // GROUPS
    if minor == 1:
        size = size // 2
        keep_rows = pl.ds(pl.multiple_of(core * size, size), size)
        down_rows = pl.ds(pl.multiple_of(core * 4 * size, 4 * size), 4 * size)
        flying[(0, 5)].wait_recv()
        down_out_ref[:, pl.ds(mine, half)] = down_last[down_rows, :]
        down_out_ref[:, pl.ds(theirs, half)] = down_last_recv[...]
        for unit in range(N_DOWN, UNITS):
            flying[(unit, 5)].wait_recv()
            spot = unit - N_DOWN
            if unit < U_OUT:
                target, lanes = up_out_ref, (unit - N_DOWN) * width
            else:
                target, lanes = out_out_ref, 0
            if unit < U_QKV:
                target[:, pl.ds(pl.multiple_of(lanes + mine, half), half)] = last[spot, keep_rows, :]
                target[:, pl.ds(pl.multiple_of(lanes + theirs, half), half)] = last_recv[spot]
            else:
                for which, value in (
                    (core, last[spot, keep_rows, :]),
                    (1 - core, last_recv[spot]),
                ):
                    at = pl.ds(pl.multiple_of((2 * (unit - U_QKV) + which) * PAIR, PAIR), PAIR)
                    for j in range(3):
                        qkv_out_ref[j, :, at] = value[:, j * PAIR : (j + 1) * PAIR]
    else:
        down_out_ref[...] = down_last[...]
        for unit in range(N_DOWN, U_OUT):
            up_out_ref[:, (unit - N_DOWN) * half : (unit - N_DOWN + 1) * half] = last[unit - N_DOWN]
        out_out_ref[...] = last[U_OUT - N_DOWN]
        for r in range(3):
            for j in range(3):
                qkv_out_ref[j, :, r * PAIR : (r + 1) * PAIR] = last[
                    U_QKV - N_DOWN + r, :, j * PAIR : (j + 1) * PAIR
                ]

    for p in range(pairs):
        flying[("kv", p)].wait_send()
    for key, copy in flying.items():
        if isinstance(key[0], int) and (key[1] > 0 or key[0] in given[-stage.shape[0] :]):
            copy.wait_send()


def run_backward(
    x, dy, attended, gain, mid_gain, mid_shift, out_bias, up_bias, down_bias,
    normed_t, queries, keys, values, probs, wo, wu, wd, wq, wk, wv, minor,
):
    rows, width = x.shape
    pairs = width // PAIR
    cols = keys.shape[1]
    hidden = wu.shape[1]
    half = width // 2
    chunk = width // GROUPS
    low, f32 = jnp.bfloat16, jnp.float32
    vmem, hbm = pl.BlockSpec(memory_space=pltpu.VMEM), pl.BlockSpec(memory_space=pl.ANY)
    if minor == 1:
        outs = [(3, chunk // 2, width), (chunk // 2, width), (chunk // 2, hidden), (2 * chunk, width)]
    else:
        outs = [(3, chunk, half), (chunk, half), (chunk, hidden // 2), (4 * chunk, half)]
    return pl.pallas_call(
        partial(backward_kernel, rows, width, pairs, minor),
        out_shape=[
            jax.ShapeDtypeStruct((rows, width), low),
            jax.ShapeDtypeStruct((rows, width), f32),
        ]
        + [jax.ShapeDtypeStruct(shape, f32) for shape in outs]
        + [jax.ShapeDtypeStruct((8, width), f32)] * 2,
        in_specs=[vmem] * 9 + [hbm] * 11,
        out_specs=[vmem] * 8,
        scratch_shapes=[
            pltpu.VMEM((width, width), low),
            pltpu.VMEM((width, hidden), low),
            pltpu.VMEM((hidden, width), low),
            pltpu.VMEM((width, rows), low),
            pltpu.VMEM((pairs, rows, PAIR), low),
            pltpu.VMEM((pairs, cols, PAIR), low),
            pltpu.VMEM((pairs, cols, PAIR), low),
            pltpu.VMEM((2, 2, rows, cols), low),
            pltpu.VMEM((rows, width), f32),
            pltpu.VMEM((rows, width), low),
            pltpu.VMEM((width, rows), low),
            pltpu.VMEM((rows, width), low),
            pltpu.VMEM((rows, width), f32),
            pltpu.VMEM((width, rows), low),
            pltpu.VMEM((rows, width), low),
            pltpu.VMEM((pairs, rows, PAIR), low),
            pltpu.VMEM((rows, 3 * width), low),
            pltpu.VMEM((pairs, 2, cols, PAIR), low),
            pltpu.VMEM((pairs, 2, rows, PAIR), low),
            pltpu.VMEM((UNITS, width, half), low),
            pltpu.VMEM((3, width, half), low),
            pltpu.VMEM((max(LANDING) + 1, width, half), low),
            pltpu.VMEM((UNITS, width // 2, half), low),
            pltpu.VMEM((UNITS, width // 4, half), low),
            pltpu.VMEM((UNITS - N_DOWN, width // 8, half), low),
            pltpu.VMEM((UNITS - N_DOWN, width // 16, half), low),
            pltpu.VMEM((2, width // 4, half), low),
            pltpu.VMEM((width // 4, half), low),
            pltpu.VMEM((UNITS - N_DOWN, chunk, half), f32),
            pltpu.VMEM((UNITS - N_DOWN, chunk // 2, half), f32),
            pltpu.VMEM((4 * chunk, half), f32),
            pltpu.VMEM((2 * chunk, half), f32),
            pltpu.VMEM((2, 5, 8, width), f32),
            pltpu.SemaphoreType.DMA((7 + 3 * pairs,)),
            pltpu.SemaphoreType.DMA((2,)),
            pltpu.SemaphoreType.DMA((UNITS, 6)),
            pltpu.SemaphoreType.DMA((UNITS, 6)),
            pltpu.SemaphoreType.DMA((pairs,)),
            pltpu.SemaphoreType.DMA((pairs,)),
            pltpu.SemaphoreType.DMA((2, 5)),
            pltpu.SemaphoreType.DMA((2, 5)),
        ],
        compiler_params=pltpu.CompilerParams(
            collective_id=2, has_side_effects=True, vmem_limit_bytes=60 << 20
        ),
    )(
        x, dy, attended, gain, mid_gain, mid_shift, out_bias, up_bias, down_bias,
        normed_t, queries, keys, values, probs, wo, wu, wd, wq, wk, wv,
    )


def finish_kernel(
    outputs_ref, input_grad_ref, qkv_ref, out_ref, up_ref, down_ref, vec_a_ref, vec_b_ref, *rest
):
    outputs_out, input_grad_out, query, key, value, out, up, down = rest[:8]
    vectors = rest[8:]
    outputs_out[...] = outputs_ref[...]
    input_grad_out[...] = input_grad_ref[...]

    def flatten(values, target):
        rows, lanes = values.shape
        parts = lanes // 128
        for j in range(parts):
            target[pl.ds(j, rows, stride=parts), :] = values[:, j * 128 : (j + 1) * 128]

    for j, target in enumerate((query, key, value)):
        flatten(qkv_ref[j], target)
    flatten(out_ref[...], out)
    flatten(up_ref[...], up)
    flatten(down_ref[...], down)
    lines = [vec_b_ref[j, :] for j in range(4)] + [vec_a_ref[j, :] for j in (1, 2, 3)]
    for line, target in zip(lines, vectors[:7]):
        target[...] = line
    width = vec_a_ref.shape[1]
    for j in range(4):
        vectors[7][j * width : (j + 1) * width] = vec_a_ref[4 + j, :]
    vectors[8][...] = vec_a_ref[0, :]


def run_finish(outputs, input_grad, qkv, out, up, down, vec_a, vec_b):
    f32 = jnp.float32
    width = vec_a.shape[1]
    vmem = pl.BlockSpec(memory_space=pltpu.VMEM)
    flat = lambda size: jax.ShapeDtypeStruct((size // 128, 128), f32)
    line = lambda size: jax.ShapeDtypeStruct((size,), f32)
    return pl.pallas_call(
        finish_kernel,
        out_shape=[
            jax.ShapeDtypeStruct(outputs.shape, outputs.dtype),
            jax.ShapeDtypeStruct(input_grad.shape, f32),
            *(flat(qkv[0].size) for _ in range(3)),
            *(flat(part.size) for part in (out, up, down)),
            *(line(width) for _ in range(7)),
            line(4 * width),
            line(width),
        ],
        in_specs=[vmem] * 8,
        out_specs=[vmem] * 17,
    )(outputs, input_grad, qkv, out, up, down, vec_a, vec_b)


def local(
    incoming_vectors,
    caption_labels,
    loss_sensitivity,
    asking_projection,
    lookup_projection,
    content_projection,
    attention_result_projection,
    expansion_projection,
    contraction_projection,
    attention_norm_scale,
    attention_norm_offset,
    asking_offset,
    content_offset,
    attention_result_offset,
    feedforward_norm_scale,
    feedforward_norm_offset,
    expansion_offset,
    contraction_offset,
):
    seqs, rows, width = incoming_vectors.shape
    chips = lax.axis_size("seq")
    minor = chips // GROUPS
    core = lax.axis_index("blk")
    x = incoming_vectors.reshape(rows, width)
    dy = loss_sensitivity.reshape(rows, width)
    normed_t, queries, keys, values, attended, probs = run_attention(
        x,
        caption_labels,
        attention_norm_scale,
        attention_norm_offset,
        asking_offset,
        content_offset,
        asking_projection,
        lookup_projection,
        content_projection,
    )
    outputs, input_grad, qkv_sum, out_sum, up_sum, down_sum, vec_a, vec_b = run_backward(
        x,
        dy,
        attended,
        attention_norm_scale,
        feedforward_norm_scale,
        feedforward_norm_offset,
        attention_result_offset,
        expansion_offset,
        contraction_offset,
        normed_t,
        queries,
        keys,
        values,
        probs,
        attention_result_projection,
        expansion_projection,
        contraction_projection,
        asking_projection,
        lookup_projection,
        content_projection,
        minor,
    )
    if minor > 1:
        teams = [[g * minor + i for i in range(minor)] for g in range(GROUPS)]
        own_half = lambda values: lax.dynamic_slice_in_dim(
            values, core * (values.shape[0] // 2), values.shape[0] // 2, 0
        )

        def rest(part, pieces):
            both = lax.all_gather(part.reshape(part.shape[0], pieces, -1), "blk", axis=2)
            whole = both.reshape(part.shape[0], -1)
            return own_half(
                lax.psum_scatter(whole, "seq", axis_index_groups=teams, tiled=True)
            )

        qkv_sum = [rest(qkv_sum[i], 3) for i in range(3)]
        out_sum, up_sum, down_sum = rest(out_sum, 1), rest(up_sum, 4), rest(down_sum, 1)
        vec_a, vec_b = lax.psum((vec_a, vec_b), "seq", axis_index_groups=teams)
        qkv_sum = jnp.stack(qkv_sum)
    flat = run_finish(outputs, input_grad, qkv_sum, out_sum, up_sum, down_sum, vec_a, vec_b)
    return (
        flat[0].reshape(seqs, rows, width),
        flat[1].reshape(seqs, rows, width),
        *(part.reshape(-1) for part in flat[2:]),
    )


def solution(mesh):
    in_specs = (
        P("seq", "blk", None),
        P("seq", None),
        P("seq", "blk", None),
        P(),
        P(),
        P(),
        P(),
        P(),
        P(),
        P(),
        P(),
        P(),
        P(),
        P(),
        P(),
        P(),
        P(),
        P(),
    )
    out_specs = (
        P("seq", "blk", None),
        P("seq", "blk", None),
        P(("seq", "blk")),
        P(("seq", "blk")),
        P(("seq", "blk")),
        P(("seq", "blk")),
        P(("seq", "blk")),
        P(("seq", "blk")),
        P(),
        P(),
        P(),
        P(),
        P(),
        P(),
        P(),
        P(),
        P(),
    )
    return jax.shard_map(local, mesh=mesh, in_specs=in_specs, out_specs=out_specs, check_vma=False)
```

```python
import math
from functools import partial

import jax
import jax.numpy as jnp
from jax import lax
from jax.experimental import pallas as pl
from jax.experimental.pallas import tpu as pltpu
from jax.sharding import PartitionSpec as P

HD = 64
MESH = pl.DeviceIdType.MESH


epsilon = 1e-05
masked_value = -1e30

HALF = 64
PAIR = 2 * HALF


def lane_mask(rows, head):
    lanes = lax.broadcasted_iota(jnp.int32, (rows, PAIR), 1)
    return (lanes < HALF) if head == 0 else (lanes >= HALF)


def only_head(values, head):
    return jnp.where(lane_mask(values.shape[0], head), values, jnp.zeros_like(values))


def as_row(ref):
    return ref[...].reshape(1, ref.shape[0])


def dot(left, right):
    return jnp.dot(left, right, preferred_element_type=jnp.float32)


def dot_bt(left, right):
    return lax.dot_general(left, right, (((1,), (1,)), ((), ())), preferred_element_type=jnp.float32)


def attention_kernel(
    rows,
    pairs,
    x_ref,
    all_ids_ref,
    gain_ref,
    shift_ref,
    query_bias_ref,
    value_bias_ref,
    wq_hbm,
    wk_hbm,
    wv_hbm,
    normed_t_ref,
    query_ref,
    key_ref,
    value_ref,
    attended_ref,
    probs_ref,
    wq,
    wk,
    wv,
    normed,
    queries,
    keys,
    values,
    attended,
    probs,
    bias,
    row_ids,
    load_sems,
    send_sems,
    recv_sems,
    out_sems,
):
    chip, core = lax.axis_index("seq"), lax.axis_index("blk")
    loads = [
        pltpu.make_async_copy(src, dst, load_sems.at[i])
        for i, (src, dst) in enumerate(((wk_hbm, wk), (wv_hbm, wv), (wq_hbm, wq)))
    ]
    for load in loads:
        load.start()
    barrier = pltpu.get_barrier_semaphore()
    pl.semaphore_signal(barrier, inc=1, device_id=(chip, 1 - core), device_id_type=MESH)

    query_bias, value_bias = as_row(query_bias_ref), as_row(value_bias_ref)
    x = x_ref[...].astype(jnp.float32)
    low = standardize(x, as_row(gain_ref), as_row(shift_ref)).astype(jnp.bfloat16)
    normed[...] = low
    own = pl.ds(pl.multiple_of(core * rows, rows), rows)

    loads[0].wait()
    for p in range(pairs):
        keys[p, own, :] = dot(low, wk[:, p * PAIR : (p + 1) * PAIR]).astype(jnp.bfloat16)
    pl.semaphore_wait(barrier, 1)
    sends = [
        pltpu.make_async_remote_copy(
            src_ref=buf.at[:, own],
            dst_ref=buf.at[:, own],
            send_sem=send_sems.at[i],
            recv_sem=recv_sems.at[i],
            device_id=(chip, 1 - core),
            device_id_type=MESH,
        )
        for i, buf in enumerate((keys, values))
    ]
    sends[0].start()
    loads[1].wait()
    for p in range(pairs):
        lanes = slice(p * PAIR, (p + 1) * PAIR)
        values[p, own, :] = (dot(low, wv[:, lanes]) + value_bias[:, lanes]).astype(jnp.bfloat16)
    sends[1].start()
    loads[2].wait()
    for p in range(pairs):
        lanes = slice(p * PAIR, (p + 1) * PAIR)
        asked = (dot(low, wq[:, lanes]) + query_bias[:, lanes]).astype(jnp.bfloat16)
        queries[p] = asked * jnp.bfloat16(HD ** (-0.5))
    col_ids = all_ids_ref[...]
    row_ids[...] = jnp.broadcast_to(col_ids.astype(jnp.float32), (8, col_ids.shape[1])).T
    own_ids = row_ids[own, 0:1].astype(jnp.int32)
    bias[...] = jnp.where((own_ids == col_ids) | (col_ids == 0), 0.0, masked_value)
    normed_t_ref[...] = low.T
    sends[0].wait()
    sends[1].wait()
    early = [
        pltpu.make_async_copy(src, dst, out_sems.at[i])
        for i, (src, dst) in enumerate(
            ((queries, query_ref), (keys, key_ref), (values, value_ref))
        )
    ]
    for copy in early:
        copy.start()

    def pair_step(p, carry):
        q, k, v = queries[p], keys[p], values[p]
        total = jnp.zeros((rows, PAIR), jnp.float32)
        for head in range(2):
            scores = dot_bt(only_head(q, head), k) + bias[...]
            expo = jnp.exp(scores - jnp.max(scores, axis=1, keepdims=True))
            share = (expo * (1.0 / jnp.sum(expo, axis=1, keepdims=True))).astype(jnp.bfloat16)
            probs[p, head] = share
            total = total + dot(share, only_head(v, head))
        attended[p] = total.astype(jnp.bfloat16)
        pltpu.make_async_copy(probs.at[p], probs_ref.at[p], out_sems.at[4 + p]).start()
        return carry

    lax.fori_loop(0, pairs, pair_step, 0)
    for p in range(pairs):
        attended_ref[:, p * PAIR : (p + 1) * PAIR] = attended[p]
    for copy in early:
        copy.wait()
    for p in range(pairs):
        pltpu.make_async_copy(probs.at[p], probs_ref.at[p], out_sems.at[4 + p]).wait()


def standardize(values, gain, shift):
    center = values - jnp.mean(values, axis=-1, keepdims=True)
    spread = jnp.mean(center * center, axis=-1, keepdims=True)
    return center * lax.rsqrt(spread + epsilon) * gain + shift


def run_attention(x, all_ids, gain, shift, query_bias, value_bias, wq, wk, wv):
    rows, width = x.shape
    cols = all_ids.shape[1]
    pairs = width // PAIR
    vmem, hbm = pl.BlockSpec(memory_space=pltpu.VMEM), pl.BlockSpec(memory_space=pl.ANY)
    low = jnp.bfloat16
    return pl.pallas_call(
        partial(attention_kernel, rows, pairs),
        out_shape=(
            jax.ShapeDtypeStruct((width, rows), low),
            jax.ShapeDtypeStruct((pairs, rows, PAIR), low),
            jax.ShapeDtypeStruct((pairs, cols, PAIR), low),
            jax.ShapeDtypeStruct((pairs, cols, PAIR), low),
            jax.ShapeDtypeStruct((rows, width), low),
            jax.ShapeDtypeStruct((pairs, 2, rows, cols), low),
        ),
        in_specs=[vmem] * 6 + [hbm] * 3,
        out_specs=(vmem, hbm, hbm, hbm, vmem, hbm),
        scratch_shapes=[
            pltpu.VMEM((width, width), low),
            pltpu.VMEM((width, width), low),
            pltpu.VMEM((width, width), low),
            pltpu.VMEM((rows, width), low),
            pltpu.VMEM((pairs, rows, PAIR), low),
            pltpu.VMEM((pairs, cols, PAIR), low),
            pltpu.VMEM((pairs, cols, PAIR), low),
            pltpu.VMEM((pairs, rows, PAIR), low),
            pltpu.VMEM((pairs, 2, rows, cols), low),
            pltpu.VMEM((rows, cols), jnp.float32),
            pltpu.VMEM((cols, 8), jnp.float32),
            pltpu.SemaphoreType.DMA((3,)),
            pltpu.SemaphoreType.DMA((2,)),
            pltpu.SemaphoreType.DMA((2,)),
            pltpu.SemaphoreType.DMA((4 + pairs,)),
        ],
        compiler_params=pltpu.CompilerParams(
            collective_id=1, has_side_effects=True, vmem_limit_bytes=56 << 20
        ),
    )(x, all_ids, gain, shift, query_bias, value_bias, wq, wk, wv)


X_BIT, Y_BIT, Z_BIT, ZZ_BIT = 1, 2, 4, 8
GROUPS = 16
CORE_ORDER = (X_BIT, Y_BIT, Z_BIT, ZZ_BIT)
N_DOWN, N_UP = 4, 4
U_OUT = N_DOWN + N_UP
U_QKV = U_OUT + 1
UNITS = U_QKV + 3
ORDERS = (
    (X_BIT, Y_BIT),
    (X_BIT, Y_BIT),
    (X_BIT, Y_BIT),
    (Y_BIT, X_BIT),
    (Z_BIT, Y_BIT, X_BIT, ZZ_BIT),
    (Z_BIT, Y_BIT, X_BIT, ZZ_BIT),
    (X_BIT, Z_BIT, Y_BIT, ZZ_BIT),
    (Z_BIT, X_BIT, Y_BIT, ZZ_BIT),
    (Z_BIT, X_BIT, Y_BIT, ZZ_BIT),
    (Y_BIT, X_BIT, Z_BIT, ZZ_BIT),
    (Y_BIT, X_BIT, Z_BIT, ZZ_BIT),
    (X_BIT, Y_BIT, Z_BIT, ZZ_BIT),
)
LANDING = (0, 1, 2, 3, 4, 5, 6, 7, 0, 1, 2, 4)


def place_of(group, order):
    place = 0
    for bit in order:
        place = 2 * place + (1 if group & bit else 0)
    return place


def normal_parts(values):
    center = values - jnp.mean(values, axis=-1, keepdims=True)
    spread = jnp.mean(center * center, axis=-1, keepdims=True)
    inverse = lax.rsqrt(spread + epsilon)
    return center * inverse, inverse


def normal_back(hat, inverse, gain, grad):
    scaled = grad * gain
    first = jnp.mean(scaled, axis=-1, keepdims=True)
    second = jnp.mean(scaled * hat, axis=-1, keepdims=True)
    return inverse * (scaled - first - hat * second)


def column_sum(values):
    return jnp.sum(values, axis=0, keepdims=True)


def backward_kernel(
    rows,
    width,
    pairs,
    minor,
    x_ref,
    dy_ref,
    attended_ref,
    gain_ref,
    mid_gain_ref,
    mid_shift_ref,
    out_bias_ref,
    up_bias_ref,
    down_bias_ref,
    normed_t_hbm,
    query_hbm,
    key_hbm,
    value_hbm,
    probs_hbm,
    wo_hbm,
    wu_hbm,
    wd_hbm,
    wq_hbm,
    wk_hbm,
    wv_hbm,
    outputs_ref,
    input_grad_ref,
    qkv_out_ref,
    out_out_ref,
    up_out_ref,
    down_out_ref,
    vec_a_ref,
    vec_b_ref,
    wo,
    wu,
    wd,
    normed_t,
    queries,
    keys,
    values,
    probs,
    mixed,
    mid,
    mid_t,
    act,
    total,
    act_t,
    hid_grad,
    att_grad,
    qkv_grad,
    kv_part,
    kv_recv,
    own,
    stage,
    recv0,
    recv1,
    recv2,
    recv3,
    recv4,
    down3,
    down4,
    last,
    last_recv,
    down_last,
    down_last_recv,
    vec_sum,
    vec_recv,
    load_sems,
    probs_sems,
    unit_send,
    unit_recv,
    kv_send,
    kv_recv_sem,
    vec_send,
    vec_recv_sem,
):
    low = jnp.bfloat16
    f32 = jnp.float32
    half = width // 2
    chip, core = lax.axis_index("seq"), lax.axis_index("blk")
    group = lax.div(chip, minor)

    def my_bit(bit):
        return lax.rem(lax.div(group, bit), 2)

    def partner(bit):
        return (chip + (1 - 2 * my_bit(bit)) * (bit * minor), core)

    sibling = (chip, 1 - core)
    mine = pl.multiple_of(core * half, half)
    theirs = pl.multiple_of((1 - core) * half, half)

    def load(src, dst, i):
        copy = pltpu.make_async_copy(src, dst, load_sems.at[i])
        copy.start()
        return copy

    load_wo = load(wo_hbm, wo, 0)
    load_wu = load(wu_hbm, wu, 1)
    load_wd = load(wd_hbm, wd, 2)
    load_nt = load(normed_t_hbm, normed_t, 3)
    load_q = load(query_hbm, queries, 4)
    load_k = load(key_hbm, keys, 5)
    load_v = load(value_hbm, values, 6)

    def probs_copy(p, slot):
        return pltpu.make_async_copy(probs_hbm.at[p], probs.at[slot], probs_sems.at[slot])

    probs_copy(0, 0).start()
    probs_copy(1, 1).start()

    barrier = pltpu.get_barrier_semaphore()
    others = [sibling] + [partner(bit) for bit in CORE_ORDER]
    for device in others:
        pl.semaphore_signal(barrier, inc=1, device_id=device, device_id_type=MESH)

    def send(src, dst, sems_at, device, start=True):
        copy = pltpu.make_async_remote_copy(
            src_ref=src,
            dst_ref=dst,
            send_sem=unit_send.at[sems_at],
            recv_sem=unit_recv.at[sems_at],
            device_id=device,
            device_id_type=MESH,
        )
        if start:
            copy.start()
        return copy

    given = []
    flying = {}
    base = {}
    recvs = (recv0, recv1, recv2, recv3, recv4)

    def landing(unit, k):
        if k == 0:
            return recv0.at[LANDING[unit]]
        return recvs[k].at[unit if k < 3 else unit - N_DOWN]

    def order_of(unit):
        return ORDERS[unit]

    def put(unit, target, value):
        order = order_of(unit)
        if unit < N_DOWN:
            step = width // 4
            for yx in range(4):
                at = place_of(yx, order) * step
                target[at : at + step, :] = value[yx * step : (yx + 1) * step, :]
        else:
            step = width // GROUPS
            for g in range(GROUPS):
                at = place_of(g, order) * step
                target[at : at + step, :] = value[g * step : (g + 1) * step, :]

    def give(unit, value):
        slot = len(given) % stage.shape[0]
        if len(given) >= stage.shape[0]:
            flying[(given[-stage.shape[0]], 0)].wait_send()
        given.append(unit)
        put(unit, stage.at[slot], value)
        flying[(unit, 0)] = send(stage.at[slot], recv0.at[LANDING[unit]], (unit, 0), sibling)

    def keep(unit, value):
        put(unit, own.at[unit], value)
        base[unit] = 0

    def step(unit, k):
        size = width >> (k - 1)
        part = size // 2
        bit = order_of(unit)[k - 1]
        side = my_bit(bit)
        at = base[unit]
        flying[(unit, k - 1)].wait_recv()
        got = landing(unit, k - 1)
        away = pl.ds(pl.multiple_of((1 - side) * part, part), part)
        away_own = pl.ds(pl.multiple_of(at + (1 - side) * part, part), part)
        stay = pl.ds(pl.multiple_of(side * part, part), part)
        stay_own = pl.ds(pl.multiple_of(at + side * part, part), part)
        own[unit, away_own, :] += got[away, :]
        flying[(unit, k)] = send(
            own.at[unit, away_own], landing(unit, k), (unit, k), partner(bit)
        )
        own[unit, stay_own, :] += got[stay, :]
        base[unit] = at + side * part

    def finish(unit):
        size = width >> 4
        flying[(unit, 4)].wait_recv()
        at = pl.ds(pl.multiple_of(base[unit], size), size)
        spot = unit - N_DOWN
        last[spot] = own[unit, at, :].astype(f32) + recv4[spot].astype(f32)
        if minor == 1:
            flying[(unit, 5)] = send(
                last.at[spot, pl.ds(pl.multiple_of((1 - core) * (size // 2), size // 2), size // 2)],
                last_recv.at[spot],
                (unit, 5),
                sibling,
            )

    def down_pair(pair):
        size = width // 4
        side = my_bit(Z_BIT)
        for c in (0, 1):
            unit = 2 * pair + c
            flying[(unit, 2)].wait_recv()
            at = pl.ds(pl.multiple_of(base[unit], size), size)
            own[unit, at, :] += recv2[unit]
        away = 2 * pair + 1 - side
        at0, at1 = base[2 * pair], base[2 * pair + 1]
        at = jnp.where(side == 1, at0, at1)
        flying[(2 * pair, 3)] = send(
            own.at[away, pl.ds(pl.multiple_of(at, size), size)],
            down3.at[pair],
            (2 * pair, 3),
            partner(Z_BIT),
        )

    def down_rows(pair):
        at = jnp.where(my_bit(Z_BIT) == 0, base[2 * pair], base[2 * pair + 1])
        return pl.ds(pl.multiple_of(at, width // 4), width // 4)

    def down_cross():
        side, high = my_bit(Z_BIT), my_bit(ZZ_BIT)
        for pair in (0, 1):
            flying[(2 * pair, 3)].wait_recv()
            own[2 * pair + side, down_rows(pair), :] += down3[pair]
        at = pl.multiple_of(jnp.where(high == 1, down_rows(0).start, down_rows(1).start), width // 4)
        flying[(0, 4)] = send(
            own.at[2 * (1 - high) + side, pl.ds(at, width // 4)], down4, (0, 4), partner(ZZ_BIT)
        )

    def down_finish():
        size = width // 4
        side, high = my_bit(Z_BIT), my_bit(ZZ_BIT)
        at = pl.multiple_of(jnp.where(high == 0, down_rows(0).start, down_rows(1).start), size)
        flying[(0, 4)].wait_recv()
        down_last[...] = own[2 * high + side, pl.ds(at, size), :].astype(f32) + down4[...].astype(f32)
        if minor == 1:
            flying[(0, 5)] = send(
                down_last.at[pl.ds(pl.multiple_of((1 - core) * (size // 2), size // 2), size // 2)],
                down_last_recv,
                (0, 5),
                sibling,
            )

    def vec_step(which, k):
        if k > 0:
            flying[("v", which, k - 1)].wait_recv()
            added = vec_sum[which, k - 1] + vec_recv[which, k - 1]
            if k == 5:
                (vec_a_ref, vec_b_ref)[which][...] = added
                return
            vec_sum[which, k] = added
        device = sibling if k == 0 else partner(CORE_ORDER[k - 1])
        copy = pltpu.make_async_remote_copy(
            src_ref=vec_sum.at[which, k],
            dst_ref=vec_recv.at[which, k],
            send_sem=vec_send.at[which, k],
            recv_sem=vec_recv_sem.at[which, k],
            device_id=device,
            device_id_type=MESH,
        )
        copy.start()
        flying[("v", which, k)] = copy

    def merge():
        load_wo.wait()
        mixed[...] = (
            x_ref[...].astype(f32) + dot(attended_ref[...], wo[...]) + as_row(out_bias_ref)
        )
        hat, _ = normal_parts(mixed[...])
        mid_low = (hat * as_row(mid_gain_ref) + as_row(mid_shift_ref)).astype(low)
        mid[...] = mid_low
        mid_t[...] = mid_low.T

    def quarter(c):
        return slice(c * width, (c + 1) * width)

    def expand(c):
        lanes = quarter(c)
        hidden = dot(mid[...], wu[:, lanes]) + as_row(up_bias_ref)[:, lanes]
        cdf = 0.5 * (1.0 + lax.erf(hidden * (0.5**0.5)))
        active = (hidden * cdf).astype(low)
        slope = cdf + hidden * (jnp.exp(-0.5 * hidden * hidden) * ((2.0 * math.pi) ** -0.5))
        act[...] = active
        act_t[...] = active.T
        back = (dot_bt(dy_ref[...], wd[lanes, :]) * slope).astype(low)
        hid_grad[...] = back
        vec_sum[0, 0, 4 + c : 5 + c, :] = column_sum(back.astype(f32))

    def down_weight(c):
        give(c, dot(act_t[...], dy_ref[:, pl.ds(theirs, half)]).astype(low))
        keep(c, dot(act_t[...], dy_ref[:, pl.ds(mine, half)]).astype(low))

    def up_weight(c):
        give(N_DOWN + c, dot(mid_t[...], hid_grad[:, pl.ds(theirs, half)]).astype(low))
        keep(N_DOWN + c, dot(mid_t[...], hid_grad[:, pl.ds(mine, half)]).astype(low))

    def contract(c):
        lanes = quarter(c)
        deeper = dot_bt(hid_grad[...], wu[:, lanes])
        further = dot(act[...], wd[lanes, :])
        if c == 0:
            input_grad_ref[...] = deeper
            total[...] = mixed[...] + as_row(down_bias_ref) + further
        else:
            input_grad_ref[...] += deeper
            total[...] += further

    def norm_back():
        outputs_ref[...] = total[...].astype(low)
        hat, inverse = normal_parts(mixed[...])
        grad = input_grad_ref[...]
        vec_sum[0, 0, 2:3, :] = column_sum(grad * hat)
        vec_sum[0, 0, 3:4, :] = column_sum(grad)
        whole = dy_ref[...].astype(f32) + normal_back(hat, inverse, as_row(mid_gain_ref), grad)
        input_grad_ref[...] = whole
        branch_low = whole.astype(low)
        hid_grad[...] = branch_low
        vec_sum[0, 0, 1:2, :] = column_sum(branch_low.astype(f32))
        vec_sum[0, 0, 0:1, :] = column_sum(dy_ref[...].astype(f32))
        act_t[...] = attended_ref[...].T

    def out_weight():
        give(U_OUT, dot(act_t[...], hid_grad[:, pl.ds(theirs, half)]).astype(low))
        keep(U_OUT, dot(act_t[...], hid_grad[:, pl.ds(mine, half)]).astype(low))

    def attended_back():
        for p in range(pairs):
            att_grad[p] = dot_bt(hid_grad[...], wo[p * PAIR : (p + 1) * PAIR, :]).astype(low)

    load_qkv = []

    def fetch():
        for p in range(pairs):
            for i, src in enumerate((wq_hbm, wk_hbm, wv_hbm)):
                at = (3 * p + i) * PAIR
                load_qkv.append(
                    load(
                        src.at[:, p * PAIR : (p + 1) * PAIR],
                        wu.at[:, at : at + PAIR],
                        7 + 3 * p + i,
                    )
                )
        for copy in (load_nt, load_q, load_k, load_v):
            copy.wait()

    def pair_back(p, slot):
        q, k, v, grad = queries[p], keys[p], values[p], att_grad[p]
        probs_copy(p, slot).wait()
        out = attended_ref[:, p * PAIR : (p + 1) * PAIR]
        product = grad.astype(f32) * out.astype(f32)
        q_t, grad_t = q.T, grad.T
        query_total = jnp.zeros((rows, PAIR), f32)
        key_parts, value_parts = [], []
        for head in range(2):
            share = probs[slot, head]
            delta = jnp.sum(only_head(product, head), axis=1, keepdims=True)
            score = dot_bt(only_head(grad, head), v)
            score = (share.astype(f32) * (score - delta)).astype(low)
            query_total = query_total + dot(score, only_head(k, head))
            at = slice(head * HALF, (head + 1) * HALF)
            key_parts.append(dot(q_t[at, :], score).astype(low))
            value_parts.append(dot(grad_t[at, :], share).astype(low))
        kv_part[p, 0] = jnp.concatenate(key_parts, axis=0).T
        kv_part[p, 1] = jnp.concatenate(value_parts, axis=0).T
        qkv_grad[:, 3 * p * PAIR : (3 * p + 1) * PAIR] = (query_total * HD ** (-0.5)).astype(low)

    own_rows = pl.ds(pl.multiple_of(core * rows, rows), rows)
    their_rows = pl.ds(pl.multiple_of((1 - core) * rows, rows), rows)

    def attention_back(p):
        pair_back(p, p % 2)
        if p + 2 < pairs:
            probs_copy(p + 2, p % 2).start()
        copy = pltpu.make_async_remote_copy(
            src_ref=kv_part.at[p, :, their_rows],
            dst_ref=kv_recv.at[p],
            send_sem=kv_send.at[p],
            recv_sem=kv_recv_sem.at[p],
            device_id=sibling,
            device_id_type=MESH,
        )
        copy.start()
        flying[("kv", p)] = copy

    def qkv_weight(r):
        for i in range(2):
            p = 2 * r + i
            flying[("kv", p)].wait_recv()
            for j in range(2):
                qkv_grad[:, (3 * p + 1 + j) * PAIR : (3 * p + 2 + j) * PAIR] = (
                    kv_part[p, j, own_rows, :] + kv_recv[p, j]
                )
        for which, action in ((1 - core, give), (core, keep)):
            at = pl.multiple_of((2 * r + which) * 3 * PAIR, PAIR)
            action(U_QKV + r, dot(normed_t[...], qkv_grad[:, pl.ds(at, 3 * PAIR)]).astype(low))

    def input_back():
        for copy in load_qkv:
            copy.wait()
        size = 3 * pairs * PAIR
        grad = dot_bt(qkv_grad[...], wu[:, :size])
        hat, inverse = normal_parts(x_ref[...].astype(f32))
        input_grad_ref[...] += normal_back(hat, inverse, as_row(gain_ref), grad)
        vec_sum[1, 0] = jnp.zeros((8, width), f32)
        vec_sum[1, 0, 0:1, :] = column_sum(grad * hat)
        vec_sum[1, 0, 1:2, :] = column_sum(grad)
        for p in range(pairs):
            lanes = slice(p * PAIR, (p + 1) * PAIR)
            for row, j in ((2, 0), (3, 2)):
                part = qkv_grad[:, (3 * p + j) * PAIR : (3 * p + j + 1) * PAIR]
                vec_sum[1, 0, row : row + 1, lanes] = column_sum(part.astype(f32))

    def first_wait():
        pl.semaphore_wait(barrier, len(others))
        load_wu.wait()
        load_wd.wait()

    merge()
    first_wait()
    expand(0)
    down_weight(0)
    up_weight(0)
    contract(0)
    expand(1)
    step(0, 1)
    down_weight(1)
    step(4, 1)
    up_weight(1)
    contract(1)
    expand(2)
    step(1, 1)
    down_weight(2)
    step(5, 1)
    up_weight(2)
    contract(2)
    expand(3)
    down_weight(3)
    step(0, 2)
    up_weight(3)
    step(4, 2)
    contract(3)
    step(2, 1)
    norm_back()
    step(3, 1)
    step(7, 1)
    vec_step(0, 0)
    out_weight()
    attended_back()
    vec_step(0, 1)
    fetch()
    attention_back(0)
    step(4, 3)
    step(1, 2)
    step(5, 2)
    step(8, 1)
    attention_back(1)
    step(6, 1)
    attention_back(2)
    step(4, 4)
    vec_step(0, 2)
    step(2, 2)
    step(3, 2)
    step(7, 2)
    attention_back(3)
    down_pair(0)
    qkv_weight(0)
    attention_back(4)
    finish(4)
    step(5, 3)
    vec_step(0, 3)
    step(6, 2)
    step(8, 2)
    step(9, 1)
    attention_back(5)
    down_pair(1)
    vec_step(0, 4)
    qkv_weight(1)
    qkv_weight(2)
    step(5, 4)
    step(6, 3)
    step(7, 3)
    input_back()
    down_cross()
    step(9, 2)
    step(10, 1)
    vec_step(1, 0)
    step(11, 1)
    step(8, 3)
    vec_step(0, 5)
    step(6, 4)
    vec_step(1, 1)
    finish(5)
    step(7, 4)
    step(9, 3)
    down_finish()
    step(10, 2)
    finish(6)
    step(8, 4)
    step(11, 2)
    vec_step(1, 2)
    finish(7)
    step(9, 4)
    step(10, 3)
    finish(8)
    step(11, 3)
    vec_step(1, 3)
    finish(9)
    step(10, 4)
    step(11, 4)
    vec_step(1, 4)
    finish(10)
    finish(11)
    vec_step(1, 5)

    size = width // GROUPS
    if minor == 1:
        size = size // 2
        keep_rows = pl.ds(pl.multiple_of(core * size, size), size)
        down_rows = pl.ds(pl.multiple_of(core * 4 * size, 4 * size), 4 * size)
        flying[(0, 5)].wait_recv()
        down_out_ref[:, pl.ds(mine, half)] = down_last[down_rows, :]
        down_out_ref[:, pl.ds(theirs, half)] = down_last_recv[...]
        for unit in range(N_DOWN, UNITS):
            flying[(unit, 5)].wait_recv()
            spot = unit - N_DOWN
            if unit < U_OUT:
                target, lanes = up_out_ref, (unit - N_DOWN) * width
            else:
                target, lanes = out_out_ref, 0
            if unit < U_QKV:
                target[:, pl.ds(pl.multiple_of(lanes + mine, half), half)] = last[spot, keep_rows, :]
                target[:, pl.ds(pl.multiple_of(lanes + theirs, half), half)] = last_recv[spot]
            else:
                for which, value in (
                    (core, last[spot, keep_rows, :]),
                    (1 - core, last_recv[spot]),
                ):
                    at = pl.ds(pl.multiple_of((2 * (unit - U_QKV) + which) * PAIR, PAIR), PAIR)
                    for j in range(3):
                        qkv_out_ref[j, :, at] = value[:, j * PAIR : (j + 1) * PAIR]
    else:
        down_out_ref[...] = down_last[...]
        for unit in range(N_DOWN, U_OUT):
            up_out_ref[:, (unit - N_DOWN) * half : (unit - N_DOWN + 1) * half] = last[unit - N_DOWN]
        out_out_ref[...] = last[U_OUT - N_DOWN]
        for r in range(3):
            for j in range(3):
                qkv_out_ref[j, :, r * PAIR : (r + 1) * PAIR] = last[
                    U_QKV - N_DOWN + r, :, j * PAIR : (j + 1) * PAIR
                ]

    for p in range(pairs):
        flying[("kv", p)].wait_send()
    for key, copy in flying.items():
        if key[0] == "v" or (isinstance(key[0], int) and (key[1] > 0 or key[0] in given[-3:])):
            copy.wait_send()


def run_backward(
    x, dy, attended, gain, mid_gain, mid_shift, out_bias, up_bias, down_bias,
    normed_t, queries, keys, values, probs, wo, wu, wd, wq, wk, wv, minor,
):
    rows, width = x.shape
    pairs = width // PAIR
    cols = keys.shape[1]
    hidden = wu.shape[1]
    half = width // 2
    chunk = width // GROUPS
    low, f32 = jnp.bfloat16, jnp.float32
    vmem, hbm = pl.BlockSpec(memory_space=pltpu.VMEM), pl.BlockSpec(memory_space=pl.ANY)
    if minor == 1:
        outs = [(3, chunk // 2, width), (chunk // 2, width), (chunk // 2, hidden), (2 * chunk, width)]
    else:
        outs = [(3, chunk, half), (chunk, half), (chunk, hidden // 2), (4 * chunk, half)]
    return pl.pallas_call(
        partial(backward_kernel, rows, width, pairs, minor),
        out_shape=[
            jax.ShapeDtypeStruct((rows, width), low),
            jax.ShapeDtypeStruct((rows, width), f32),
        ]
        + [jax.ShapeDtypeStruct(shape, f32) for shape in outs]
        + [jax.ShapeDtypeStruct((8, width), f32)] * 2,
        in_specs=[vmem] * 9 + [hbm] * 11,
        out_specs=[vmem] * 8,
        scratch_shapes=[
            pltpu.VMEM((width, width), low),
            pltpu.VMEM((width, hidden), low),
            pltpu.VMEM((hidden, width), low),
            pltpu.VMEM((width, rows), low),
            pltpu.VMEM((pairs, rows, PAIR), low),
            pltpu.VMEM((pairs, cols, PAIR), low),
            pltpu.VMEM((pairs, cols, PAIR), low),
            pltpu.VMEM((2, 2, rows, cols), low),
            pltpu.VMEM((rows, width), f32),
            pltpu.VMEM((rows, width), low),
            pltpu.VMEM((width, rows), low),
            pltpu.VMEM((rows, width), low),
            pltpu.VMEM((rows, width), f32),
            pltpu.VMEM((width, rows), low),
            pltpu.VMEM((rows, width), low),
            pltpu.VMEM((pairs, rows, PAIR), low),
            pltpu.VMEM((rows, 3 * width), low),
            pltpu.VMEM((pairs, 2, cols, PAIR), low),
            pltpu.VMEM((pairs, 2, rows, PAIR), low),
            pltpu.VMEM((UNITS, width, half), low),
            pltpu.VMEM((3, width, half), low),
            pltpu.VMEM((max(LANDING) + 1, width, half), low),
            pltpu.VMEM((UNITS, width // 2, half), low),
            pltpu.VMEM((UNITS, width // 4, half), low),
            pltpu.VMEM((UNITS - N_DOWN, width // 8, half), low),
            pltpu.VMEM((UNITS - N_DOWN, width // 16, half), low),
            pltpu.VMEM((2, width // 4, half), low),
            pltpu.VMEM((width // 4, half), low),
            pltpu.VMEM((UNITS - N_DOWN, chunk, half), f32),
            pltpu.VMEM((UNITS - N_DOWN, chunk // 2, half), f32),
            pltpu.VMEM((4 * chunk, half), f32),
            pltpu.VMEM((2 * chunk, half), f32),
            pltpu.VMEM((2, 5, 8, width), f32),
            pltpu.VMEM((2, 5, 8, width), f32),
            pltpu.SemaphoreType.DMA((7 + 3 * pairs,)),
            pltpu.SemaphoreType.DMA((2,)),
            pltpu.SemaphoreType.DMA((UNITS, 6)),
            pltpu.SemaphoreType.DMA((UNITS, 6)),
            pltpu.SemaphoreType.DMA((pairs,)),
            pltpu.SemaphoreType.DMA((pairs,)),
            pltpu.SemaphoreType.DMA((2, 5)),
            pltpu.SemaphoreType.DMA((2, 5)),
        ],
        compiler_params=pltpu.CompilerParams(
            collective_id=2, has_side_effects=True, vmem_limit_bytes=60 << 20
        ),
    )(
        x, dy, attended, gain, mid_gain, mid_shift, out_bias, up_bias, down_bias,
        normed_t, queries, keys, values, probs, wo, wu, wd, wq, wk, wv,
    )


def finish_kernel(
    outputs_ref, input_grad_ref, qkv_ref, out_ref, up_ref, down_ref, vec_a_ref, vec_b_ref, *rest
):
    outputs_out, input_grad_out, query, key, value, out, up, down = rest[:8]
    vectors = rest[8:]
    outputs_out[...] = outputs_ref[...]
    input_grad_out[...] = input_grad_ref[...]

    def flatten(values, target):
        rows, lanes = values.shape
        parts = lanes // 128
        for j in range(parts):
            target[pl.ds(j, rows, stride=parts), :] = values[:, j * 128 : (j + 1) * 128]

    for j, target in enumerate((query, key, value)):
        flatten(qkv_ref[j], target)
    flatten(out_ref[...], out)
    flatten(up_ref[...], up)
    flatten(down_ref[...], down)
    lines = [vec_b_ref[j, :] for j in range(4)] + [vec_a_ref[j, :] for j in (1, 2, 3)]
    for line, target in zip(lines, vectors[:7]):
        target[...] = line
    width = vec_a_ref.shape[1]
    for j in range(4):
        vectors[7][j * width : (j + 1) * width] = vec_a_ref[4 + j, :]
    vectors[8][...] = vec_a_ref[0, :]


def run_finish(outputs, input_grad, qkv, out, up, down, vec_a, vec_b):
    f32 = jnp.float32
    width = vec_a.shape[1]
    vmem = pl.BlockSpec(memory_space=pltpu.VMEM)
    flat = lambda size: jax.ShapeDtypeStruct((size // 128, 128), f32)
    line = lambda size: jax.ShapeDtypeStruct((size,), f32)
    return pl.pallas_call(
        finish_kernel,
        out_shape=[
            jax.ShapeDtypeStruct(outputs.shape, outputs.dtype),
            jax.ShapeDtypeStruct(input_grad.shape, f32),
            *(flat(qkv[0].size) for _ in range(3)),
            *(flat(part.size) for part in (out, up, down)),
            *(line(width) for _ in range(7)),
            line(4 * width),
            line(width),
        ],
        in_specs=[vmem] * 8,
        out_specs=[vmem] * 17,
    )(outputs, input_grad, qkv, out, up, down, vec_a, vec_b)


def local(
    incoming_vectors,
    caption_labels,
    loss_sensitivity,
    asking_projection,
    lookup_projection,
    content_projection,
    attention_result_projection,
    expansion_projection,
    contraction_projection,
    attention_norm_scale,
    attention_norm_offset,
    asking_offset,
    content_offset,
    attention_result_offset,
    feedforward_norm_scale,
    feedforward_norm_offset,
    expansion_offset,
    contraction_offset,
):
    seqs, rows, width = incoming_vectors.shape
    chips = lax.axis_size("seq")
    minor = chips // GROUPS
    core = lax.axis_index("blk")
    x = incoming_vectors.reshape(rows, width)
    dy = loss_sensitivity.reshape(rows, width)
    normed_t, queries, keys, values, attended, probs = run_attention(
        x,
        caption_labels,
        attention_norm_scale,
        attention_norm_offset,
        asking_offset,
        content_offset,
        asking_projection,
        lookup_projection,
        content_projection,
    )
    outputs, input_grad, qkv_sum, out_sum, up_sum, down_sum, vec_a, vec_b = run_backward(
        x,
        dy,
        attended,
        attention_norm_scale,
        feedforward_norm_scale,
        feedforward_norm_offset,
        attention_result_offset,
        expansion_offset,
        contraction_offset,
        normed_t,
        queries,
        keys,
        values,
        probs,
        attention_result_projection,
        expansion_projection,
        contraction_projection,
        asking_projection,
        lookup_projection,
        content_projection,
        minor,
    )
    if minor > 1:
        teams = [[g * minor + i for i in range(minor)] for g in range(GROUPS)]
        own_half = lambda values: lax.dynamic_slice_in_dim(
            values, core * (values.shape[0] // 2), values.shape[0] // 2, 0
        )

        def rest(part, pieces):
            both = lax.all_gather(part.reshape(part.shape[0], pieces, -1), "blk", axis=2)
            whole = both.reshape(part.shape[0], -1)
            return own_half(
                lax.psum_scatter(whole, "seq", axis_index_groups=teams, tiled=True)
            )

        qkv_sum = [rest(qkv_sum[i], 3) for i in range(3)]
        out_sum, up_sum, down_sum = rest(out_sum, 1), rest(up_sum, 4), rest(down_sum, 1)
        vec_a, vec_b = lax.psum((vec_a, vec_b), "seq", axis_index_groups=teams)
        qkv_sum = jnp.stack(qkv_sum)
    flat = run_finish(outputs, input_grad, qkv_sum, out_sum, up_sum, down_sum, vec_a, vec_b)
    return (
        flat[0].reshape(seqs, rows, width),
        flat[1].reshape(seqs, rows, width),
        *(part.reshape(-1) for part in flat[2:]),
    )


def solution(mesh):
    in_specs = (
        P("seq", "blk", None),
        P("seq", None),
        P("seq", "blk", None),
        P(),
        P(),
        P(),
        P(),
        P(),
        P(),
        P(),
        P(),
        P(),
        P(),
        P(),
        P(),
        P(),
        P(),
        P(),
    )
    out_specs = (
        P("seq", "blk", None),
        P("seq", "blk", None),
        P(("seq", "blk")),
        P(("seq", "blk")),
        P(("seq", "blk")),
        P(("seq", "blk")),
        P(("seq", "blk")),
        P(("seq", "blk")),
        P(),
        P(),
        P(),
        P(),
        P(),
        P(),
        P(),
        P(),
        P(),
    )
    return jax.shard_map(local, mesh=mesh, in_specs=in_specs, out_specs=out_specs, check_vma=False)
```

```python
import math
from functools import partial

import jax
import jax.numpy as jnp
from jax import lax
from jax.experimental import pallas as pl
from jax.experimental.pallas import tpu as pltpu
from jax.sharding import PartitionSpec as P

HD = 64
MESH = pl.DeviceIdType.MESH


epsilon = 1e-05
masked_value = -1e30

HALF = 64
PAIR = 2 * HALF
LABELS = 9


def lane_mask(rows, head):
    lanes = lax.broadcasted_iota(jnp.int32, (rows, PAIR), 1)
    return (lanes < HALF) if head == 0 else (lanes >= HALF)


def only_head(values, head):
    return jnp.where(lane_mask(values.shape[0], head), values, jnp.zeros_like(values))


def as_row(ref):
    return ref[...].reshape(1, ref.shape[0])


def dot(left, right):
    return jnp.dot(left, right, preferred_element_type=jnp.float32)


def dot_bt(left, right):
    return lax.dot_general(left, right, (((1,), (1,)), ((), ())), preferred_element_type=jnp.float32)


def both(first, second):
    return jnp.where(lane_mask(first.shape[0], 0), first, second)


def standardize(values, gain, shift):
    center = values - jnp.mean(values, axis=-1, keepdims=True)
    spread = jnp.mean(center * center, axis=-1, keepdims=True)
    return center * lax.rsqrt(spread + epsilon) * gain + shift


X_BIT, Y_BIT, Z_BIT, ZZ_BIT = 1, 2, 4, 8
GROUPS = 16
CORE_ORDER = (X_BIT, Y_BIT, Z_BIT, ZZ_BIT)
N_DOWN, N_UP = 4, 4
U_OUT = N_DOWN + N_UP
U_QKV = U_OUT + 1
UNITS = U_QKV + 3
PARTS = (
    (0, 0, 384, (X_BIT, Y_BIT)),
    (1, 0, 384, (X_BIT, Y_BIT)),
    (2, 0, 384, (Y_BIT, X_BIT)),
    (3, 0, 384, (Y_BIT, X_BIT)),
    (4, 0, 384, (Z_BIT, ZZ_BIT, Y_BIT, X_BIT)),
    (5, 0, 384, (Y_BIT, Z_BIT, ZZ_BIT, X_BIT)),
    (6, 0, 384, (Z_BIT, ZZ_BIT, Y_BIT, X_BIT)),
    (7, 0, 384, (X_BIT, Z_BIT, ZZ_BIT, Y_BIT)),
    (8, 0, 384, (X_BIT, Y_BIT, Z_BIT, ZZ_BIT)),
    (9, 0, 384, (Y_BIT, X_BIT, Z_BIT, ZZ_BIT)),
    (10, 0, 384, (Y_BIT, X_BIT, Z_BIT, ZZ_BIT)),
    (11, 0, 384, (X_BIT, Y_BIT, Z_BIT, ZZ_BIT)),
)
PART_SEMS = len(PARTS)
LANDING = (0, 1, 2, 3, 4, 5, 6, 7, 0, 1, 2, 4)


def place_of(group, order):
    place = 0
    for bit in order:
        place = 2 * place + (1 if group & bit else 0)
    return place


def normal_parts(values):
    center = values - jnp.mean(values, axis=-1, keepdims=True)
    spread = jnp.mean(center * center, axis=-1, keepdims=True)
    inverse = lax.rsqrt(spread + epsilon)
    return center * inverse, inverse


def normal_back(hat, inverse, gain, grad):
    scaled = grad * gain
    first = jnp.mean(scaled, axis=-1, keepdims=True)
    second = jnp.mean(scaled * hat, axis=-1, keepdims=True)
    return inverse * (scaled - first - hat * second)


def column_sum(values):
    return jnp.sum(values, axis=0, keepdims=True)


def layer_kernel(
    rows,
    width,
    pairs,
    minor,
    x_hbm,
    dy_hbm,
    all_ids_ref,
    gain_ref,
    shift_ref,
    query_bias_ref,
    value_bias_ref,
    mid_gain_ref,
    mid_shift_ref,
    out_bias_ref,
    up_bias_ref,
    down_bias_ref,
    wo_hbm,
    wu_hbm,
    wd_hbm,
    wq_hbm,
    wk_hbm,
    wv_hbm,
    outputs_hbm,
    input_grad_hbm,
    qkv_out_ref,
    out_out_ref,
    up_out_ref,
    down_out_ref,
    vec_a_ref,
    vec_b_ref,
    probs_hbm,
    input_grad_ref,
    big,
    inverse_ref,
    row_codes,
    col_codes,
    row_ids,
    x_ref,
    dy_ref,
    attended_ref,
    wo,
    wu,
    wd,
    normed_t,
    queries,
    keys,
    values,
    probs,
    mid,
    mid_t,
    act,
    outputs,
    act_t,
    hid_grad,
    att_grad,
    qkv_grad,
    kv_part,
    kv_recv,
    own,
    stage,
    recv0,
    recv1,
    recv2,
    recv3,
    recv4,
    down3,
    down4,
    last,
    last_recv,
    down_last,
    down_last_recv,
    vec_sum,
    vec_recv,
    swap_send,
    swap_recv,
    load_sems,
    save_sems,
    probs_sems,
    unit_send,
    unit_recv,
    give_send,
    give_recv,
    kv_send,
    kv_recv_sem,
    vec_send,
    vec_recv_sem,
):
    low = jnp.bfloat16
    f32 = jnp.float32
    half = width // 2
    cols = all_ids_ref.shape[1]
    scores = (big.at[0], big.at[1])
    mixed, total = big.at[0, :, pl.ds(0, width)], big.at[1, :, pl.ds(0, width)]
    chip, core = lax.axis_index("seq"), lax.axis_index("blk")
    group = lax.div(chip, minor)

    def my_bit(bit):
        return lax.rem(lax.div(group, bit), 2)

    def partner(bit):
        return (chip + (1 - 2 * my_bit(bit)) * (bit * minor), core)

    sibling = (chip, 1 - core)
    mine = pl.multiple_of(core * half, half)
    theirs = pl.multiple_of((1 - core) * half, half)

    def load(src, dst, i):
        copy = pltpu.make_async_copy(src, dst, load_sems.at[i])
        copy.start()
        return copy

    saves = []

    def save(src, dst, i):
        copy = pltpu.make_async_copy(src, dst, save_sems.at[i])
        copy.start()
        saves.append(copy)

    load_x = load(x_hbm, x_ref, 0)
    load_w = [
        [
            load(src.at[:, pl.ds(h * half, half)], own.at[6 + 2 * i + h], 1 + 2 * i + h)
            for h in range(2)
        ]
        for i, src in ((1, wk_hbm), (2, wv_hbm), (0, wq_hbm))
    ]

    def probs_copy(p, slot):
        return pltpu.make_async_copy(probs_hbm.at[p - 2], probs.at[slot], probs_sems.at[slot])

    def probs_save(i):
        slot = lax.rem(i, 2)
        return pltpu.make_async_copy(probs.at[slot], probs_hbm.at[i], probs_sems.at[slot])

    barrier = pltpu.get_barrier_semaphore()
    others = [sibling] + [partner(bit) for bit in CORE_ORDER]
    for device in others:
        pl.semaphore_signal(barrier, inc=1, device_id=device, device_id_type=MESH)

    def send(src, dst, sems_at, device, start=True):
        copy = pltpu.make_async_remote_copy(
            src_ref=src,
            dst_ref=dst,
            send_sem=unit_send.at[sems_at],
            recv_sem=unit_recv.at[sems_at],
            device_id=device,
            device_id_type=MESH,
        )
        if start:
            copy.start()
        return copy

    given = []
    flying = {}
    base = {}
    landed = set()
    recvs = (recv0, recv1, recv2, recv3, recv4)

    def lanes_of(part):
        unit, start, count, order = PARTS[part]
        return unit, slice(start, start + count), order

    def parts_of(unit):
        return [part for part in range(len(PARTS)) if PARTS[part][0] == unit]

    def put(unit, target, value):
        for part in parts_of(unit):
            _, lanes, order = lanes_of(part)
            if unit < N_DOWN:
                step = width // 4
                for yx in range(4):
                    at = place_of(yx, order) * step
                    target[at : at + step, lanes] = value[yx * step : (yx + 1) * step, lanes]
            else:
                step = width // GROUPS
                for g in range(GROUPS):
                    at = place_of(g, order) * step
                    target[at : at + step, lanes] = value[g * step : (g + 1) * step, lanes]

    def give(unit, value):
        slot = len(given) % stage.shape[0]
        if len(given) >= stage.shape[0]:
            flying[("give", given[-stage.shape[0]])].wait_send()
        given.append(unit)
        put(unit, stage.at[slot], value)
        copy = pltpu.make_async_remote_copy(
            src_ref=stage.at[slot],
            dst_ref=recv0.at[LANDING[unit]],
            send_sem=give_send.at[unit],
            recv_sem=give_recv.at[unit],
            device_id=sibling,
            device_id_type=MESH,
        )
        copy.start()
        flying[("give", unit)] = copy

    def keep(unit, value):
        put(unit, own.at[unit], value)
        for part in parts_of(unit):
            base[part] = 0

    def arrived(part, k):
        unit, lanes, _ = lanes_of(part)
        if k > 0:
            flying[(part, k)].wait_recv()
        elif unit not in landed:
            landed.add(unit)
            flying[("give", unit)].wait_recv()
        if k == 0:
            return recv0.at[LANDING[unit], :, lanes]
        return recvs[k].at[unit if k < 3 else unit - N_DOWN, :, lanes]

    def step(part, k):
        unit, lanes, order = lanes_of(part)
        size = (width >> (k - 1)) // 2
        bit = order[k - 1]
        side = my_bit(bit)
        at = base[part]
        got = arrived(part, k - 1)
        away = pl.ds(pl.multiple_of((1 - side) * size, size), size)
        away_own = pl.ds(pl.multiple_of(at + (1 - side) * size, size), size)
        stay = pl.ds(pl.multiple_of(side * size, size), size)
        stay_own = pl.ds(pl.multiple_of(at + side * size, size), size)
        own[unit, away_own, lanes] += got[away, :]
        flying[(part, k)] = send(
            own.at[unit, away_own, lanes],
            recvs[k].at[unit if k < 3 else unit - N_DOWN, :, lanes],
            (part, k),
            partner(bit),
        )
        own[unit, stay_own, lanes] += got[stay, :]
        base[part] = at + side * size

    def finish(part):
        unit, lanes, _ = lanes_of(part)
        size = width >> 4
        got = arrived(part, 4)
        at = pl.ds(pl.multiple_of(base[part], size), size)
        spot = unit - N_DOWN
        last[spot, :, lanes] = own[unit, at, lanes].astype(f32) + got[...].astype(f32)
        if minor == 1:
            size = size // 2
            rows_away = pl.ds(pl.multiple_of((1 - core) * size, size), size)
            flying[(part, 5)] = send(
                last.at[spot, rows_away, lanes], last_recv.at[spot, :, lanes], (part, 5), sibling
            )

    def down_pair(pair):
        size = width // 4
        side = my_bit(Z_BIT)
        for c in (0, 1):
            unit = 2 * pair + c
            flying[(unit, 2)].wait_recv()
            at = pl.ds(pl.multiple_of(base[unit], size), size)
            own[unit, at, :] += recv2[unit]
        away = 2 * pair + 1 - side
        at0, at1 = base[2 * pair], base[2 * pair + 1]
        at = jnp.where(side == 1, at0, at1)
        flying[(2 * pair, 3)] = send(
            own.at[away, pl.ds(pl.multiple_of(at, size), size)],
            down3.at[pair],
            (2 * pair, 3),
            partner(Z_BIT),
        )

    def down_rows(pair):
        at = jnp.where(my_bit(Z_BIT) == 0, base[2 * pair], base[2 * pair + 1])
        return pl.ds(pl.multiple_of(at, width // 4), width // 4)

    def down_cross():
        side, high = my_bit(Z_BIT), my_bit(ZZ_BIT)
        for pair in (0, 1):
            flying[(2 * pair, 3)].wait_recv()
            own[2 * pair + side, down_rows(pair), :] += down3[pair]
        at = pl.multiple_of(jnp.where(high == 1, down_rows(0).start, down_rows(1).start), width // 4)
        flying[(0, 4)] = send(
            own.at[2 * (1 - high) + side, pl.ds(at, width // 4)], down4, (0, 4), partner(ZZ_BIT)
        )

    def down_finish():
        size = width // 4
        side, high = my_bit(Z_BIT), my_bit(ZZ_BIT)
        at = pl.multiple_of(jnp.where(high == 0, down_rows(0).start, down_rows(1).start), size)
        flying[(0, 4)].wait_recv()
        down_last[...] = own[2 * high + side, pl.ds(at, size), :].astype(f32) + down4[...].astype(f32)
        if minor == 1:
            flying[(0, 5)] = send(
                down_last.at[pl.ds(pl.multiple_of((1 - core) * (size // 2), size // 2), size // 2)],
                down_last_recv,
                (0, 5),
                sibling,
            )

    def vec_step(which, k):
        if k > 0:
            flying[("v", which, k - 1)].wait_recv()
            added = vec_sum[which, k - 1] + vec_recv[which, k - 1]
            if k == 5:
                (vec_a_ref, vec_b_ref)[which][...] = added
                return
            vec_sum[which, k] = added
        device = sibling if k == 0 else partner(CORE_ORDER[k - 1])
        copy = pltpu.make_async_remote_copy(
            src_ref=vec_sum.at[which, k],
            dst_ref=vec_recv.at[which, k],
            send_sem=vec_send.at[which, k],
            recv_sem=vec_recv_sem.at[which, k],
            device_id=device,
            device_id_type=MESH,
        )
        copy.start()
        flying[("v", which, k)] = copy

    own_rows = pl.ds(pl.multiple_of(core * rows, rows), rows)
    their_rows = pl.ds(pl.multiple_of((1 - core) * rows, rows), rows)

    ids = jnp.broadcast_to(all_ids_ref[...].astype(f32), (8, cols)).T
    row_ids[...] = ids
    own_ids, all_ids = row_ids[own_rows, 0:1], ids[:, 0:1]
    lanes = lax.broadcasted_iota(jnp.int32, (rows, PAIR), 1).astype(f32)
    row_codes[...] = jnp.where(own_ids == lanes, 1.0, 0.0).astype(low)
    lanes = lax.broadcasted_iota(jnp.int32, (cols, PAIR), 1).astype(f32)
    barred = (all_ids != 0) & (all_ids != lanes) & (lanes < LABELS)
    col_codes[...] = jnp.where(barred, masked_value, 0.0).astype(low)

    query_bias, value_bias = as_row(query_bias_ref), as_row(value_bias_ref)
    load_x.wait()
    normed = standardize(x_ref[...].astype(f32), as_row(gain_ref), as_row(shift_ref)).astype(low)

    def projected(i, loads):
        for copy in loads:
            copy.wait()
        return dot(normed, jnp.concatenate([own[6 + 2 * i], own[7 + 2 * i]], axis=1))

    def spread(target, at, value):
        for p in range(pairs):
            target[p, at, :] = value[:, p * PAIR : (p + 1) * PAIR]

    spread(keys, own_rows, projected(1, load_w[0]).astype(low))
    pl.semaphore_wait(barrier, len(others))
    swaps = [
        pltpu.make_async_remote_copy(
            src_ref=buf.at[:, own_rows],
            dst_ref=buf.at[:, own_rows],
            send_sem=swap_send.at[i],
            recv_sem=swap_recv.at[i],
            device_id=sibling,
            device_id_type=MESH,
        )
        for i, buf in enumerate((keys, values))
    ]
    swaps[0].start()
    spread(values, own_rows, (projected(2, load_w[1]) + value_bias).astype(low))
    swaps[1].start()
    asked = (projected(0, load_w[2]) + query_bias).astype(low)
    spread(queries, slice(None), asked * jnp.bfloat16(HD ** (-0.5)))
    normed_t[...] = normed.T
    load_wo = load(wo_hbm, wo, 7)
    load_wu = load(wu_hbm, wu, 8)
    load_dy = load(dy_hbm, dy_ref, 9)
    load_wd = load(wd_hbm, wd, 10)
    inverse_ref[...] = jnp.zeros((rows, PAIR), f32)
    for swap in swaps:
        swap.wait_recv()

    def score(p, head):
        q_codes = jnp.concatenate([only_head(queries[p], head), row_codes[...]], axis=1)
        k_codes = jnp.concatenate([keys[p], col_codes[...]], axis=1)
        scores[head][...] = dot_bt(q_codes, k_codes)

    def blend(p, slot, head):
        part = scores[head][...]
        expo = jnp.exp(part - jnp.max(part, axis=1, keepdims=True)).astype(low)
        probs[slot, head] = expo
        v = values[p]
        return dot(expo, jnp.where(lane_mask(cols, head), v, jnp.ones_like(v)))

    score(2, 0)

    def pair_step(i, carry):
        p, slot = lax.rem(i + 2, pairs), lax.rem(i, 2)

        @pl.when(i >= 2)
        def _():
            probs_save(i - 2).wait()

        score(p, 1)
        first = blend(p, slot, 0)
        score(lax.rem(i + 3, pairs), 0)
        second = blend(p, slot, 1)

        @pl.when(i < pairs - 2)
        def _():
            probs_save(i).start()

        share = 1.0 / pltpu.roll(both(second, first), HALF, 1)
        at = pl.ds(pl.multiple_of(p * PAIR, PAIR), PAIR)
        attended_ref[:, at] = (both(first, second) * share).astype(low)
        lanes = lax.broadcasted_iota(jnp.int32, (rows, PAIR), 1)
        inverse_ref[...] = jnp.where((lanes == p) | (lanes == HALF + p), share, inverse_ref[...])
        return carry

    lax.fori_loop(0, pairs, pair_step, 0)

    def merge():
        load_wo.wait()
        mixed[...] = (
            x_ref[...].astype(f32) + dot(attended_ref[...], wo[...]) + as_row(out_bias_ref)
        )
        hat, _ = normal_parts(mixed[...])
        mid_low = (hat * as_row(mid_gain_ref) + as_row(mid_shift_ref)).astype(low)
        mid[...] = mid_low
        mid_t[...] = mid_low.T

    def quarter(c):
        return slice(c * width, (c + 1) * width)

    def expand(c):
        lanes = quarter(c)
        hidden = dot(mid[...], wu[:, lanes]) + as_row(up_bias_ref)[:, lanes]
        cdf = 0.5 * (1.0 + lax.erf(hidden * (0.5**0.5)))
        active = (hidden * cdf).astype(low)
        slope = cdf + hidden * (jnp.exp(-0.5 * hidden * hidden) * ((2.0 * math.pi) ** -0.5))
        act[...] = active
        act_t[...] = active.T
        back = (dot_bt(dy_ref[...], wd[lanes, :]) * slope).astype(low)
        hid_grad[...] = back
        vec_sum[0, 0, 4 + c : 5 + c, :] = column_sum(back.astype(f32))

    def weigh(unit, left_t, right):
        product = dot(left_t, right).astype(low)
        first, second = product[:, :half], product[:, half:]
        give(unit, jnp.where(core == 0, second, first))
        keep(unit, jnp.where(core == 0, first, second))

    def down_weight(c):
        weigh(c, act_t[...], dy_ref[...])

    def up_weight(c):
        weigh(N_DOWN + c, mid_t[...], hid_grad[...])

    def contract(c):
        lanes = quarter(c)
        deeper = dot_bt(hid_grad[...], wu[:, lanes])
        further = dot(act[...], wd[lanes, :])
        if c == 0:
            input_grad_ref[...] = deeper
            total[...] = mixed[...] + as_row(down_bias_ref) + further
        else:
            input_grad_ref[...] += deeper
            total[...] += further

    def norm_back():
        outputs[...] = total[...].astype(low)
        save(outputs, outputs_hbm, 0)
        hat, inverse = normal_parts(mixed[...])
        grad = input_grad_ref[...]
        vec_sum[0, 0, 2:3, :] = column_sum(grad * hat)
        vec_sum[0, 0, 3:4, :] = column_sum(grad)
        whole = dy_ref[...].astype(f32) + normal_back(hat, inverse, as_row(mid_gain_ref), grad)
        input_grad_ref[...] = whole
        branch_low = whole.astype(low)
        hid_grad[...] = branch_low
        vec_sum[0, 0, 1:2, :] = column_sum(branch_low.astype(f32))
        vec_sum[0, 0, 0:1, :] = column_sum(dy_ref[...].astype(f32))
        act_t[...] = attended_ref[...].T

    def out_weight():
        weigh(U_OUT, act_t[...], hid_grad[...])

    def attended_back():
        grad = dot_bt(hid_grad[...], wo[...])
        for p in range(pairs):
            share = both(inverse_ref[:, p : p + 1], inverse_ref[:, HALF + p : HALF + p + 1])
            att_grad[p] = (grad[:, p * PAIR : (p + 1) * PAIR] * share).astype(low)

    load_qkv = []

    def fetch():
        for p in range(pairs):
            for i, src in enumerate((wq_hbm, wk_hbm, wv_hbm)):
                at = (3 * p + i) * PAIR
                load_qkv.append(
                    load(
                        src.at[:, p * PAIR : (p + 1) * PAIR],
                        wu.at[:, at : at + PAIR],
                        11 + 3 * p + i,
                    )
                )

    def pair_back(p, slot):
        q, k, v, grad = queries[p], keys[p], values[p], att_grad[p]
        if p >= 2:
            probs_copy(p, slot).wait()
        out = attended_ref[:, p * PAIR : (p + 1) * PAIR]
        product = grad.astype(f32) * out.astype(f32)
        q_t, grad_t = q.T, grad.T
        query_total = jnp.zeros((rows, PAIR), f32)
        key_parts, value_parts = [], []
        for head in range(2):
            share = probs[slot, head]
            delta = jnp.sum(only_head(product, head), axis=1, keepdims=True)
            score = dot_bt(only_head(grad, head), v)
            score = (share.astype(f32) * (score - delta)).astype(low)
            query_total = query_total + dot(score, only_head(k, head))
            at = slice(head * HALF, (head + 1) * HALF)
            key_parts.append(dot(q_t[at, :], score).astype(low))
            value_parts.append(dot(grad_t[at, :], share).astype(low))
        kv_part[p % kv_part.shape[0], 0] = jnp.concatenate(key_parts, axis=0).T
        kv_part[p % kv_part.shape[0], 1] = jnp.concatenate(value_parts, axis=0).T
        qkv_grad[:, 3 * p * PAIR : (3 * p + 1) * PAIR] = (query_total * HD ** (-0.5)).astype(low)

    def attention_back(p):
        if p >= kv_part.shape[0]:
            flying[("kv", p - kv_part.shape[0])].wait_send()
        pair_back(p, p % 2)
        if p + 2 < pairs:
            probs_copy(p + 2, p % 2).start()
        copy = pltpu.make_async_remote_copy(
            src_ref=kv_part.at[p % kv_part.shape[0], :, their_rows],
            dst_ref=kv_recv.at[p],
            send_sem=kv_send.at[p],
            recv_sem=kv_recv_sem.at[p],
            device_id=sibling,
            device_id_type=MESH,
        )
        copy.start()
        flying[("kv", p)] = copy

    def qkv_weight(r):
        for i in range(2):
            p = 2 * r + i
            flying[("kv", p)].wait_recv()
            for j in range(2):
                qkv_grad[:, (3 * p + 1 + j) * PAIR : (3 * p + 2 + j) * PAIR] = (
                    kv_part[p % kv_part.shape[0], j, own_rows, :] + kv_recv[p, j]
                )
        weigh(U_QKV + r, normed_t[...], qkv_grad[:, 6 * r * PAIR : 6 * (r + 1) * PAIR])

    def input_back():
        for copy in load_qkv:
            copy.wait()
        size = 3 * pairs * PAIR
        grad = dot_bt(qkv_grad[...], wu[:, :size])
        hat, inverse = normal_parts(x_ref[...].astype(f32))
        input_grad_ref[...] += normal_back(hat, inverse, as_row(gain_ref), grad)
        save(input_grad_ref, input_grad_hbm, 1)
        vec_sum[1, 0] = jnp.zeros((8, width), f32)
        vec_sum[1, 0, 0:1, :] = column_sum(grad * hat)
        vec_sum[1, 0, 1:2, :] = column_sum(grad)
        for p in range(pairs):
            lanes = slice(p * PAIR, (p + 1) * PAIR)
            for row, j in ((2, 0), (3, 2)):
                part = qkv_grad[:, (3 * p + j) * PAIR : (3 * p + j + 1) * PAIR]
                vec_sum[1, 0, row : row + 1, lanes] = column_sum(part.astype(f32))

    def first_wait():
        for copy in (load_wu, load_dy, load_wd):
            copy.wait()

    merge()
    first_wait()
    expand(0)
    down_weight(0)
    up_weight(0)
    contract(0)
    expand(1)
    step(4, 1)
    up_weight(1)
    step(0, 1)
    down_weight(1)
    contract(1)
    step(5, 1)
    expand(2)
    up_weight(2)
    down_weight(2)
    contract(2)
    step(6, 1)
    step(1, 1)
    expand(3)
    step(2, 1)
    down_weight(3)
    up_weight(3)
    contract(3)
    step(4, 2)
    norm_back()
    vec_step(0, 0)
    step(7, 1)
    out_weight()
    step(0, 2)
    attended_back()
    vec_step(0, 1)
    fetch()
    step(5, 2)
    step(1, 2)
    step(3, 1)
    step(6, 2)
    step(2, 2)
    attention_back(0)
    attention_back(1)
    step(8, 1)
    attention_back(2)
    step(7, 2)
    attention_back(3)
    qkv_weight(0)
    down_pair(0)
    vec_step(0, 2)
    attention_back(4)
    step(9, 1)
    attention_back(5)
    step(3, 2)
    step(5, 3)
    qkv_weight(1)
    qkv_weight(2)
    step(7, 3)
    step(8, 2)
    input_back()
    step(11, 1)
    vec_step(0, 3)
    step(10, 1)
    down_pair(1)
    vec_step(0, 4)
    step(8, 3)
    vec_step(1, 0)
    vec_step(1, 1)
    step(9, 2)
    down_cross()
    step(11, 2)
    step(5, 4)
    vec_step(0, 5)
    step(8, 4)
    vec_step(1, 2)
    step(4, 3)
    step(10, 2)
    step(6, 3)
    step(9, 3)
    step(11, 3)
    vec_step(1, 3)
    step(10, 3)
    step(9, 4)
    step(7, 4)
    finish(5)
    finish(8)
    step(4, 4)
    step(11, 4)
    step(10, 4)
    vec_step(1, 4)
    finish(7)
    step(6, 4)
    finish(9)
    finish(4)
    finish(11)
    finish(6)
    down_finish()
    finish(10)
    vec_step(1, 5)

    size = width // GROUPS
    if minor == 1:
        size = size // 2
        keep_rows = pl.ds(pl.multiple_of(core * size, size), size)
        down_rows = pl.ds(pl.multiple_of(core * 4 * size, 4 * size), 4 * size)
        flying[(0, 5)].wait_recv()
        down_out_ref[:, pl.ds(mine, half)] = down_last[down_rows, :]
        down_out_ref[:, pl.ds(theirs, half)] = down_last_recv[...]
        for part in range(N_DOWN, len(PARTS)):
            flying[(part, 5)].wait_recv()
        for unit in range(N_DOWN, UNITS):
            spot = unit - N_DOWN
            if unit < U_OUT:
                target, lanes = up_out_ref, (unit - N_DOWN) * width
            else:
                target, lanes = out_out_ref, 0
            if unit < U_QKV:
                target[:, pl.ds(pl.multiple_of(lanes + mine, half), half)] = last[spot, keep_rows, :]
                target[:, pl.ds(pl.multiple_of(lanes + theirs, half), half)] = last_recv[spot]
            else:
                for which, value in (
                    (core, last[spot, keep_rows, :]),
                    (1 - core, last_recv[spot]),
                ):
                    at = pl.ds(pl.multiple_of((2 * (unit - U_QKV) + which) * PAIR, PAIR), PAIR)
                    for j in range(3):
                        qkv_out_ref[j, :, at] = value[:, j * PAIR : (j + 1) * PAIR]
    else:
        down_out_ref[...] = down_last[...]
        for unit in range(N_DOWN, U_OUT):
            up_out_ref[:, (unit - N_DOWN) * half : (unit - N_DOWN + 1) * half] = last[unit - N_DOWN]
        out_out_ref[...] = last[U_OUT - N_DOWN]
        for r in range(3):
            for j in range(3):
                qkv_out_ref[j, :, r * PAIR : (r + 1) * PAIR] = last[
                    U_QKV - N_DOWN + r, :, j * PAIR : (j + 1) * PAIR
                ]

    for copy in saves:
        copy.wait()
    for swap in swaps:
        swap.wait_send()
    for p in range(pairs - kv_part.shape[0], pairs):
        flying[("kv", p)].wait_send()
    for key, copy in flying.items():
        if key[0] == "v" or isinstance(key[0], int) or key in [("give", u) for u in given[-2:]]:
            copy.wait_send()


def run_layer(x, dy, ids, vectors, weights, minor):
    rows, width = x.shape
    pairs = width // PAIR
    cols = ids.shape[1]
    hidden = weights[1].shape[1]
    half = width // 2
    chunk = width // GROUPS
    low, f32 = jnp.bfloat16, jnp.float32
    vmem, hbm = pl.BlockSpec(memory_space=pltpu.VMEM), pl.BlockSpec(memory_space=pl.ANY)
    if minor == 1:
        outs = [(3, chunk // 2, width), (chunk // 2, width), (chunk // 2, hidden), (2 * chunk, width)]
    else:
        outs = [(3, chunk, half), (chunk, half), (chunk, hidden // 2), (4 * chunk, half)]
    late = UNITS - N_DOWN
    return pl.pallas_call(
        partial(layer_kernel, rows, width, pairs, minor),
        out_shape=[
            jax.ShapeDtypeStruct((rows, width), low),
            jax.ShapeDtypeStruct((rows, width), f32),
        ]
        + [jax.ShapeDtypeStruct(shape, f32) for shape in outs]
        + [jax.ShapeDtypeStruct((8, width), f32)] * 2
        + [jax.ShapeDtypeStruct((pairs - 2, 2, rows, cols), low)],
        in_specs=[hbm] * 2 + [vmem] * 10 + [hbm] * 6,
        out_specs=[hbm] * 2 + [vmem] * 6 + [hbm],
        scratch_shapes=[
            pltpu.VMEM((rows, width), f32),
            pltpu.VMEM((2, rows, cols), f32),
            pltpu.VMEM((rows, PAIR), f32),
            pltpu.VMEM((rows, PAIR), low),
            pltpu.VMEM((cols, PAIR), low),
            pltpu.VMEM((cols, 8), f32),
            pltpu.VMEM((rows, width), low),
            pltpu.VMEM((rows, width), low),
            pltpu.VMEM((rows, width), low),
            pltpu.VMEM((width, width), low),
            pltpu.VMEM((width, hidden), low),
            pltpu.VMEM((hidden, width), low),
            pltpu.VMEM((width, rows), low),
            pltpu.VMEM((pairs, rows, PAIR), low),
            pltpu.VMEM((pairs, cols, PAIR), low),
            pltpu.VMEM((pairs, cols, PAIR), low),
            pltpu.VMEM((2, 2, rows, cols), low),
            pltpu.VMEM((rows, width), low),
            pltpu.VMEM((width, rows), low),
            pltpu.VMEM((rows, width), low),
            pltpu.VMEM((rows, width), low),
            pltpu.VMEM((width, rows), low),
            pltpu.VMEM((rows, width), low),
            pltpu.VMEM((pairs, rows, PAIR), low),
            pltpu.VMEM((rows, 3 * width), low),
            pltpu.VMEM((4, 2, cols, PAIR), low),
            pltpu.VMEM((pairs, 2, rows, PAIR), low),
            pltpu.VMEM((UNITS, width, half), low),
            pltpu.VMEM((2, width, half), low),
            pltpu.VMEM((max(LANDING) + 1, width, half), low),
            pltpu.VMEM((UNITS, width // 2, half), low),
            pltpu.VMEM((UNITS, width // 4, half), low),
            pltpu.VMEM((late, width // 8, half), low),
            pltpu.VMEM((late, width // 16, half), low),
            pltpu.VMEM((2, width // 4, half), low),
            pltpu.VMEM((width // 4, half), low),
            pltpu.VMEM((late, chunk, half), f32),
            pltpu.VMEM((late, chunk // 2, half), f32),
            pltpu.VMEM((4 * chunk, half), f32),
            pltpu.VMEM((2 * chunk, half), f32),
            pltpu.VMEM((2, 5, 8, width), f32),
            pltpu.VMEM((2, 5, 8, width), f32),
            pltpu.SemaphoreType.DMA((2,)),
            pltpu.SemaphoreType.DMA((2,)),
            pltpu.SemaphoreType.DMA((11 + 3 * pairs,)),
            pltpu.SemaphoreType.DMA((2,)),
            pltpu.SemaphoreType.DMA((2,)),
            pltpu.SemaphoreType.DMA((PART_SEMS, 6)),
            pltpu.SemaphoreType.DMA((PART_SEMS, 6)),
            pltpu.SemaphoreType.DMA((UNITS,)),
            pltpu.SemaphoreType.DMA((UNITS,)),
            pltpu.SemaphoreType.DMA((pairs,)),
            pltpu.SemaphoreType.DMA((pairs,)),
            pltpu.SemaphoreType.DMA((2, 5)),
            pltpu.SemaphoreType.DMA((2, 5)),
        ],
        compiler_params=pltpu.CompilerParams(
            collective_id=1, has_side_effects=True, vmem_limit_bytes=61 << 20
        ),
    )(x, dy, ids, *vectors, *weights)


def finish_kernel(
    outputs_ref, input_grad_ref, qkv_ref, out_ref, up_ref, down_ref, vec_a_ref, vec_b_ref, *rest
):
    outputs_out, input_grad_out, query, key, value, out, up, down = rest[:8]
    vectors = rest[8:]
    outputs_out[...] = outputs_ref[...]
    input_grad_out[...] = input_grad_ref[...]

    def flatten(values, target):
        rows, lanes = values.shape
        parts = lanes // 128
        for j in range(parts):
            target[pl.ds(j, rows, stride=parts), :] = values[:, j * 128 : (j + 1) * 128]

    for j, target in enumerate((query, key, value)):
        flatten(qkv_ref[j], target)
    flatten(out_ref[...], out)
    flatten(up_ref[...], up)
    flatten(down_ref[...], down)
    lines = [vec_b_ref[j, :] for j in range(4)] + [vec_a_ref[j, :] for j in (1, 2, 3)]
    for line, target in zip(lines, vectors[:7]):
        target[...] = line
    width = vec_a_ref.shape[1]
    for j in range(4):
        vectors[7][j * width : (j + 1) * width] = vec_a_ref[4 + j, :]
    vectors[8][...] = vec_a_ref[0, :]


def run_finish(outputs, input_grad, qkv, out, up, down, vec_a, vec_b):
    f32 = jnp.float32
    width = vec_a.shape[1]
    vmem = pl.BlockSpec(memory_space=pltpu.VMEM)
    flat = lambda size: jax.ShapeDtypeStruct((size // 128, 128), f32)
    line = lambda size: jax.ShapeDtypeStruct((size,), f32)
    return pl.pallas_call(
        finish_kernel,
        out_shape=[
            jax.ShapeDtypeStruct(outputs.shape, outputs.dtype),
            jax.ShapeDtypeStruct(input_grad.shape, f32),
            *(flat(qkv[0].size) for _ in range(3)),
            *(flat(part.size) for part in (out, up, down)),
            *(line(width) for _ in range(7)),
            line(4 * width),
            line(width),
        ],
        in_specs=[vmem] * 8,
        out_specs=[vmem] * 17,
    )(outputs, input_grad, qkv, out, up, down, vec_a, vec_b)


def local(
    incoming_vectors,
    caption_labels,
    loss_sensitivity,
    asking_projection,
    lookup_projection,
    content_projection,
    attention_result_projection,
    expansion_projection,
    contraction_projection,
    attention_norm_scale,
    attention_norm_offset,
    asking_offset,
    content_offset,
    attention_result_offset,
    feedforward_norm_scale,
    feedforward_norm_offset,
    expansion_offset,
    contraction_offset,
):
    seqs, rows, width = incoming_vectors.shape
    chips = lax.axis_size("seq")
    minor = chips // GROUPS
    core = lax.axis_index("blk")
    x = incoming_vectors.reshape(rows, width)
    dy = loss_sensitivity.reshape(rows, width)
    vectors = (
        attention_norm_scale,
        attention_norm_offset,
        asking_offset,
        content_offset,
        feedforward_norm_scale,
        feedforward_norm_offset,
        attention_result_offset,
        expansion_offset,
        contraction_offset,
    )
    weights = (
        attention_result_projection,
        expansion_projection,
        contraction_projection,
        asking_projection,
        lookup_projection,
        content_projection,
    )
    outputs, input_grad, qkv_sum, out_sum, up_sum, down_sum, vec_a, vec_b, _ = run_layer(
        x, dy, caption_labels, vectors, weights, minor
    )
    if minor > 1:
        teams = [[g * minor + i for i in range(minor)] for g in range(GROUPS)]
        own_half = lambda values: lax.dynamic_slice_in_dim(
            values, core * (values.shape[0] // 2), values.shape[0] // 2, 0
        )

        def rest(part, pieces):
            both = lax.all_gather(part.reshape(part.shape[0], pieces, -1), "blk", axis=2)
            whole = both.reshape(part.shape[0], -1)
            return own_half(
                lax.psum_scatter(whole, "seq", axis_index_groups=teams, tiled=True)
            )

        qkv_sum = [rest(qkv_sum[i], 3) for i in range(3)]
        out_sum, up_sum, down_sum = rest(out_sum, 1), rest(up_sum, 4), rest(down_sum, 1)
        vec_a, vec_b = lax.psum((vec_a, vec_b), "seq", axis_index_groups=teams)
        qkv_sum = jnp.stack(qkv_sum)
    flat = run_finish(outputs, input_grad, qkv_sum, out_sum, up_sum, down_sum, vec_a, vec_b)
    return (
        flat[0].reshape(seqs, rows, width),
        flat[1].reshape(seqs, rows, width),
        *(part.reshape(-1) for part in flat[2:]),
    )


def solution(mesh):
    in_specs = (
        P("seq", "blk", None),
        P("seq", None),
        P("seq", "blk", None),
        P(),
        P(),
        P(),
        P(),
        P(),
        P(),
        P(),
        P(),
        P(),
        P(),
        P(),
        P(),
        P(),
        P(),
        P(),
    )
    out_specs = (
        P("seq", "blk", None),
        P("seq", "blk", None),
        P(("seq", "blk")),
        P(("seq", "blk")),
        P(("seq", "blk")),
        P(("seq", "blk")),
        P(("seq", "blk")),
        P(("seq", "blk")),
        P(),
        P(),
        P(),
        P(),
        P(),
        P(),
        P(),
        P(),
        P(),
    )
    return jax.shard_map(local, mesh=mesh, in_specs=in_specs, out_specs=out_specs, check_vma=False)
```

```python
import math
from functools import partial

import jax
import jax.numpy as jnp
from jax import lax
from jax.experimental import pallas as pl
from jax.experimental.pallas import tpu as pltpu
from jax.sharding import PartitionSpec as P

HD = 64
MESH = pl.DeviceIdType.MESH


epsilon = 1e-05
masked_value = -1e30

HALF = 64
PAIR = 2 * HALF
LABELS = 9


def lane_mask(rows, head):
    lanes = lax.broadcasted_iota(jnp.int32, (rows, PAIR), 1)
    return (lanes < HALF) if head == 0 else (lanes >= HALF)


def only_head(values, head):
    return jnp.where(lane_mask(values.shape[0], head), values, jnp.zeros_like(values))


def as_row(ref):
    return ref[...].reshape(1, ref.shape[0])


def dot(left, right):
    return jnp.dot(left, right, preferred_element_type=jnp.float32)


def dot_bt(left, right):
    return lax.dot_general(left, right, (((1,), (1,)), ((), ())), preferred_element_type=jnp.float32)


def both(first, second):
    return jnp.where(lane_mask(first.shape[0], 0), first, second)


def standardize(values, gain, shift):
    center = values - jnp.mean(values, axis=-1, keepdims=True)
    spread = jnp.mean(center * center, axis=-1, keepdims=True)
    return center * lax.rsqrt(spread + epsilon) * gain + shift


X_BIT, Y_BIT, Z_BIT, ZZ_BIT = 1, 2, 4, 8
GROUPS = 16
CORE_ORDER = (X_BIT, Y_BIT, Z_BIT, ZZ_BIT)
N_DOWN, N_UP = 4, 4
U_OUT = N_DOWN + N_UP
U_QKV = U_OUT + 1
UNITS = U_QKV + 3
PARTS = (
    (0, 0, 384, (Y_BIT, X_BIT)),
    (1, 0, 384, (X_BIT, Y_BIT)),
    (2, 0, 384, (Y_BIT, X_BIT)),
    (3, 0, 384, (X_BIT, Y_BIT)),
    (4, 0, 384, (Z_BIT, Y_BIT, X_BIT, ZZ_BIT)),
    (5, 0, 128, (Z_BIT, Y_BIT, ZZ_BIT, X_BIT)),
    (5, 128, 128, (Z_BIT, X_BIT, ZZ_BIT, Y_BIT)),
    (5, 256, 128, (Y_BIT, Z_BIT, X_BIT, ZZ_BIT)),
    (6, 0, 256, (Z_BIT, X_BIT, ZZ_BIT, Y_BIT)),
    (6, 256, 128, (Z_BIT, X_BIT, Y_BIT, ZZ_BIT)),
    (7, 0, 128, (Y_BIT, X_BIT, Z_BIT, ZZ_BIT)),
    (7, 128, 256, (Z_BIT, ZZ_BIT, X_BIT, Y_BIT)),
    (8, 0, 128, (Z_BIT, X_BIT, Y_BIT, ZZ_BIT)),
    (8, 128, 128, (Y_BIT, X_BIT, Z_BIT, ZZ_BIT)),
    (8, 256, 128, (X_BIT, Y_BIT, Z_BIT, ZZ_BIT)),
    (9, 0, 256, (Y_BIT, Z_BIT, X_BIT, ZZ_BIT)),
    (9, 256, 128, (Y_BIT, Z_BIT, X_BIT, ZZ_BIT)),
    (10, 0, 128, (Y_BIT, Z_BIT, X_BIT, ZZ_BIT)),
    (10, 128, 256, (X_BIT, Y_BIT, Z_BIT, ZZ_BIT)),
    (11, 0, 256, (Y_BIT, X_BIT, Z_BIT, ZZ_BIT)),
    (11, 256, 128, (X_BIT, Y_BIT, Z_BIT, ZZ_BIT)),
)
PART_SEMS = len(PARTS)
LANDING = (0, 1, 2, 3, 4, 5, 6, 7, 0, 1, 2, 4)


def place_of(group, order):
    place = 0
    for bit in order:
        place = 2 * place + (1 if group & bit else 0)
    return place


def normal_parts(values):
    center = values - jnp.mean(values, axis=-1, keepdims=True)
    spread = jnp.mean(center * center, axis=-1, keepdims=True)
    inverse = lax.rsqrt(spread + epsilon)
    return center * inverse, inverse


def normal_back(hat, inverse, gain, grad):
    scaled = grad * gain
    first = jnp.mean(scaled, axis=-1, keepdims=True)
    second = jnp.mean(scaled * hat, axis=-1, keepdims=True)
    return inverse * (scaled - first - hat * second)


def column_sum(values):
    return jnp.sum(values, axis=0, keepdims=True)


def layer_kernel(
    rows,
    width,
    pairs,
    minor,
    x_hbm,
    dy_hbm,
    all_ids_ref,
    gain_ref,
    shift_ref,
    query_bias_ref,
    value_bias_ref,
    mid_gain_ref,
    mid_shift_ref,
    out_bias_ref,
    up_bias_ref,
    down_bias_ref,
    wo_hbm,
    wu_hbm,
    wd_hbm,
    wq_hbm,
    wk_hbm,
    wv_hbm,
    outputs_hbm,
    input_grad_hbm,
    qkv_out_ref,
    out_out_ref,
    up_out_ref,
    down_out_ref,
    vec_a_ref,
    vec_b_ref,
    probs_hbm,
    input_grad_ref,
    big,
    inverse_ref,
    row_codes,
    col_codes,
    row_ids,
    x_ref,
    dy_ref,
    attended_ref,
    wo,
    wu,
    wd,
    normed_t,
    queries,
    keys,
    values,
    probs,
    mid,
    mid_t,
    act,
    outputs,
    act_t,
    hid_grad,
    att_grad,
    qkv_grad,
    kv_part,
    kv_recv,
    own,
    stage,
    recv0,
    recv1,
    recv2,
    recv3,
    recv4,
    down3,
    down4,
    last,
    last_recv,
    down_last,
    down_last_recv,
    vec_sum,
    vec_recv,
    swap_send,
    swap_recv,
    load_sems,
    save_sems,
    probs_sems,
    unit_send,
    unit_recv,
    give_send,
    give_recv,
    kv_send,
    kv_recv_sem,
    vec_send,
    vec_recv_sem,
):
    low = jnp.bfloat16
    f32 = jnp.float32
    half = width // 2
    cols = all_ids_ref.shape[1]
    scores = (big.at[0], big.at[1])
    mixed, total = big.at[0, :, pl.ds(0, width)], big.at[1, :, pl.ds(0, width)]
    chip, core = lax.axis_index("seq"), lax.axis_index("blk")
    group = lax.div(chip, minor)

    def my_bit(bit):
        return lax.rem(lax.div(group, bit), 2)

    def partner(bit):
        return (chip + (1 - 2 * my_bit(bit)) * (bit * minor), core)

    sibling = (chip, 1 - core)
    mine = pl.multiple_of(core * half, half)
    theirs = pl.multiple_of((1 - core) * half, half)

    def load(src, dst, i):
        copy = pltpu.make_async_copy(src, dst, load_sems.at[i])
        copy.start()
        return copy

    saves = []

    def save(src, dst, i):
        copy = pltpu.make_async_copy(src, dst, save_sems.at[i])
        copy.start()
        saves.append(copy)

    load_x = load(x_hbm, x_ref, 0)
    load_w = [
        [
            load(src.at[:, pl.ds(h * half, half)], own.at[6 + 2 * i + h], 1 + 2 * i + h)
            for h in range(2)
        ]
        for i, src in ((1, wk_hbm), (2, wv_hbm), (0, wq_hbm))
    ]

    def probs_copy(p, slot):
        return pltpu.make_async_copy(probs_hbm.at[p - 2], probs.at[slot], probs_sems.at[slot])

    def probs_save(i):
        slot = lax.rem(i, 2)
        return pltpu.make_async_copy(probs.at[slot], probs_hbm.at[i], probs_sems.at[slot])

    barrier = pltpu.get_barrier_semaphore()
    others = [sibling] + [partner(bit) for bit in CORE_ORDER]
    for device in others:
        pl.semaphore_signal(barrier, inc=1, device_id=device, device_id_type=MESH)

    def send(src, dst, sems_at, device, start=True):
        copy = pltpu.make_async_remote_copy(
            src_ref=src,
            dst_ref=dst,
            send_sem=unit_send.at[sems_at],
            recv_sem=unit_recv.at[sems_at],
            device_id=device,
            device_id_type=MESH,
        )
        if start:
            copy.start()
        return copy

    given = []
    flying = {}
    base = {}
    landed = set()
    recvs = (recv0, recv1, recv2, recv3, recv4)

    def lanes_of(part):
        unit, start, count, order = PARTS[part]
        return unit, slice(start, start + count), order

    def parts_of(unit):
        return [part for part in range(len(PARTS)) if PARTS[part][0] == unit]

    def put(unit, target, value):
        for part in parts_of(unit):
            _, lanes, order = lanes_of(part)
            if unit < N_DOWN:
                step = width // 4
                for yx in range(4):
                    at = place_of(yx, order) * step
                    target[at : at + step, lanes] = value[yx * step : (yx + 1) * step, lanes]
            else:
                step = width // GROUPS
                for g in range(GROUPS):
                    at = place_of(g, order) * step
                    target[at : at + step, lanes] = value[g * step : (g + 1) * step, lanes]

    def give(unit, value):
        slot = len(given) % stage.shape[0]
        if len(given) >= stage.shape[0]:
            flying[("give", given[-stage.shape[0]])].wait_send()
        given.append(unit)
        put(unit, stage.at[slot], value)
        copy = pltpu.make_async_remote_copy(
            src_ref=stage.at[slot],
            dst_ref=recv0.at[LANDING[unit]],
            send_sem=give_send.at[unit],
            recv_sem=give_recv.at[unit],
            device_id=sibling,
            device_id_type=MESH,
        )
        copy.start()
        flying[("give", unit)] = copy

    def keep(unit, value):
        put(unit, own.at[unit], value)
        for part in parts_of(unit):
            base[part] = 0

    def arrived(part, k):
        unit, lanes, _ = lanes_of(part)
        if k > 0:
            flying[(part, k)].wait_recv()
        elif unit not in landed:
            landed.add(unit)
            flying[("give", unit)].wait_recv()
        if k == 0:
            return recv0.at[LANDING[unit], :, lanes]
        return recvs[k].at[unit if k < 3 else unit - N_DOWN, :, lanes]

    def step(part, k):
        unit, lanes, order = lanes_of(part)
        size = (width >> (k - 1)) // 2
        bit = order[k - 1]
        side = my_bit(bit)
        at = base[part]
        got = arrived(part, k - 1)
        away = pl.ds(pl.multiple_of((1 - side) * size, size), size)
        away_own = pl.ds(pl.multiple_of(at + (1 - side) * size, size), size)
        stay = pl.ds(pl.multiple_of(side * size, size), size)
        stay_own = pl.ds(pl.multiple_of(at + side * size, size), size)
        own[unit, away_own, lanes] += got[away, :]
        flying[(part, k)] = send(
            own.at[unit, away_own, lanes],
            recvs[k].at[unit if k < 3 else unit - N_DOWN, :, lanes],
            (part, k),
            partner(bit),
        )
        own[unit, stay_own, lanes] += got[stay, :]
        base[part] = at + side * size

    def finish(part):
        unit, lanes, _ = lanes_of(part)
        size = width >> 4
        got = arrived(part, 4)
        at = pl.ds(pl.multiple_of(base[part], size), size)
        spot = unit - N_DOWN
        last[spot, :, lanes] = own[unit, at, lanes].astype(f32) + got[...].astype(f32)
        if minor == 1:
            size = size // 2
            rows_away = pl.ds(pl.multiple_of((1 - core) * size, size), size)
            flying[(part, 5)] = send(
                last.at[spot, rows_away, lanes], last_recv.at[spot, :, lanes], (part, 5), sibling
            )

    def down_pair(pair):
        size = width // 4
        side = my_bit(Z_BIT)
        for c in (0, 1):
            unit = 2 * pair + c
            flying[(unit, 2)].wait_recv()
            at = pl.ds(pl.multiple_of(base[unit], size), size)
            own[unit, at, :] += recv2[unit]
        away = 2 * pair + 1 - side
        at0, at1 = base[2 * pair], base[2 * pair + 1]
        at = jnp.where(side == 1, at0, at1)
        flying[(2 * pair, 3)] = send(
            own.at[away, pl.ds(pl.multiple_of(at, size), size)],
            down3.at[pair],
            (2 * pair, 3),
            partner(Z_BIT),
        )

    def down_rows(pair):
        at = jnp.where(my_bit(Z_BIT) == 0, base[2 * pair], base[2 * pair + 1])
        return pl.ds(pl.multiple_of(at, width // 4), width // 4)

    def down_cross():
        side, high = my_bit(Z_BIT), my_bit(ZZ_BIT)
        for pair in (0, 1):
            flying[(2 * pair, 3)].wait_recv()
            own[2 * pair + side, down_rows(pair), :] += down3[pair]
        at = pl.multiple_of(jnp.where(high == 1, down_rows(0).start, down_rows(1).start), width // 4)
        flying[(0, 4)] = send(
            own.at[2 * (1 - high) + side, pl.ds(at, width // 4)], down4, (0, 4), partner(ZZ_BIT)
        )

    def down_finish():
        size = width // 4
        side, high = my_bit(Z_BIT), my_bit(ZZ_BIT)
        at = pl.multiple_of(jnp.where(high == 0, down_rows(0).start, down_rows(1).start), size)
        flying[(0, 4)].wait_recv()
        down_last[...] = own[2 * high + side, pl.ds(at, size), :].astype(f32) + down4[...].astype(f32)
        if minor == 1:
            flying[(0, 5)] = send(
                down_last.at[pl.ds(pl.multiple_of((1 - core) * (size // 2), size // 2), size // 2)],
                down_last_recv,
                (0, 5),
                sibling,
            )

    def vec_step(which, k):
        if k > 0:
            flying[("v", which, k - 1)].wait_recv()
            added = vec_sum[which, k - 1] + vec_recv[which, k - 1]
            if k == 5:
                (vec_a_ref, vec_b_ref)[which][...] = added
                return
            vec_sum[which, k] = added
        device = sibling if k == 0 else partner(CORE_ORDER[k - 1])
        copy = pltpu.make_async_remote_copy(
            src_ref=vec_sum.at[which, k],
            dst_ref=vec_recv.at[which, k],
            send_sem=vec_send.at[which, k],
            recv_sem=vec_recv_sem.at[which, k],
            device_id=device,
            device_id_type=MESH,
        )
        copy.start()
        flying[("v", which, k)] = copy

    own_rows = pl.ds(pl.multiple_of(core * rows, rows), rows)
    their_rows = pl.ds(pl.multiple_of((1 - core) * rows, rows), rows)

    ids = jnp.broadcast_to(all_ids_ref[...].astype(f32), (8, cols)).T
    row_ids[...] = ids
    own_ids, all_ids = row_ids[own_rows, 0:1], ids[:, 0:1]
    lanes = lax.broadcasted_iota(jnp.int32, (rows, PAIR), 1).astype(f32)
    row_codes[...] = jnp.where(own_ids == lanes, 1.0, 0.0).astype(low)
    lanes = lax.broadcasted_iota(jnp.int32, (cols, PAIR), 1).astype(f32)
    barred = (all_ids != 0) & (all_ids != lanes) & (lanes < LABELS)
    col_codes[...] = jnp.where(barred, masked_value, 0.0).astype(low)

    query_bias, value_bias = as_row(query_bias_ref), as_row(value_bias_ref)
    load_x.wait()
    normed = standardize(x_ref[...].astype(f32), as_row(gain_ref), as_row(shift_ref)).astype(low)

    def projected(i, loads):
        for copy in loads:
            copy.wait()
        return dot(normed, jnp.concatenate([own[6 + 2 * i], own[7 + 2 * i]], axis=1))

    def spread(target, at, value):
        for p in range(pairs):
            target[p, at, :] = value[:, p * PAIR : (p + 1) * PAIR]

    spread(keys, own_rows, projected(1, load_w[0]).astype(low))
    pl.semaphore_wait(barrier, len(others))
    swaps = [
        pltpu.make_async_remote_copy(
            src_ref=buf.at[pl.ds(first, count), own_rows],
            dst_ref=buf.at[pl.ds(first, count), own_rows],
            send_sem=swap_send.at[i],
            recv_sem=swap_recv.at[i],
            device_id=sibling,
            device_id_type=MESH,
        )
        for i, (buf, first, count) in enumerate(
            ((keys, 2, 2), (values, 2, 2), (keys, 4, 2), (values, 4, 2), (keys, 0, 2), (values, 0, 2))
        )
    ]
    swaps[0].start()
    spread(values, own_rows, (projected(2, load_w[1]) + value_bias).astype(low))
    for swap in swaps[1:]:
        swap.start()
    asked = (projected(0, load_w[2]) + query_bias).astype(low)
    spread(queries, slice(None), asked * jnp.bfloat16(HD ** (-0.5)))
    normed_t[...] = normed.T
    load_wo = load(wo_hbm, wo, 7)
    load_wu = load(wu_hbm, wu, 8)
    load_dy = load(dy_hbm, dy_ref, 9)
    load_wd = load(wd_hbm, wd, 10)
    inverse_ref[...] = jnp.zeros((rows, PAIR), f32)
    swaps[0].wait_recv()

    def score(p, head):
        q_codes = jnp.concatenate([only_head(queries[p], head), row_codes[...]], axis=1)
        k_codes = jnp.concatenate([keys[p], col_codes[...]], axis=1)
        scores[head][...] = dot_bt(q_codes, k_codes)

    def blend(p, slot, head):
        part = scores[head][...]
        expo = jnp.exp(part - jnp.max(part, axis=1, keepdims=True)).astype(low)
        probs[slot, head] = expo
        v = values[p]
        return dot(expo, jnp.where(lane_mask(cols, head), v, jnp.ones_like(v)))

    score(2, 0)
    swaps[1].wait_recv()

    def pair_step(i, carry):
        p, slot = lax.rem(i + 2, pairs), lax.rem(i, 2)

        @pl.when(i >= 2)
        def _():
            probs_save(i - 2).wait()

        for turn in (1, 2):

            @pl.when(i == 2 * turn - 1)
            def _(turn=turn):
                swaps[2 * turn].wait_recv()
                swaps[2 * turn + 1].wait_recv()

        score(p, 1)
        first = blend(p, slot, 0)
        score(lax.rem(i + 3, pairs), 0)
        second = blend(p, slot, 1)

        @pl.when(i < pairs - 2)
        def _():
            probs_save(i).start()

        share = 1.0 / pltpu.roll(both(second, first), HALF, 1)
        at = pl.ds(pl.multiple_of(p * PAIR, PAIR), PAIR)
        attended_ref[:, at] = (both(first, second) * share).astype(low)
        lanes = lax.broadcasted_iota(jnp.int32, (rows, PAIR), 1)
        inverse_ref[...] = jnp.where((lanes == p) | (lanes == HALF + p), share, inverse_ref[...])
        return carry

    lax.fori_loop(0, pairs, pair_step, 0)

    def merge():
        load_wo.wait()
        mixed[...] = (
            x_ref[...].astype(f32) + dot(attended_ref[...], wo[...]) + as_row(out_bias_ref)
        )
        hat, _ = normal_parts(mixed[...])
        mid_low = (hat * as_row(mid_gain_ref) + as_row(mid_shift_ref)).astype(low)
        mid[...] = mid_low
        mid_t[...] = mid_low.T

    def quarter(c):
        return slice(c * width, (c + 1) * width)

    def expand(c):
        lanes = quarter(c)
        hidden = dot(mid[...], wu[:, lanes]) + as_row(up_bias_ref)[:, lanes]
        cdf = 0.5 * (1.0 + lax.erf(hidden * (0.5**0.5)))
        active = (hidden * cdf).astype(low)
        slope = cdf + hidden * (jnp.exp(-0.5 * hidden * hidden) * ((2.0 * math.pi) ** -0.5))
        act[...] = active
        act_t[...] = active.T
        back = (dot_bt(dy_ref[...], wd[lanes, :]) * slope).astype(low)
        hid_grad[...] = back
        vec_sum[0, 0, 4 + c : 5 + c, :] = column_sum(back.astype(f32))

    def weigh(unit, left_t, right):
        product = dot(left_t, right).astype(low)
        first, second = product[:, :half], product[:, half:]
        give(unit, jnp.where(core == 0, second, first))
        keep(unit, jnp.where(core == 0, first, second))

    def down_weight(c):
        weigh(c, act_t[...], dy_ref[...])

    def up_weight(c):
        weigh(N_DOWN + c, mid_t[...], hid_grad[...])

    def contract(c):
        lanes = quarter(c)
        deeper = dot_bt(hid_grad[...], wu[:, lanes])
        further = dot(act[...], wd[lanes, :])
        if c == 0:
            input_grad_ref[...] = deeper
            total[...] = mixed[...] + as_row(down_bias_ref) + further
        else:
            input_grad_ref[...] += deeper
            total[...] += further

    def norm_back():
        outputs[...] = total[...].astype(low)
        save(outputs, outputs_hbm, 0)
        hat, inverse = normal_parts(mixed[...])
        grad = input_grad_ref[...]
        vec_sum[0, 0, 2:3, :] = column_sum(grad * hat)
        vec_sum[0, 0, 3:4, :] = column_sum(grad)
        whole = dy_ref[...].astype(f32) + normal_back(hat, inverse, as_row(mid_gain_ref), grad)
        input_grad_ref[...] = whole
        branch_low = whole.astype(low)
        hid_grad[...] = branch_low
        vec_sum[0, 0, 1:2, :] = column_sum(branch_low.astype(f32))
        vec_sum[0, 0, 0:1, :] = column_sum(dy_ref[...].astype(f32))
        act_t[...] = attended_ref[...].T

    def out_weight():
        weigh(U_OUT, act_t[...], hid_grad[...])

    def attended_back():
        grad = dot_bt(hid_grad[...], wo[...])
        for p in range(pairs):
            share = both(inverse_ref[:, p : p + 1], inverse_ref[:, HALF + p : HALF + p + 1])
            att_grad[p] = (grad[:, p * PAIR : (p + 1) * PAIR] * share).astype(low)

    load_qkv = []

    def fetch():
        for p in range(pairs):
            for i, src in enumerate((wq_hbm, wk_hbm, wv_hbm)):
                at = (3 * p + i) * PAIR
                load_qkv.append(
                    load(
                        src.at[:, p * PAIR : (p + 1) * PAIR],
                        wu.at[:, at : at + PAIR],
                        11 + 3 * p + i,
                    )
                )

    def pair_back(p, slot):
        q, k, v, grad = queries[p], keys[p], values[p], att_grad[p]
        if p >= 2:
            probs_copy(p, slot).wait()
        out = attended_ref[:, p * PAIR : (p + 1) * PAIR]
        product = grad.astype(f32) * out.astype(f32)
        q_t, grad_t = q.T, grad.T
        query_total = jnp.zeros((rows, PAIR), f32)
        key_parts, value_parts = [], []
        for head in range(2):
            share = probs[slot, head]
            delta = jnp.sum(only_head(product, head), axis=1, keepdims=True)
            score = dot_bt(only_head(grad, head), v)
            score = (share.astype(f32) * (score - delta)).astype(low)
            query_total = query_total + dot(score, only_head(k, head))
            at = slice(head * HALF, (head + 1) * HALF)
            key_parts.append(dot(q_t[at, :], score).astype(low))
            value_parts.append(dot(grad_t[at, :], share).astype(low))
        kv_part[p % kv_part.shape[0], 0] = jnp.concatenate(key_parts, axis=0).T
        kv_part[p % kv_part.shape[0], 1] = jnp.concatenate(value_parts, axis=0).T
        qkv_grad[:, 3 * p * PAIR : (3 * p + 1) * PAIR] = (query_total * HD ** (-0.5)).astype(low)

    def attention_back(p):
        if p >= kv_part.shape[0]:
            flying[("kv", p - kv_part.shape[0])].wait_send()
        pair_back(p, p % 2)
        if p + 2 < pairs:
            probs_copy(p + 2, p % 2).start()
        copy = pltpu.make_async_remote_copy(
            src_ref=kv_part.at[p % kv_part.shape[0], :, their_rows],
            dst_ref=kv_recv.at[p],
            send_sem=kv_send.at[p],
            recv_sem=kv_recv_sem.at[p],
            device_id=sibling,
            device_id_type=MESH,
        )
        copy.start()
        flying[("kv", p)] = copy

    def qkv_weight(r):
        for i in range(2):
            p = 2 * r + i
            flying[("kv", p)].wait_recv()
            for j in range(2):
                qkv_grad[:, (3 * p + 1 + j) * PAIR : (3 * p + 2 + j) * PAIR] = (
                    kv_part[p % kv_part.shape[0], j, own_rows, :] + kv_recv[p, j]
                )
        weigh(U_QKV + r, normed_t[...], qkv_grad[:, 6 * r * PAIR : 6 * (r + 1) * PAIR])

    def input_back():
        for copy in load_qkv:
            copy.wait()
        size = 3 * pairs * PAIR
        grad = dot_bt(qkv_grad[...], wu[:, :size])
        hat, inverse = normal_parts(x_ref[...].astype(f32))
        input_grad_ref[...] += normal_back(hat, inverse, as_row(gain_ref), grad)
        save(input_grad_ref, input_grad_hbm, 1)
        vec_sum[1, 0] = jnp.zeros((8, width), f32)
        vec_sum[1, 0, 0:1, :] = column_sum(grad * hat)
        vec_sum[1, 0, 1:2, :] = column_sum(grad)
        for p in range(pairs):
            lanes = slice(p * PAIR, (p + 1) * PAIR)
            for row, j in ((2, 0), (3, 2)):
                part = qkv_grad[:, (3 * p + j) * PAIR : (3 * p + j + 1) * PAIR]
                vec_sum[1, 0, row : row + 1, lanes] = column_sum(part.astype(f32))

    def first_wait():
        for copy in (load_wu, load_dy, load_wd):
            copy.wait()

    merge()
    first_wait()
    expand(0)
    down_weight(0)
    up_weight(0)
    contract(0)
    expand(1)
    step(4, 1)
    step(0, 1)
    down_weight(1)
    up_weight(1)
    contract(1)
    expand(2)
    step(7, 1)
    step(6, 1)
    step(1, 1)
    down_weight(2)
    up_weight(2)
    step(5, 1)
    contract(2)
    step(2, 1)
    expand(3)
    step(8, 1)
    down_weight(3)
    step(0, 2)
    step(9, 1)
    up_weight(3)
    contract(3)
    step(1, 2)
    norm_back()
    step(3, 1)
    vec_step(0, 0)
    step(11, 1)
    out_weight()
    attended_back()
    step(4, 2)
    fetch()
    step(2, 2)
    attention_back(0)
    step(13, 1)
    step(12, 1)
    down_pair(0)
    attention_back(1)
    attention_back(2)
    step(3, 2)
    step(6, 2)
    step(7, 2)
    step(5, 2)
    step(11, 2)
    attention_back(3)
    step(8, 2)
    qkv_weight(0)
    step(10, 1)
    step(6, 3)
    step(4, 3)
    attention_back(4)
    down_pair(1)
    step(13, 2)
    step(15, 1)
    step(14, 1)
    attention_back(5)
    vec_step(0, 1)
    step(8, 3)
    step(12, 2)
    qkv_weight(1)
    step(4, 4)
    step(7, 3)
    step(16, 1)
    step(10, 2)
    step(5, 3)
    qkv_weight(2)
    step(13, 3)
    step(18, 1)
    step(17, 1)
    step(15, 2)
    input_back()
    step(19, 1)
    vec_step(0, 2)
    step(10, 3)
    step(20, 1)
    vec_step(1, 0)
    down_cross()
    step(15, 3)
    step(14, 2)
    step(16, 2)
    vec_step(1, 1)
    step(12, 3)
    step(17, 2)
    step(13, 4)
    step(9, 2)
    step(20, 2)
    step(19, 2)
    step(10, 4)
    vec_step(0, 3)
    step(18, 2)
    step(5, 4)
    step(15, 4)
    step(11, 3)
    step(14, 3)
    vec_step(1, 2)
    step(12, 4)
    step(9, 3)
    step(16, 3)
    step(17, 3)
    step(7, 4)
    step(6, 4)
    step(20, 3)
    down_finish()
    vec_step(0, 4)
    finish(4)
    step(19, 3)
    step(18, 3)
    vec_step(1, 3)
    step(17, 4)
    finish(12)
    step(20, 4)
    step(11, 4)
    finish(15)
    finish(6)
    step(9, 4)
    step(16, 4)
    step(8, 4)
    step(14, 4)
    finish(10)
    finish(5)
    step(19, 4)
    step(18, 4)
    vec_step(1, 4)
    finish(7)
    finish(20)
    finish(14)
    finish(17)
    finish(9)
    finish(16)
    finish(19)
    finish(11)
    finish(8)
    finish(13)
    finish(18)
    vec_step(1, 5)
    vec_step(0, 5)

    size = width // GROUPS
    if minor == 1:
        size = size // 2
        keep_rows = pl.ds(pl.multiple_of(core * size, size), size)
        down_rows = pl.ds(pl.multiple_of(core * 4 * size, 4 * size), 4 * size)
        flying[(0, 5)].wait_recv()
        down_out_ref[:, pl.ds(mine, half)] = down_last[down_rows, :]
        down_out_ref[:, pl.ds(theirs, half)] = down_last_recv[...]
        for part in range(N_DOWN, len(PARTS)):
            flying[(part, 5)].wait_recv()
        for unit in range(N_DOWN, UNITS):
            spot = unit - N_DOWN
            if unit < U_OUT:
                target, lanes = up_out_ref, (unit - N_DOWN) * width
            else:
                target, lanes = out_out_ref, 0
            if unit < U_QKV:
                target[:, pl.ds(pl.multiple_of(lanes + mine, half), half)] = last[spot, keep_rows, :]
                target[:, pl.ds(pl.multiple_of(lanes + theirs, half), half)] = last_recv[spot]
            else:
                for which, value in (
                    (core, last[spot, keep_rows, :]),
                    (1 - core, last_recv[spot]),
                ):
                    at = pl.ds(pl.multiple_of((2 * (unit - U_QKV) + which) * PAIR, PAIR), PAIR)
                    for j in range(3):
                        qkv_out_ref[j, :, at] = value[:, j * PAIR : (j + 1) * PAIR]
    else:
        down_out_ref[...] = down_last[...]
        for unit in range(N_DOWN, U_OUT):
            up_out_ref[:, (unit - N_DOWN) * half : (unit - N_DOWN + 1) * half] = last[unit - N_DOWN]
        out_out_ref[...] = last[U_OUT - N_DOWN]
        for r in range(3):
            for j in range(3):
                qkv_out_ref[j, :, r * PAIR : (r + 1) * PAIR] = last[
                    U_QKV - N_DOWN + r, :, j * PAIR : (j + 1) * PAIR
                ]

    for copy in saves:
        copy.wait()
    for swap in swaps:
        swap.wait_send()
    for p in range(pairs - kv_part.shape[0], pairs):
        flying[("kv", p)].wait_send()
    for key, copy in flying.items():
        if key[0] == "v" or isinstance(key[0], int) or key in [("give", u) for u in given[-2:]]:
            copy.wait_send()


def run_layer(x, dy, ids, vectors, weights, minor):
    rows, width = x.shape
    pairs = width // PAIR
    cols = ids.shape[1]
    hidden = weights[1].shape[1]
    half = width // 2
    chunk = width // GROUPS
    low, f32 = jnp.bfloat16, jnp.float32
    vmem, hbm = pl.BlockSpec(memory_space=pltpu.VMEM), pl.BlockSpec(memory_space=pl.ANY)
    if minor == 1:
        outs = [(3, chunk // 2, width), (chunk // 2, width), (chunk // 2, hidden), (2 * chunk, width)]
    else:
        outs = [(3, chunk, half), (chunk, half), (chunk, hidden // 2), (4 * chunk, half)]
    late = UNITS - N_DOWN
    return pl.pallas_call(
        partial(layer_kernel, rows, width, pairs, minor),
        out_shape=[
            jax.ShapeDtypeStruct((rows, width), low),
            jax.ShapeDtypeStruct((rows, width), f32),
        ]
        + [jax.ShapeDtypeStruct(shape, f32) for shape in outs]
        + [jax.ShapeDtypeStruct((8, width), f32)] * 2
        + [jax.ShapeDtypeStruct((pairs - 2, 2, rows, cols), low)],
        in_specs=[hbm] * 2 + [vmem] * 10 + [hbm] * 6,
        out_specs=[hbm] * 2 + [vmem] * 6 + [hbm],
        scratch_shapes=[
            pltpu.VMEM((rows, width), f32),
            pltpu.VMEM((2, rows, cols), f32),
            pltpu.VMEM((rows, PAIR), f32),
            pltpu.VMEM((rows, PAIR), low),
            pltpu.VMEM((cols, PAIR), low),
            pltpu.VMEM((cols, 8), f32),
            pltpu.VMEM((rows, width), low),
            pltpu.VMEM((rows, width), low),
            pltpu.VMEM((rows, width), low),
            pltpu.VMEM((width, width), low),
            pltpu.VMEM((width, hidden), low),
            pltpu.VMEM((hidden, width), low),
            pltpu.VMEM((width, rows), low),
            pltpu.VMEM((pairs, rows, PAIR), low),
            pltpu.VMEM((pairs, cols, PAIR), low),
            pltpu.VMEM((pairs, cols, PAIR), low),
            pltpu.VMEM((2, 2, rows, cols), low),
            pltpu.VMEM((rows, width), low),
            pltpu.VMEM((width, rows), low),
            pltpu.VMEM((rows, width), low),
            pltpu.VMEM((rows, width), low),
            pltpu.VMEM((width, rows), low),
            pltpu.VMEM((rows, width), low),
            pltpu.VMEM((pairs, rows, PAIR), low),
            pltpu.VMEM((rows, 3 * width), low),
            pltpu.VMEM((4, 2, cols, PAIR), low),
            pltpu.VMEM((pairs, 2, rows, PAIR), low),
            pltpu.VMEM((UNITS, width, half), low),
            pltpu.VMEM((2, width, half), low),
            pltpu.VMEM((max(LANDING) + 1, width, half), low),
            pltpu.VMEM((UNITS, width // 2, half), low),
            pltpu.VMEM((UNITS, width // 4, half), low),
            pltpu.VMEM((late, width // 8, half), low),
            pltpu.VMEM((late, width // 16, half), low),
            pltpu.VMEM((2, width // 4, half), low),
            pltpu.VMEM((width // 4, half), low),
            pltpu.VMEM((late, chunk, half), f32),
            pltpu.VMEM((late, chunk // 2, half), f32),
            pltpu.VMEM((4 * chunk, half), f32),
            pltpu.VMEM((2 * chunk, half), f32),
            pltpu.VMEM((2, 5, 8, width), f32),
            pltpu.VMEM((2, 5, 8, width), f32),
            pltpu.SemaphoreType.DMA((6,)),
            pltpu.SemaphoreType.DMA((6,)),
            pltpu.SemaphoreType.DMA((11 + 3 * pairs,)),
            pltpu.SemaphoreType.DMA((2,)),
            pltpu.SemaphoreType.DMA((2,)),
            pltpu.SemaphoreType.DMA((PART_SEMS, 6)),
            pltpu.SemaphoreType.DMA((PART_SEMS, 6)),
            pltpu.SemaphoreType.DMA((UNITS,)),
            pltpu.SemaphoreType.DMA((UNITS,)),
            pltpu.SemaphoreType.DMA((pairs,)),
            pltpu.SemaphoreType.DMA((pairs,)),
            pltpu.SemaphoreType.DMA((2, 5)),
            pltpu.SemaphoreType.DMA((2, 5)),
        ],
        compiler_params=pltpu.CompilerParams(
            collective_id=1, has_side_effects=True, vmem_limit_bytes=61 << 20
        ),
    )(x, dy, ids, *vectors, *weights)


def finish_kernel(
    outputs_ref, input_grad_ref, qkv_ref, out_ref, up_ref, down_ref, vec_a_ref, vec_b_ref, *rest
):
    outputs_out, input_grad_out, query, key, value, out, up, down = rest[:8]
    vectors = rest[8:]
    outputs_out[...] = outputs_ref[...]
    input_grad_out[...] = input_grad_ref[...]

    def flatten(values, target):
        rows, lanes = values.shape
        parts = lanes // 128
        for j in range(parts):
            target[pl.ds(j, rows, stride=parts), :] = values[:, j * 128 : (j + 1) * 128]

    @pl.when(pl.program_id(0) == 0)
    def _():
        for j, target in enumerate((query, key, value)):
            flatten(qkv_ref[j], target)
        flatten(out_ref[...], out)
        flatten(up_ref[...], up)
        flatten(down_ref[...], down)
        lines = [vec_b_ref[j, :] for j in range(4)] + [vec_a_ref[j, :] for j in (1, 2, 3)]
        for line, target in zip(lines, vectors[:7]):
            target[...] = line
        width = vec_a_ref.shape[1]
        for j in range(4):
            vectors[7][j * width : (j + 1) * width] = vec_a_ref[4 + j, :]
        vectors[8][...] = vec_a_ref[0, :]


def run_finish(outputs, input_grad, qkv, out, up, down, vec_a, vec_b):
    f32 = jnp.float32
    width = vec_a.shape[1]
    steps = 2
    whole = lambda shape: pl.BlockSpec(shape, lambda i: (0,) * len(shape))
    piece = pl.BlockSpec((outputs.shape[0] // steps, width), lambda i: (i, 0))
    flat = lambda size: jax.ShapeDtypeStruct((size // 128, 128), f32)
    line = lambda size: jax.ShapeDtypeStruct((size,), f32)
    shapes = [
            jax.ShapeDtypeStruct(outputs.shape, outputs.dtype),
            jax.ShapeDtypeStruct(input_grad.shape, f32),
            *(flat(qkv[0].size) for _ in range(3)),
            *(flat(part.size) for part in (out, up, down)),
            *(line(width) for _ in range(7)),
            line(4 * width),
            line(width),
        ]
    return pl.pallas_call(
        finish_kernel,
        grid=(steps,),
        out_shape=shapes,
        in_specs=[piece] * 2 + [whole(part.shape) for part in (qkv, out, up, down, vec_a, vec_b)],
        out_specs=[piece] * 2 + [whole(shape.shape) for shape in shapes[2:]],
    )(outputs, input_grad, qkv, out, up, down, vec_a, vec_b)


def local(
    incoming_vectors,
    caption_labels,
    loss_sensitivity,
    asking_projection,
    lookup_projection,
    content_projection,
    attention_result_projection,
    expansion_projection,
    contraction_projection,
    attention_norm_scale,
    attention_norm_offset,
    asking_offset,
    content_offset,
    attention_result_offset,
    feedforward_norm_scale,
    feedforward_norm_offset,
    expansion_offset,
    contraction_offset,
):
    seqs, rows, width = incoming_vectors.shape
    chips = lax.axis_size("seq")
    minor = chips // GROUPS
    core = lax.axis_index("blk")
    x = incoming_vectors.reshape(rows, width)
    dy = loss_sensitivity.reshape(rows, width)
    vectors = (
        attention_norm_scale,
        attention_norm_offset,
        asking_offset,
        content_offset,
        feedforward_norm_scale,
        feedforward_norm_offset,
        attention_result_offset,
        expansion_offset,
        contraction_offset,
    )
    weights = (
        attention_result_projection,
        expansion_projection,
        contraction_projection,
        asking_projection,
        lookup_projection,
        content_projection,
    )
    outputs, input_grad, qkv_sum, out_sum, up_sum, down_sum, vec_a, vec_b, _ = run_layer(
        x, dy, caption_labels, vectors, weights, minor
    )
    if minor > 1:
        teams = [[g * minor + i for i in range(minor)] for g in range(GROUPS)]
        own_half = lambda values: lax.dynamic_slice_in_dim(
            values, core * (values.shape[0] // 2), values.shape[0] // 2, 0
        )

        def rest(part, pieces):
            both = lax.all_gather(part.reshape(part.shape[0], pieces, -1), "blk", axis=2)
            whole = both.reshape(part.shape[0], -1)
            return own_half(
                lax.psum_scatter(whole, "seq", axis_index_groups=teams, tiled=True)
            )

        qkv_sum = [rest(qkv_sum[i], 3) for i in range(3)]
        out_sum, up_sum, down_sum = rest(out_sum, 1), rest(up_sum, 4), rest(down_sum, 1)
        vec_a, vec_b = lax.psum((vec_a, vec_b), "seq", axis_index_groups=teams)
        qkv_sum = jnp.stack(qkv_sum)
    flat = run_finish(outputs, input_grad, qkv_sum, out_sum, up_sum, down_sum, vec_a, vec_b)
    return (
        flat[0].reshape(seqs, rows, width),
        flat[1].reshape(seqs, rows, width),
        *(part.reshape(-1) for part in flat[2:]),
    )


def solution(mesh):
    in_specs = (
        P("seq", "blk", None),
        P("seq", None),
        P("seq", "blk", None),
        P(),
        P(),
        P(),
        P(),
        P(),
        P(),
        P(),
        P(),
        P(),
        P(),
        P(),
        P(),
        P(),
        P(),
        P(),
    )
    out_specs = (
        P("seq", "blk", None),
        P("seq", "blk", None),
        P(("seq", "blk")),
        P(("seq", "blk")),
        P(("seq", "blk")),
        P(("seq", "blk")),
        P(("seq", "blk")),
        P(("seq", "blk")),
        P(),
        P(),
        P(),
        P(),
        P(),
        P(),
        P(),
        P(),
        P(),
    )
    return jax.shard_map(local, mesh=mesh, in_specs=in_specs, out_specs=out_specs, check_vma=False)
```

```python
import math
from functools import partial

import jax
import jax.numpy as jnp
from jax import lax
from jax.experimental import pallas as pl
from jax.experimental.pallas import tpu as pltpu
from jax.sharding import PartitionSpec as P

HD = 64
MESH = pl.DeviceIdType.MESH


epsilon = 1e-05
masked_value = -1e30

HALF = 64
PAIR = 2 * HALF
LABELS = 9


def lane_mask(rows, head):
    lanes = lax.broadcasted_iota(jnp.int32, (rows, PAIR), 1)
    return (lanes < HALF) if head == 0 else (lanes >= HALF)


def only_head(values, head):
    return jnp.where(lane_mask(values.shape[0], head), values, jnp.zeros_like(values))


def as_row(ref):
    return ref[...].reshape(1, ref.shape[0])


def dot(left, right):
    return jnp.dot(left, right, preferred_element_type=jnp.float32)


def dot_bt(left, right):
    return lax.dot_general(left, right, (((1,), (1,)), ((), ())), preferred_element_type=jnp.float32)


def both(first, second):
    return jnp.where(lane_mask(first.shape[0], 0), first, second)


def standardize(values, gain, shift):
    center = values - jnp.mean(values, axis=-1, keepdims=True)
    spread = jnp.mean(center * center, axis=-1, keepdims=True)
    return center * lax.rsqrt(spread + epsilon) * gain + shift


X_BIT, Y_BIT, Z_BIT, ZZ_BIT = 1, 2, 4, 8
GROUPS = 16
CORE_ORDER = (X_BIT, Y_BIT, Z_BIT, ZZ_BIT)
N_DOWN, N_UP = 4, 4
U_OUT = N_DOWN + N_UP
U_QKV = U_OUT + 1
UNITS = U_QKV + 3
PARTS = (
    (0, 0, 384, (Y_BIT, X_BIT)),
    (1, 0, 384, (X_BIT, Y_BIT)),
    (2, 0, 384, (Y_BIT, X_BIT)),
    (3, 0, 384, (X_BIT, Y_BIT)),
    (4, 0, 384, (Z_BIT, Y_BIT, X_BIT, ZZ_BIT)),
    (5, 0, 128, (Z_BIT, Y_BIT, ZZ_BIT, X_BIT)),
    (5, 128, 128, (Z_BIT, X_BIT, ZZ_BIT, Y_BIT)),
    (5, 256, 128, (Y_BIT, Z_BIT, X_BIT, ZZ_BIT)),
    (6, 0, 256, (Z_BIT, X_BIT, ZZ_BIT, Y_BIT)),
    (6, 256, 128, (Z_BIT, X_BIT, Y_BIT, ZZ_BIT)),
    (7, 0, 128, (Y_BIT, X_BIT, Z_BIT, ZZ_BIT)),
    (7, 128, 256, (Z_BIT, ZZ_BIT, X_BIT, Y_BIT)),
    (8, 0, 128, (Z_BIT, X_BIT, Y_BIT, ZZ_BIT)),
    (8, 128, 128, (Y_BIT, X_BIT, Z_BIT, ZZ_BIT)),
    (8, 256, 128, (X_BIT, Y_BIT, Z_BIT, ZZ_BIT)),
    (9, 0, 256, (Y_BIT, Z_BIT, X_BIT, ZZ_BIT)),
    (9, 256, 128, (Y_BIT, Z_BIT, X_BIT, ZZ_BIT)),
    (10, 0, 128, (Y_BIT, Z_BIT, X_BIT, ZZ_BIT)),
    (10, 128, 256, (X_BIT, Y_BIT, Z_BIT, ZZ_BIT)),
    (11, 0, 256, (Y_BIT, X_BIT, Z_BIT, ZZ_BIT)),
    (11, 256, 128, (X_BIT, Y_BIT, Z_BIT, ZZ_BIT)),
)
PART_SEMS = len(PARTS)
LANDING = (0, 1, 2, 3, 4, 5, 6, 7, 0, 1, 2, 4)


def place_of(group, order):
    place = 0
    for bit in order:
        place = 2 * place + (1 if group & bit else 0)
    return place


def normal_parts(values):
    center = values - jnp.mean(values, axis=-1, keepdims=True)
    spread = jnp.mean(center * center, axis=-1, keepdims=True)
    inverse = lax.rsqrt(spread + epsilon)
    return center * inverse, inverse


def normal_back(hat, inverse, gain, grad):
    scaled = grad * gain
    first = jnp.mean(scaled, axis=-1, keepdims=True)
    second = jnp.mean(scaled * hat, axis=-1, keepdims=True)
    return inverse * (scaled - first - hat * second)


def column_sum(values):
    return jnp.sum(values, axis=0, keepdims=True)


def layer_kernel(
    rows,
    width,
    pairs,
    minor,
    x_hbm,
    dy_hbm,
    all_ids_ref,
    gain_ref,
    shift_ref,
    query_bias_ref,
    value_bias_ref,
    mid_gain_ref,
    mid_shift_ref,
    out_bias_ref,
    up_bias_ref,
    down_bias_ref,
    wo_hbm,
    wu_hbm,
    wd_hbm,
    wq_hbm,
    wk_hbm,
    wv_hbm,
    outputs_hbm,
    input_grad_hbm,
    qkv_out_ref,
    out_out_ref,
    up_out_ref,
    down_out_ref,
    vec_a_ref,
    vec_b_ref,
    probs_hbm,
    input_grad_ref,
    big,
    inverse_ref,
    row_codes,
    col_codes,
    row_ids,
    x_ref,
    dy_ref,
    attended_ref,
    wo,
    wu,
    wd,
    normed_t,
    queries,
    keys,
    values,
    probs,
    mid,
    mid_t,
    act,
    outputs,
    act_t,
    hid_grad,
    att_grad,
    qkv_grad,
    kv_part,
    kv_recv,
    own,
    stage,
    recv0,
    recv1,
    recv2,
    recv3,
    recv4,
    down3,
    down4,
    last,
    last_recv,
    down_last,
    down_last_recv,
    vec_sum,
    vec_recv,
    swap_send,
    swap_recv,
    load_sems,
    save_sems,
    probs_sems,
    unit_send,
    unit_recv,
    give_send,
    give_recv,
    kv_send,
    kv_recv_sem,
    vec_send,
    vec_recv_sem,
):
    low = jnp.bfloat16
    f32 = jnp.float32
    half = width // 2
    cols = all_ids_ref.shape[1]
    scores = (big.at[0], big.at[1])
    mixed, total = big.at[0, :, pl.ds(0, width)], big.at[1, :, pl.ds(0, width)]
    chip, core = lax.axis_index("seq"), lax.axis_index("blk")
    group = lax.div(chip, minor)

    def my_bit(bit):
        return lax.rem(lax.div(group, bit), 2)

    def partner(bit):
        return (chip + (1 - 2 * my_bit(bit)) * (bit * minor), core)

    sibling = (chip, 1 - core)
    mine = pl.multiple_of(core * half, half)
    theirs = pl.multiple_of((1 - core) * half, half)

    def load(src, dst, i):
        copy = pltpu.make_async_copy(src, dst, load_sems.at[i])
        copy.start()
        return copy

    saves = []

    def save(src, dst, i):
        copy = pltpu.make_async_copy(src, dst, save_sems.at[i])
        copy.start()
        saves.append(copy)

    load_x = load(x_hbm, x_ref, 0)
    load_w = [
        [
            load(src.at[:, pl.ds(h * half, half)], own.at[6 + 2 * i + h], 1 + 2 * i + h)
            for h in range(2)
        ]
        for i, src in ((1, wk_hbm), (2, wv_hbm), (0, wq_hbm))
    ]

    def probs_copy(p, slot):
        return pltpu.make_async_copy(probs_hbm.at[p - 2], probs.at[slot], probs_sems.at[slot])

    def probs_save(i):
        slot = lax.rem(i, 2)
        return pltpu.make_async_copy(probs.at[slot], probs_hbm.at[i], probs_sems.at[slot])

    barrier = pltpu.get_barrier_semaphore()
    others = [sibling] + [partner(bit) for bit in CORE_ORDER]
    for device in others:
        pl.semaphore_signal(barrier, inc=1, device_id=device, device_id_type=MESH)

    def send(src, dst, sems_at, device, start=True):
        copy = pltpu.make_async_remote_copy(
            src_ref=src,
            dst_ref=dst,
            send_sem=unit_send.at[sems_at],
            recv_sem=unit_recv.at[sems_at],
            device_id=device,
            device_id_type=MESH,
        )
        if start:
            copy.start()
        return copy

    given = []
    flying = {}
    base = {}
    landed = set()
    recvs = (recv0, recv1, recv2, recv3, recv4)

    def lanes_of(part):
        unit, start, count, order = PARTS[part]
        return unit, slice(start, start + count), order

    def parts_of(unit):
        return [part for part in range(len(PARTS)) if PARTS[part][0] == unit]

    def put(unit, target, value):
        for part in parts_of(unit):
            _, lanes, order = lanes_of(part)
            if unit < N_DOWN:
                step = width // 4
                for yx in range(4):
                    at = place_of(yx, order) * step
                    target[at : at + step, lanes] = value[yx * step : (yx + 1) * step, lanes]
            else:
                step = width // GROUPS
                for g in range(GROUPS):
                    at = place_of(g, order) * step
                    target[at : at + step, lanes] = value[g * step : (g + 1) * step, lanes]

    def give(unit, value):
        slot = len(given) % stage.shape[0]
        if len(given) >= stage.shape[0]:
            flying[("give", given[-stage.shape[0]])].wait_send()
        given.append(unit)
        put(unit, stage.at[slot], value)
        copy = pltpu.make_async_remote_copy(
            src_ref=stage.at[slot],
            dst_ref=recv0.at[LANDING[unit]],
            send_sem=give_send.at[unit],
            recv_sem=give_recv.at[unit],
            device_id=sibling,
            device_id_type=MESH,
        )
        copy.start()
        flying[("give", unit)] = copy

    def keep(unit, value):
        put(unit, own.at[unit], value)
        for part in parts_of(unit):
            base[part] = 0

    def arrived(part, k):
        unit, lanes, _ = lanes_of(part)
        if k > 0:
            flying[(part, k)].wait_recv()
        elif unit not in landed:
            landed.add(unit)
            flying[("give", unit)].wait_recv()
        if k == 0:
            return recv0.at[LANDING[unit], :, lanes]
        return recvs[k].at[unit if k < 3 else unit - N_DOWN, :, lanes]

    def step(part, k):
        unit, lanes, order = lanes_of(part)
        size = (width >> (k - 1)) // 2
        bit = order[k - 1]
        side = my_bit(bit)
        at = base[part]
        got = arrived(part, k - 1)
        away = pl.ds(pl.multiple_of((1 - side) * size, size), size)
        away_own = pl.ds(pl.multiple_of(at + (1 - side) * size, size), size)
        stay = pl.ds(pl.multiple_of(side * size, size), size)
        stay_own = pl.ds(pl.multiple_of(at + side * size, size), size)
        own[unit, away_own, lanes] += got[away, :]
        flying[(part, k)] = send(
            own.at[unit, away_own, lanes],
            recvs[k].at[unit if k < 3 else unit - N_DOWN, :, lanes],
            (part, k),
            partner(bit),
        )
        own[unit, stay_own, lanes] += got[stay, :]
        base[part] = at + side * size

    def finish(part):
        unit, lanes, _ = lanes_of(part)
        size = width >> 4
        got = arrived(part, 4)
        at = pl.ds(pl.multiple_of(base[part], size), size)
        spot = unit - N_DOWN
        last[spot, :, lanes] = own[unit, at, lanes].astype(f32) + got[...].astype(f32)
        if minor == 1:
            size = size // 2
            rows_away = pl.ds(pl.multiple_of((1 - core) * size, size), size)
            flying[(part, 5)] = send(
                last.at[spot, rows_away, lanes], last_recv.at[spot, :, lanes], (part, 5), sibling
            )

    def down_pair(pair):
        size = width // 4
        side = my_bit(Z_BIT)
        for c in (0, 1):
            unit = 2 * pair + c
            flying[(unit, 2)].wait_recv()
            at = pl.ds(pl.multiple_of(base[unit], size), size)
            own[unit, at, :] += recv2[unit]
        away = 2 * pair + 1 - side
        at0, at1 = base[2 * pair], base[2 * pair + 1]
        at = jnp.where(side == 1, at0, at1)
        flying[(2 * pair, 3)] = send(
            own.at[away, pl.ds(pl.multiple_of(at, size), size)],
            down3.at[pair],
            (2 * pair, 3),
            partner(Z_BIT),
        )

    def down_rows(pair):
        at = jnp.where(my_bit(Z_BIT) == 0, base[2 * pair], base[2 * pair + 1])
        return pl.ds(pl.multiple_of(at, width // 4), width // 4)

    def down_cross():
        side, high = my_bit(Z_BIT), my_bit(ZZ_BIT)
        for pair in (0, 1):
            flying[(2 * pair, 3)].wait_recv()
            own[2 * pair + side, down_rows(pair), :] += down3[pair]
        at = pl.multiple_of(jnp.where(high == 1, down_rows(0).start, down_rows(1).start), width // 4)
        flying[(0, 4)] = send(
            own.at[2 * (1 - high) + side, pl.ds(at, width // 4)], down4, (0, 4), partner(ZZ_BIT)
        )

    def down_finish():
        size = width // 4
        side, high = my_bit(Z_BIT), my_bit(ZZ_BIT)
        at = pl.multiple_of(jnp.where(high == 0, down_rows(0).start, down_rows(1).start), size)
        flying[(0, 4)].wait_recv()
        down_last[...] = own[2 * high + side, pl.ds(at, size), :].astype(f32) + down4[...].astype(f32)
        if minor == 1:
            flying[(0, 5)] = send(
                down_last.at[pl.ds(pl.multiple_of((1 - core) * (size // 2), size // 2), size // 2)],
                down_last_recv,
                (0, 5),
                sibling,
            )

    def vec_step(k):
        if k > 0:
            flying[("v", k - 1)].wait_recv()
            added = vec_sum[k - 1] + vec_recv[k - 1]
            if k == 5:
                vec_a_ref[...] = added[:8]
                vec_b_ref[...] = added[8:]
                return
            vec_sum[k] = added
        device = sibling if k == 0 else partner(CORE_ORDER[k - 1])
        copy = pltpu.make_async_remote_copy(
            src_ref=vec_sum.at[k],
            dst_ref=vec_recv.at[k],
            send_sem=vec_send.at[k],
            recv_sem=vec_recv_sem.at[k],
            device_id=device,
            device_id_type=MESH,
        )
        copy.start()
        flying[("v", k)] = copy

    own_rows = pl.ds(pl.multiple_of(core * rows, rows), rows)
    their_rows = pl.ds(pl.multiple_of((1 - core) * rows, rows), rows)

    ids = jnp.broadcast_to(all_ids_ref[...].astype(f32), (8, cols)).T
    row_ids[...] = ids
    own_ids, all_ids = row_ids[own_rows, 0:1], ids[:, 0:1]
    lanes = lax.broadcasted_iota(jnp.int32, (rows, PAIR), 1).astype(f32)
    row_codes[...] = jnp.where(own_ids == lanes, 1.0, 0.0).astype(low)
    lanes = lax.broadcasted_iota(jnp.int32, (cols, PAIR), 1).astype(f32)
    barred = (all_ids != 0) & (all_ids != lanes) & (lanes < LABELS)
    col_codes[...] = jnp.where(barred, masked_value, 0.0).astype(low)

    query_bias, value_bias = as_row(query_bias_ref), as_row(value_bias_ref)
    load_x.wait()
    normed = standardize(x_ref[...].astype(f32), as_row(gain_ref), as_row(shift_ref)).astype(low)

    def projected(i, loads):
        for copy in loads:
            copy.wait()
        return dot(normed, jnp.concatenate([own[6 + 2 * i], own[7 + 2 * i]], axis=1))

    def spread(target, at, value):
        for p in range(pairs):
            target[p, at, :] = value[:, p * PAIR : (p + 1) * PAIR]

    spread(keys, own_rows, projected(1, load_w[0]).astype(low))
    pl.semaphore_wait(barrier, len(others))
    swaps = [
        pltpu.make_async_remote_copy(
            src_ref=buf.at[pl.ds(first, count), own_rows],
            dst_ref=buf.at[pl.ds(first, count), own_rows],
            send_sem=swap_send.at[i],
            recv_sem=swap_recv.at[i],
            device_id=sibling,
            device_id_type=MESH,
        )
        for i, (buf, first, count) in enumerate(
            ((keys, 2, 2), (values, 2, 2), (keys, 4, 2), (values, 4, 2), (keys, 0, 2), (values, 0, 2))
        )
    ]
    swaps[0].start()
    spread(values, own_rows, (projected(2, load_w[1]) + value_bias).astype(low))
    for swap in swaps[1:]:
        swap.start()
    asked = (projected(0, load_w[2]) + query_bias).astype(low)
    spread(queries, slice(None), asked * jnp.bfloat16(HD ** (-0.5)))
    normed_t[...] = normed.T
    load_wo = load(wo_hbm, wo, 7)
    load_wu = load(wu_hbm, wu, 8)
    load_dy = load(dy_hbm, dy_ref, 9)
    load_wd = load(wd_hbm, wd, 10)
    inverse_ref[...] = jnp.zeros((rows, PAIR), f32)
    swaps[0].wait_recv()

    def score(p, head):
        q_codes = jnp.concatenate([only_head(queries[p], head), row_codes[...]], axis=1)
        k_codes = jnp.concatenate([keys[p], col_codes[...]], axis=1)
        scores[head][...] = dot_bt(q_codes, k_codes)

    def blend(p, slot, head):
        part = scores[head][...]
        expo = jnp.exp(part - jnp.max(part, axis=1, keepdims=True)).astype(low)
        probs[slot, head] = expo
        v = values[p]
        return dot(expo, jnp.where(lane_mask(cols, head), v, jnp.ones_like(v)))

    score(2, 0)
    swaps[1].wait_recv()

    def pair_step(i, carry):
        p, slot = lax.rem(i + 2, pairs), lax.rem(i, 2)

        @pl.when(i >= 2)
        def _():
            probs_save(i - 2).wait()

        for turn in (1, 2):

            @pl.when(i == 2 * turn - 1)
            def _(turn=turn):
                swaps[2 * turn].wait_recv()
                swaps[2 * turn + 1].wait_recv()

        score(p, 1)
        first = blend(p, slot, 0)
        score(lax.rem(i + 3, pairs), 0)
        second = blend(p, slot, 1)

        @pl.when(i < pairs - 2)
        def _():
            probs_save(i).start()

        share = 1.0 / pltpu.roll(both(second, first), HALF, 1)
        at = pl.ds(pl.multiple_of(p * PAIR, PAIR), PAIR)
        attended_ref[:, at] = (both(first, second) * share).astype(low)
        lanes = lax.broadcasted_iota(jnp.int32, (rows, PAIR), 1)
        inverse_ref[...] = jnp.where((lanes == p) | (lanes == HALF + p), share, inverse_ref[...])
        return carry

    lax.fori_loop(0, pairs, pair_step, 0)

    def merge():
        load_wo.wait()
        mixed[...] = (
            x_ref[...].astype(f32) + dot(attended_ref[...], wo[...]) + as_row(out_bias_ref)
        )
        hat, _ = normal_parts(mixed[...])
        mid_low = (hat * as_row(mid_gain_ref) + as_row(mid_shift_ref)).astype(low)
        mid[...] = mid_low
        mid_t[...] = mid_low.T

    def quarter(c):
        return slice(c * width, (c + 1) * width)

    def expand(c):
        lanes = quarter(c)
        hidden = dot(mid[...], wu[:, lanes]) + as_row(up_bias_ref)[:, lanes]
        cdf = 0.5 * (1.0 + lax.erf(hidden * (0.5**0.5)))
        active = (hidden * cdf).astype(low)
        slope = cdf + hidden * (jnp.exp(-0.5 * hidden * hidden) * ((2.0 * math.pi) ** -0.5))
        act[...] = active
        act_t[...] = active.T
        back = (dot_bt(dy_ref[...], wd[lanes, :]) * slope).astype(low)
        hid_grad[...] = back
        vec_sum[0, 4 + c : 5 + c, :] = column_sum(back.astype(f32))

    def weigh(unit, left_t, right):
        product = dot(left_t, right).astype(low)
        first, second = product[:, :half], product[:, half:]
        give(unit, jnp.where(core == 0, second, first))
        keep(unit, jnp.where(core == 0, first, second))

    def down_weight(c):
        weigh(c, act_t[...], dy_ref[...])

    def up_weight(c):
        weigh(N_DOWN + c, mid_t[...], hid_grad[...])

    def contract(c):
        lanes = quarter(c)
        deeper = dot_bt(hid_grad[...], wu[:, lanes])
        further = dot(act[...], wd[lanes, :])
        if c == 0:
            input_grad_ref[...] = deeper
            total[...] = mixed[...] + as_row(down_bias_ref) + further
        else:
            input_grad_ref[...] += deeper
            total[...] += further

    def norm_back():
        outputs[...] = total[...].astype(low)
        save(outputs, outputs_hbm, 0)
        hat, inverse = normal_parts(mixed[...])
        grad = input_grad_ref[...]
        vec_sum[0, 2:3, :] = column_sum(grad * hat)
        vec_sum[0, 3:4, :] = column_sum(grad)
        whole = dy_ref[...].astype(f32) + normal_back(hat, inverse, as_row(mid_gain_ref), grad)
        input_grad_ref[...] = whole
        branch_low = whole.astype(low)
        hid_grad[...] = branch_low
        vec_sum[0, 1:2, :] = column_sum(branch_low.astype(f32))
        vec_sum[0, 0:1, :] = column_sum(dy_ref[...].astype(f32))
        act_t[...] = attended_ref[...].T

    def out_weight():
        weigh(U_OUT, act_t[...], hid_grad[...])

    def attended_back():
        grad = dot_bt(hid_grad[...], wo[...])
        for p in range(pairs):
            share = both(inverse_ref[:, p : p + 1], inverse_ref[:, HALF + p : HALF + p + 1])
            att_grad[p] = (grad[:, p * PAIR : (p + 1) * PAIR] * share).astype(low)

    load_qkv = []

    def fetch():
        for p in range(pairs):
            for i, src in enumerate((wq_hbm, wk_hbm, wv_hbm)):
                at = (3 * p + i) * PAIR
                load_qkv.append(
                    load(
                        src.at[:, p * PAIR : (p + 1) * PAIR],
                        wu.at[:, at : at + PAIR],
                        11 + 3 * p + i,
                    )
                )

    def pair_back(p, slot):
        q, k, v, grad = queries[p], keys[p], values[p], att_grad[p]
        if p >= 2:
            probs_copy(p, slot).wait()
        out = attended_ref[:, p * PAIR : (p + 1) * PAIR]
        product = grad.astype(f32) * out.astype(f32)
        q_t, grad_t = q.T, grad.T
        query_total = jnp.zeros((rows, PAIR), f32)
        key_parts, value_parts = [], []
        for head in range(2):
            share = probs[slot, head]
            delta = jnp.sum(only_head(product, head), axis=1, keepdims=True)
            score = dot_bt(only_head(grad, head), v)
            score = (share.astype(f32) * (score - delta)).astype(low)
            query_total = query_total + dot(score, only_head(k, head))
            at = slice(head * HALF, (head + 1) * HALF)
            key_parts.append(dot(q_t[at, :], score).astype(low))
            value_parts.append(dot(grad_t[at, :], share).astype(low))
        kv_part[p % kv_part.shape[0], 0] = jnp.concatenate(key_parts, axis=0).T
        kv_part[p % kv_part.shape[0], 1] = jnp.concatenate(value_parts, axis=0).T
        qkv_grad[:, 3 * p * PAIR : (3 * p + 1) * PAIR] = (query_total * HD ** (-0.5)).astype(low)

    def attention_back(p):
        if p >= kv_part.shape[0]:
            flying[("kv", p - kv_part.shape[0])].wait_send()
        pair_back(p, p % 2)
        if p + 2 < pairs:
            probs_copy(p + 2, p % 2).start()
        copy = pltpu.make_async_remote_copy(
            src_ref=kv_part.at[p % kv_part.shape[0], :, their_rows],
            dst_ref=kv_recv.at[p],
            send_sem=kv_send.at[p],
            recv_sem=kv_recv_sem.at[p],
            device_id=sibling,
            device_id_type=MESH,
        )
        copy.start()
        flying[("kv", p)] = copy

    def qkv_weight(r):
        for i in range(2):
            p = 2 * r + i
            flying[("kv", p)].wait_recv()
            for j in range(2):
                qkv_grad[:, (3 * p + 1 + j) * PAIR : (3 * p + 2 + j) * PAIR] = (
                    kv_part[p % kv_part.shape[0], j, own_rows, :] + kv_recv[p, j]
                )
        weigh(U_QKV + r, normed_t[...], qkv_grad[:, 6 * r * PAIR : 6 * (r + 1) * PAIR])

    def input_back():
        for copy in load_qkv:
            copy.wait()
        size = 3 * pairs * PAIR
        grad = dot_bt(qkv_grad[...], wu[:, :size])
        hat, inverse = normal_parts(x_ref[...].astype(f32))
        input_grad_ref[...] += normal_back(hat, inverse, as_row(gain_ref), grad)
        save(input_grad_ref, input_grad_hbm, 1)
        vec_sum[0, 8:16, :] = jnp.zeros((8, width), f32)
        vec_sum[0, 8:9, :] = column_sum(grad * hat)
        vec_sum[0, 9:10, :] = column_sum(grad)
        for p in range(pairs):
            lanes = slice(p * PAIR, (p + 1) * PAIR)
            for row, j in ((2, 0), (3, 2)):
                part = qkv_grad[:, (3 * p + j) * PAIR : (3 * p + j + 1) * PAIR]
                vec_sum[0, 8 + row : 9 + row, lanes] = column_sum(part.astype(f32))

    def first_wait():
        for copy in (load_wu, load_dy, load_wd):
            copy.wait()

    merge()
    first_wait()
    expand(0)
    down_weight(0)
    up_weight(0)
    contract(0)
    expand(1)
    step(4, 1)
    step(0, 1)
    down_weight(1)
    up_weight(1)
    contract(1)
    expand(2)
    step(7, 1)
    step(6, 1)
    step(1, 1)
    down_weight(2)
    up_weight(2)
    step(5, 1)
    contract(2)
    step(2, 1)
    expand(3)
    step(8, 1)
    down_weight(3)
    step(0, 2)
    step(9, 1)
    up_weight(3)
    contract(3)
    step(1, 2)
    norm_back()
    step(3, 1)
    step(11, 1)
    out_weight()
    attended_back()
    step(4, 2)
    fetch()
    step(2, 2)
    attention_back(0)
    step(13, 1)
    step(12, 1)
    down_pair(0)
    attention_back(1)
    attention_back(2)
    step(3, 2)
    step(6, 2)
    step(7, 2)
    step(5, 2)
    step(11, 2)
    attention_back(3)
    step(8, 2)
    qkv_weight(0)
    step(10, 1)
    step(6, 3)
    step(4, 3)
    attention_back(4)
    down_pair(1)
    step(13, 2)
    step(15, 1)
    step(14, 1)
    attention_back(5)
    step(8, 3)
    step(12, 2)
    qkv_weight(1)
    step(4, 4)
    step(7, 3)
    step(16, 1)
    step(10, 2)
    step(5, 3)
    qkv_weight(2)
    step(13, 3)
    step(18, 1)
    step(17, 1)
    step(15, 2)
    input_back()
    step(19, 1)
    step(10, 3)
    step(20, 1)
    vec_step(0)
    down_cross()
    step(15, 3)
    step(14, 2)
    step(16, 2)
    vec_step(1)
    step(12, 3)
    step(17, 2)
    step(13, 4)
    step(9, 2)
    step(20, 2)
    step(19, 2)
    step(10, 4)
    step(18, 2)
    step(5, 4)
    step(15, 4)
    step(11, 3)
    step(14, 3)
    vec_step(2)
    step(12, 4)
    step(9, 3)
    step(16, 3)
    step(17, 3)
    step(7, 4)
    step(6, 4)
    step(20, 3)
    down_finish()
    finish(4)
    step(19, 3)
    step(18, 3)
    vec_step(3)
    step(17, 4)
    finish(12)
    step(20, 4)
    step(11, 4)
    finish(15)
    finish(6)
    step(9, 4)
    step(16, 4)
    step(8, 4)
    step(14, 4)
    finish(10)
    finish(5)
    step(19, 4)
    step(18, 4)
    vec_step(4)
    finish(7)
    finish(20)
    finish(14)
    finish(17)
    finish(9)
    finish(16)
    finish(19)
    finish(11)
    finish(8)
    finish(13)
    finish(18)
    vec_step(5)

    size = width // GROUPS
    if minor == 1:
        size = size // 2
        keep_rows = pl.ds(pl.multiple_of(core * size, size), size)
        down_rows = pl.ds(pl.multiple_of(core * 4 * size, 4 * size), 4 * size)
        flying[(0, 5)].wait_recv()
        down_out_ref[:, pl.ds(mine, half)] = down_last[down_rows, :]
        down_out_ref[:, pl.ds(theirs, half)] = down_last_recv[...]
        for part in range(N_DOWN, len(PARTS)):
            flying[(part, 5)].wait_recv()
        for unit in range(N_DOWN, UNITS):
            spot = unit - N_DOWN
            if unit < U_OUT:
                target, lanes = up_out_ref, (unit - N_DOWN) * width
            else:
                target, lanes = out_out_ref, 0
            if unit < U_QKV:
                target[:, pl.ds(pl.multiple_of(lanes + mine, half), half)] = last[spot, keep_rows, :]
                target[:, pl.ds(pl.multiple_of(lanes + theirs, half), half)] = last_recv[spot]
            else:
                for which, value in (
                    (core, last[spot, keep_rows, :]),
                    (1 - core, last_recv[spot]),
                ):
                    at = pl.ds(pl.multiple_of((2 * (unit - U_QKV) + which) * PAIR, PAIR), PAIR)
                    for j in range(3):
                        qkv_out_ref[j, :, at] = value[:, j * PAIR : (j + 1) * PAIR]
    else:
        down_out_ref[...] = down_last[...]
        for unit in range(N_DOWN, U_OUT):
            up_out_ref[:, (unit - N_DOWN) * half : (unit - N_DOWN + 1) * half] = last[unit - N_DOWN]
        out_out_ref[...] = last[U_OUT - N_DOWN]
        for r in range(3):
            for j in range(3):
                qkv_out_ref[j, :, r * PAIR : (r + 1) * PAIR] = last[
                    U_QKV - N_DOWN + r, :, j * PAIR : (j + 1) * PAIR
                ]

    for copy in saves:
        copy.wait()
    for swap in swaps:
        swap.wait_send()
    for p in range(pairs - kv_part.shape[0], pairs):
        flying[("kv", p)].wait_send()
    for key, copy in flying.items():
        if key[0] == "v" or isinstance(key[0], int) or key in [("give", u) for u in given[-2:]]:
            copy.wait_send()


def run_layer(x, dy, ids, vectors, weights, minor):
    rows, width = x.shape
    pairs = width // PAIR
    cols = ids.shape[1]
    hidden = weights[1].shape[1]
    half = width // 2
    chunk = width // GROUPS
    low, f32 = jnp.bfloat16, jnp.float32
    vmem, hbm = pl.BlockSpec(memory_space=pltpu.VMEM), pl.BlockSpec(memory_space=pl.ANY)
    if minor == 1:
        outs = [(3, chunk // 2, width), (chunk // 2, width), (chunk // 2, hidden), (2 * chunk, width)]
    else:
        outs = [(3, chunk, half), (chunk, half), (chunk, hidden // 2), (4 * chunk, half)]
    late = UNITS - N_DOWN
    return pl.pallas_call(
        partial(layer_kernel, rows, width, pairs, minor),
        out_shape=[
            jax.ShapeDtypeStruct((rows, width), low),
            jax.ShapeDtypeStruct((rows, width), f32),
        ]
        + [jax.ShapeDtypeStruct(shape, f32) for shape in outs]
        + [jax.ShapeDtypeStruct((8, width), f32)] * 2
        + [jax.ShapeDtypeStruct((pairs - 2, 2, rows, cols), low)],
        in_specs=[hbm] * 2 + [vmem] * 10 + [hbm] * 6,
        out_specs=[hbm] * 2 + [vmem] * 6 + [hbm],
        scratch_shapes=[
            pltpu.VMEM((rows, width), f32),
            pltpu.VMEM((2, rows, cols), f32),
            pltpu.VMEM((rows, PAIR), f32),
            pltpu.VMEM((rows, PAIR), low),
            pltpu.VMEM((cols, PAIR), low),
            pltpu.VMEM((cols, 8), f32),
            pltpu.VMEM((rows, width), low),
            pltpu.VMEM((rows, width), low),
            pltpu.VMEM((rows, width), low),
            pltpu.VMEM((width, width), low),
            pltpu.VMEM((width, hidden), low),
            pltpu.VMEM((hidden, width), low),
            pltpu.VMEM((width, rows), low),
            pltpu.VMEM((pairs, rows, PAIR), low),
            pltpu.VMEM((pairs, cols, PAIR), low),
            pltpu.VMEM((pairs, cols, PAIR), low),
            pltpu.VMEM((2, 2, rows, cols), low),
            pltpu.VMEM((rows, width), low),
            pltpu.VMEM((width, rows), low),
            pltpu.VMEM((rows, width), low),
            pltpu.VMEM((rows, width), low),
            pltpu.VMEM((width, rows), low),
            pltpu.VMEM((rows, width), low),
            pltpu.VMEM((pairs, rows, PAIR), low),
            pltpu.VMEM((rows, 3 * width), low),
            pltpu.VMEM((4, 2, cols, PAIR), low),
            pltpu.VMEM((pairs, 2, rows, PAIR), low),
            pltpu.VMEM((UNITS, width, half), low),
            pltpu.VMEM((2, width, half), low),
            pltpu.VMEM((max(LANDING) + 1, width, half), low),
            pltpu.VMEM((UNITS, width // 2, half), low),
            pltpu.VMEM((UNITS, width // 4, half), low),
            pltpu.VMEM((late, width // 8, half), low),
            pltpu.VMEM((late, width // 16, half), low),
            pltpu.VMEM((2, width // 4, half), low),
            pltpu.VMEM((width // 4, half), low),
            pltpu.VMEM((late, chunk, half), f32),
            pltpu.VMEM((late, chunk // 2, half), f32),
            pltpu.VMEM((4 * chunk, half), f32),
            pltpu.VMEM((2 * chunk, half), f32),
            pltpu.VMEM((5, 16, width), f32),
            pltpu.VMEM((5, 16, width), f32),
            pltpu.SemaphoreType.DMA((6,)),
            pltpu.SemaphoreType.DMA((6,)),
            pltpu.SemaphoreType.DMA((11 + 3 * pairs,)),
            pltpu.SemaphoreType.DMA((2,)),
            pltpu.SemaphoreType.DMA((2,)),
            pltpu.SemaphoreType.DMA((PART_SEMS, 6)),
            pltpu.SemaphoreType.DMA((PART_SEMS, 6)),
            pltpu.SemaphoreType.DMA((UNITS,)),
            pltpu.SemaphoreType.DMA((UNITS,)),
            pltpu.SemaphoreType.DMA((pairs,)),
            pltpu.SemaphoreType.DMA((pairs,)),
            pltpu.SemaphoreType.DMA((5,)),
            pltpu.SemaphoreType.DMA((5,)),
        ],
        compiler_params=pltpu.CompilerParams(
            collective_id=1, has_side_effects=True, vmem_limit_bytes=61 << 20
        ),
    )(x, dy, ids, *vectors, *weights)


def finish_kernel(
    outputs_ref, input_grad_ref, qkv_ref, out_ref, up_ref, down_ref, vec_a_ref, vec_b_ref, *rest
):
    outputs_out, input_grad_out, query, key, value, out, up, down = rest[:8]
    vectors = rest[8:]
    outputs_out[...] = outputs_ref[...]
    input_grad_out[...] = input_grad_ref[...]

    def flatten(values, target):
        rows, lanes = values.shape
        parts = lanes // 128
        for j in range(parts):
            target[pl.ds(j, rows, stride=parts), :] = values[:, j * 128 : (j + 1) * 128]

    @pl.when(pl.program_id(0) == 0)
    def _():
        for j, target in enumerate((query, key, value)):
            flatten(qkv_ref[j], target)
        flatten(out_ref[...], out)
        flatten(up_ref[...], up)
        flatten(down_ref[...], down)
        lines = [vec_b_ref[j, :] for j in range(4)] + [vec_a_ref[j, :] for j in (1, 2, 3)]
        for line, target in zip(lines, vectors[:7]):
            target[...] = line
        width = vec_a_ref.shape[1]
        for j in range(4):
            vectors[7][j * width : (j + 1) * width] = vec_a_ref[4 + j, :]
        vectors[8][...] = vec_a_ref[0, :]


def run_finish(outputs, input_grad, qkv, out, up, down, vec_a, vec_b):
    f32 = jnp.float32
    width = vec_a.shape[1]
    steps = 2
    whole = lambda shape: pl.BlockSpec(shape, lambda i: (0,) * len(shape))
    piece = pl.BlockSpec((outputs.shape[0] // steps, width), lambda i: (i, 0))
    flat = lambda size: jax.ShapeDtypeStruct((size // 128, 128), f32)
    line = lambda size: jax.ShapeDtypeStruct((size,), f32)
    shapes = [
            jax.ShapeDtypeStruct(outputs.shape, outputs.dtype),
            jax.ShapeDtypeStruct(input_grad.shape, f32),
            *(flat(qkv[0].size) for _ in range(3)),
            *(flat(part.size) for part in (out, up, down)),
            *(line(width) for _ in range(7)),
            line(4 * width),
            line(width),
        ]
    return pl.pallas_call(
        finish_kernel,
        grid=(steps,),
        out_shape=shapes,
        in_specs=[piece] * 2 + [whole(part.shape) for part in (qkv, out, up, down, vec_a, vec_b)],
        out_specs=[piece] * 2 + [whole(shape.shape) for shape in shapes[2:]],
    )(outputs, input_grad, qkv, out, up, down, vec_a, vec_b)


def local(
    incoming_vectors,
    caption_labels,
    loss_sensitivity,
    asking_projection,
    lookup_projection,
    content_projection,
    attention_result_projection,
    expansion_projection,
    contraction_projection,
    attention_norm_scale,
    attention_norm_offset,
    asking_offset,
    content_offset,
    attention_result_offset,
    feedforward_norm_scale,
    feedforward_norm_offset,
    expansion_offset,
    contraction_offset,
):
    seqs, rows, width = incoming_vectors.shape
    chips = lax.axis_size("seq")
    minor = chips // GROUPS
    core = lax.axis_index("blk")
    x = incoming_vectors.reshape(rows, width)
    dy = loss_sensitivity.reshape(rows, width)
    vectors = (
        attention_norm_scale,
        attention_norm_offset,
        asking_offset,
        content_offset,
        feedforward_norm_scale,
        feedforward_norm_offset,
        attention_result_offset,
        expansion_offset,
        contraction_offset,
    )
    weights = (
        attention_result_projection,
        expansion_projection,
        contraction_projection,
        asking_projection,
        lookup_projection,
        content_projection,
    )
    outputs, input_grad, qkv_sum, out_sum, up_sum, down_sum, vec_a, vec_b, _ = run_layer(
        x, dy, caption_labels, vectors, weights, minor
    )
    if minor > 1:
        teams = [[g * minor + i for i in range(minor)] for g in range(GROUPS)]
        own_half = lambda values: lax.dynamic_slice_in_dim(
            values, core * (values.shape[0] // 2), values.shape[0] // 2, 0
        )

        def rest(part, pieces):
            both = lax.all_gather(part.reshape(part.shape[0], pieces, -1), "blk", axis=2)
            whole = both.reshape(part.shape[0], -1)
            return own_half(
                lax.psum_scatter(whole, "seq", axis_index_groups=teams, tiled=True)
            )

        qkv_sum = [rest(qkv_sum[i], 3) for i in range(3)]
        out_sum, up_sum, down_sum = rest(out_sum, 1), rest(up_sum, 4), rest(down_sum, 1)
        vec_a, vec_b = lax.psum((vec_a, vec_b), "seq", axis_index_groups=teams)
        qkv_sum = jnp.stack(qkv_sum)
    flat = run_finish(outputs, input_grad, qkv_sum, out_sum, up_sum, down_sum, vec_a, vec_b)
    return (
        flat[0].reshape(seqs, rows, width),
        flat[1].reshape(seqs, rows, width),
        *(part.reshape(-1) for part in flat[2:]),
    )


def solution(mesh):
    in_specs = (
        P("seq", "blk", None),
        P("seq", None),
        P("seq", "blk", None),
        P(),
        P(),
        P(),
        P(),
        P(),
        P(),
        P(),
        P(),
        P(),
        P(),
        P(),
        P(),
        P(),
        P(),
        P(),
    )
    out_specs = (
        P("seq", "blk", None),
        P("seq", "blk", None),
        P(("seq", "blk")),
        P(("seq", "blk")),
        P(("seq", "blk")),
        P(("seq", "blk")),
        P(("seq", "blk")),
        P(("seq", "blk")),
        P(),
        P(),
        P(),
        P(),
        P(),
        P(),
        P(),
        P(),
        P(),
    )
    return jax.shard_map(local, mesh=mesh, in_specs=in_specs, out_specs=out_specs, check_vma=False)
```
